32 devices in a mesh: groups: 2 (over y), hid: 4 (over z), wid: 2 (over x), tok: 2 (over core).
Axes of the slice: x: 2, y: 2, z: 4, core: 2. Of those that a mesh axis runs over, the one named last changes fastest.
Arguments:
- acts: bfloat16 [768, 4096], P(('groups', 'tok'), ('wid', 'hid')), parts along dimension 0, may hold values from -6 to 6
- grad_out: bfloat16 [768, 4096], P(('groups', 'tok'), ('wid', 'hid')), parts along dimension 0, may hold values from -4 to 4
- w_gate: bfloat16 [4096, 14336], P('wid', ('hid', 'tok')), may hold values from -0.125 to 0.125
- w_up: bfloat16 [4096, 14336], P('wid', ('hid', 'tok')), may hold values from -0.09375 to 0.09375
- w_down: bfloat16 [14336, 4096], P(('hid', 'tok'), 'wid'), may hold values from -0.046875 to 0.046875
Outputs:
- input_grad: bfloat16 [768, 4096], P(('groups', 'tok'), ('wid', 'hid')), parts along dimension 0
- grad_gate: bfloat16 [8192, 14336], P(('groups', 'wid'), ('hid', 'tok')), parts along dimension 0
- grad_up: bfloat16 [8192, 14336], P(('groups', 'wid'), ('hid', 'tok')), parts along dimension 0
- grad_down: bfloat16 [28672, 4096], P(('groups', 'hid', 'tok'), 'wid'), parts along dimension 0
The draws below stay inside these ranges and needn't reach their ends.
There are 2 independent parts, one for each index of `groups`. The reference program is written for one: setup_inputs(seed, part) draws one part's arguments, and reference() takes and returns one part's arrays. A program takes and returns all parts, laid end to end along the dimension named above; an argument that names none is the same for every part. Nothing has to cross between parts.
All inputs are finite; a program needn't handle non-finite values.
Results may differ from the reference program's by a relative error of at most 0.02.
Values may be sent and summed in bfloat16 or wider, within the bound.
No kernel may reach another device: no remote copies, remote signals or barrier semaphores. Data moves between devices by JAX's collectives and lax.ppermute only.
A program may use at most 256 MiB of HBM per device.

```python
import jax
import jax.numpy as jnp
from jax import lax

D = 4096
FF = 14336
TOK_DEV = 192
TOKENS = 384
N_HID = 4
N_TOK = 2


def raised(values, own_key, source, target, shards_of, factor):
    owner, partner = [(jnp.arange(values.shape[position]) // (values.shape[position] // shards_of)).reshape([-1 if axis == position else 1 for axis in range(values.ndim)]) for position in (source, target)]
    chosen = jax.random.permutation(own_key, shards_of)[partner]
    strong = (owner == chosen) | (owner == (partner + shards_of // 2) % shards_of)
    return jnp.where(strong, factor * values, values)


def levels(key, dims, split, least, top_value):
    def one(axis_at, shards_of):
        heights = jax.random.uniform(jax.random.fold_in(jax.random.fold_in(key, 6), axis_at), (shards_of,), jnp.float32, least / len(split), top_value / len(split))
        return jnp.repeat(jnp.exp(heights), dims[axis_at] // shards_of).reshape((-1,) + (1,) * (len(dims) - axis_at - 1))

    level = one(*split[0])
    for cut in split[1:]:
        level = level * one(*cut)
    return level


def noise(stream_key, extent, scale, most, shards=(), held_as=jnp.bfloat16):
    drawn = jax.random.normal(stream_key, extent, jnp.float32) * scale
    if len(shards) > 0:
        drawn = levels(stream_key, extent, shards, -0.22, 0.18) * drawn
    return jnp.clip(drawn, min=-most, max=most).astype(held_as)


def bell_draw_with(own_key, shape, deviation, most, cuts, heavy, kind=jnp.bfloat16):
    array = deviation * jax.random.normal(own_key, shape, jnp.float32)
    if cuts:
        array = array * levels(own_key, shape, cuts, -0.22, 0.18)
    return jnp.clip(raised(array, jax.random.fold_in(own_key, 3), *heavy), -most, most).astype(kind)


def setup_inputs(seed: int = 0, part: int = 0) -> dict:
    key_list = jax.random.split(jax.random.key(seed), 6)
    part_keys = jax.random.split(jax.random.fold_in(key_list[5], part), 6)
    return {
        "acts": noise(part_keys[0], (TOKENS, D), 1.0, 6.0, ((0, 2), (1, 8))),
        "grad_out": noise(part_keys[1], (TOKENS, D), 0.25, 4.0, ((0, 2), (1, 8))),
        "w_gate": bell_draw_with(key_list[2], (D, FF), D ** -0.5, 0.125, ((0, 2), (1, 8)), (1, 0, 8, 2.0)),
        "w_up": noise(key_list[3], (D, FF), D ** -0.5, 0.09375, ((0, 2), (1, 8))),
        "w_down": noise(key_list[4], (FF, D), FF ** -0.5, 0.046875, ((0, 8), (1, 2))),
    }


def swiglu_grads(gate, up, dhid):
    sig = jax.nn.sigmoid(gate)
    hidden = (gate * sig * up).astype(jnp.bfloat16)
    d_gate = (dhid * up * sig * (1.0 + gate * (1.0 - sig))).astype(jnp.bfloat16)
    d_up = (dhid * gate * sig).astype(jnp.bfloat16)
    return hidden, d_gate, d_up


def blockwise(left, right):
    total = jnp.zeros((left.shape[1], right.shape[1]), jnp.float32)
    for block in range(N_TOK):
        lower = block * TOK_DEV
        piece = jnp.dot(left[lower:lower + TOK_DEV].T, right[lower:lower + TOK_DEV], preferred_element_type=jnp.float32)
        total = total + lax.optimization_barrier(piece.astype(jnp.bfloat16)).astype(jnp.float32)
    return total.astype(jnp.bfloat16)


def reference(acts, grad_out, w_gate, w_up, w_down):
    gate = jnp.dot(acts, w_gate, preferred_element_type=jnp.float32)
    up = jnp.dot(acts, w_up, preferred_element_type=jnp.float32)
    dhid = jnp.dot(grad_out, w_down.T, preferred_element_type=jnp.float32)
    hidden, d_gate, d_up = swiglu_grads(gate, up, dhid)
    width = FF // N_HID
    total = jnp.zeros((acts.shape[0], acts.shape[1]), jnp.float32)
    for block in range(N_HID):
        lower = block * width
        upper = lower + width
        part = jnp.dot(d_gate[:, lower:upper], w_gate[:, lower:upper].T, preferred_element_type=jnp.float32)
        part = part + jnp.dot(d_up[:, lower:upper], w_up[:, lower:upper].T, preferred_element_type=jnp.float32)
        total = total + lax.optimization_barrier(part.astype(jnp.bfloat16)).astype(jnp.float32)
    grad_gate = blockwise(acts, d_gate)
    grad_up = blockwise(acts, d_up)
    grad_down = blockwise(hidden, grad_out)
    return total.astype(jnp.bfloat16), grad_gate, grad_up, grad_down
```

```python
import jax
import jax.numpy as jnp
from jax import lax
from jax.sharding import PartitionSpec as P

PIECES = (1, 2, 3)


def swiglu_grads(gate, up, dhid):
    sig = jax.nn.sigmoid(gate)
    hidden = (gate * sig * up).astype(jnp.bfloat16)
    d_gate = (dhid * up * sig * (1.0 + gate * (1.0 - sig))).astype(jnp.bfloat16)
    d_up = (dhid * gate * sig).astype(jnp.bfloat16)
    return hidden, d_gate, d_up


def dot(left, right, dims):
    return lax.dot_general(left, right, (dims, ((), ())), preferred_element_type=jnp.float32)


def shifted(value, axis, step):
    n = lax.axis_size(axis)
    return lax.ppermute(value, axis, [(i, (i + step) % n) for i in range(n)])


def gather_cols(value, axis):
    n = lax.axis_size(axis)
    if n > 4:
        return lax.all_gather(value, axis, axis=1, tiled=True)
    me = lax.axis_index(axis)
    width = value.shape[1]
    out = jnp.zeros((value.shape[0], n * width), value.dtype)
    for step in range(n):
        block = shifted(value, axis, step) if step else value
        out = lax.dynamic_update_slice(out, block, (0, lax.rem(me - step + n, n) * width))
    return out


def scatter_cols(value, axis):
    n = lax.axis_size(axis)
    if n > 4:
        return lax.psum_scatter(value, axis, scatter_dimension=1, tiled=True).astype(jnp.float32)
    me = lax.axis_index(axis)
    width = value.shape[1] // n
    total = None
    for step in range(n):
        block = lax.dynamic_slice(value, (0, lax.rem(me + step, n) * width), (value.shape[0], width))
        block = shifted(block, axis, step) if step else block
        block = block.astype(jnp.float32)
        total = block if total is None else total + block
    return total


def summed(value, axis):
    total = value.astype(jnp.float32)
    for step in range(1, lax.axis_size(axis)):
        total = total + shifted(value, axis, step).astype(jnp.float32)
    return total


def own_first(value, axis):
    return jnp.concatenate([value] + [shifted(value, axis, step) for step in range(1, lax.axis_size(axis))], axis=0)


def pieces(rows):
    unit = rows // sum(PIECES)
    bounds = [0]
    for part in PIECES:
        bounds.append(bounds[-1] + part * unit)
    return list(zip(bounds[:-1], bounds[1:]))


def shards(acts, grad_out, w_gate, w_up, w_down):
    ins, backs = [], []
    spans = pieces(acts.shape[0])
    for lower, upper in spans:
        x = own_first(gather_cols(acts[lower:upper], "hid"), "tok")
        dy = own_first(gather_cols(grad_out[lower:upper], "hid"), "tok")
        ins.append((x, dy))
    halves = []
    for x, dy in ins:
        gate = dot(x, w_gate, ((1,), (0,))).astype(jnp.bfloat16)
        up = dot(x, w_up, ((1,), (0,))).astype(jnp.bfloat16)
        dhid = dot(dy, w_down, ((1,), (1,))).astype(jnp.bfloat16)
        halves.append((gate, up, dhid))
    grads = []
    for (lower, upper), parts in zip(spans, halves):
        gate, up, dhid = [summed(part, "wid") for part in parts]
        hidden, d_gate, d_up = swiglu_grads(gate, up, dhid)
        grads.append((hidden, d_gate, d_up))
        back = dot(d_gate, w_gate, ((1,), (1,))) + dot(d_up, w_up, ((1,), (1,)))
        rows = upper - lower
        n = lax.axis_size("tok")
        back = back.astype(jnp.bfloat16)
        total = back[:rows].astype(jnp.float32)
        for step in range(1, n):
            block = back[step * rows : (step + 1) * rows]
            total = total + shifted(block, "tok", n - step).astype(jnp.float32)
        backs.append(scatter_cols(total.astype(jnp.bfloat16), "hid").astype(jnp.bfloat16))
    x_all = jnp.concatenate([x for x, _ in ins], axis=0)
    dy_all = jnp.concatenate([dy for _, dy in ins], axis=0)
    hidden, d_gate, d_up = [jnp.concatenate([g[i] for g in grads], axis=0) for i in range(3)]
    grad_gate = dot(x_all, d_gate, ((0,), (0,))).astype(jnp.bfloat16)
    grad_up = dot(x_all, d_up, ((0,), (0,))).astype(jnp.bfloat16)
    grad_down = dot(hidden, dy_all, ((0,), (0,))).astype(jnp.bfloat16)
    return jnp.concatenate(backs, axis=0), grad_gate, grad_up, grad_down


def solution(mesh):
    placed = (
        P(("groups", "tok"), ("wid", "hid")),
        P(("groups", "tok"), ("wid", "hid")),
        P("wid", ("hid", "tok")),
        P("wid", ("hid", "tok")),
        P(("hid", "tok"), "wid"),
    )
    return jax.shard_map(
        shards,
        mesh=mesh,
        in_specs=placed,
        out_specs=(
            P(("groups", "tok"), ("wid", "hid")),
            P(("groups", "wid"), ("hid", "tok")),
            P(("groups", "wid"), ("hid", "tok")),
            P(("groups", "hid", "tok"), "wid"),
        ),
        check_vma=False,
    )
```

```python
import jax
import jax.numpy as jnp
from jax import lax
from jax.sharding import PartitionSpec as P

PIECES = (3, 5, 4)


def swiglu_grads(gate, up, dhid):
    sig = jax.nn.sigmoid(gate)
    hidden = (gate * sig * up).astype(jnp.bfloat16)
    d_gate = (dhid * up * sig * (1.0 + gate * (1.0 - sig))).astype(jnp.bfloat16)
    d_up = (dhid * gate * sig).astype(jnp.bfloat16)
    return hidden, d_gate, d_up


def dot(left, right, dims):
    return lax.dot_general(left, right, (dims, ((), ())), preferred_element_type=jnp.float32)


def shifted(value, axis, step):
    n = lax.axis_size(axis)
    return lax.ppermute(value, axis, [(i, (i + step) % n) for i in range(n)])


def swapped(value, axis, bit):
    n = lax.axis_size(axis)
    return lax.ppermute(value, axis, [(i, i ^ bit) for i in range(n)])


def gather_cols(value, axis):
    n = lax.axis_size(axis)
    if n != 4:
        return lax.all_gather(value, axis, axis=1, tiled=True)
    me = lax.axis_index(axis)
    width = value.shape[1]
    far = swapped(value, axis, 2)
    near = swapped(jnp.concatenate([value, far], axis=1), axis, 1)
    own = (value, far)
    other = (near[:, :width], near[:, width:])
    odd, upper = lax.rem(me, 2) == 1, me >= 2
    blocks = []
    for pair in range(2):
        blocks.append(jnp.where(odd, other[pair], own[pair]))
        blocks.append(jnp.where(odd, own[pair], other[pair]))
    blocks = [jnp.where(upper, blocks[i ^ 2], blocks[i]) for i in range(4)]
    return jnp.concatenate(blocks, axis=1)


def scatter_cols(value, axis):
    n = lax.axis_size(axis)
    if n != 4:
        return lax.psum_scatter(value.astype(jnp.bfloat16), axis, scatter_dimension=1, tiled=True)
    me = lax.axis_index(axis)
    width = value.shape[1] // n
    odd, upper = lax.rem(me, 2) == 1, me >= 2
    blocks = [value[:, i * width : (i + 1) * width] for i in range(4)]
    keep = [jnp.where(odd, blocks[2 * i + 1], blocks[2 * i]) for i in range(2)]
    give = [jnp.where(odd, blocks[2 * i], blocks[2 * i + 1]) for i in range(2)]
    near = swapped(jnp.concatenate(give, axis=1).astype(jnp.bfloat16), axis, 1).astype(jnp.float32)
    sums = [keep[i] + near[:, i * width : (i + 1) * width] for i in range(2)]
    mine = jnp.where(upper, sums[1], sums[0])
    theirs = jnp.where(upper, sums[0], sums[1])
    return (mine + swapped(theirs.astype(jnp.bfloat16), axis, 2).astype(jnp.float32)).astype(jnp.bfloat16)


def summed(value, axis):
    total = value.astype(jnp.float32)
    for step in range(1, lax.axis_size(axis)):
        total = total + shifted(value, axis, step).astype(jnp.float32)
    return total


def own_first(value, axis):
    return jnp.concatenate([value] + [shifted(value, axis, step) for step in range(1, lax.axis_size(axis))], axis=0)


def pieces(rows):
    unit = rows // sum(PIECES)
    bounds = [0]
    for part in PIECES:
        bounds.append(bounds[-1] + part * unit)
    return list(zip(bounds[:-1], bounds[1:]))


def shards(acts, grad_out, w_gate, w_up, w_down):
    spans = pieces(acts.shape[0])
    ins, backs = [], []
    held = None
    for index, (lower, upper) in enumerate(spans):
        rows = upper - lower
        x, dy = acts[lower:upper], grad_out[lower:upper]
        if index == 0:
            x = gather_cols(x, "hid")
            dy = gather_cols(dy, "hid")
            held = dy
            x, dy = own_first(x, "tok"), own_first(dy, "tok")
        else:
            both, held = lax.optimization_barrier((jnp.concatenate([x, dy], axis=0), held))
            both = gather_cols(both, "hid")
            held = both
            blocks = own_first(both, "tok")
            count = blocks.shape[0] // rows
            x = jnp.concatenate([blocks[i * rows : (i + 1) * rows] for i in range(0, count, 2)], axis=0)
            dy = jnp.concatenate([blocks[i * rows : (i + 1) * rows] for i in range(1, count, 2)], axis=0)
        ins.append((x, dy))
    halves = []
    for x, dy in ins:
        gate = dot(x, w_gate, ((1,), (0,))).astype(jnp.bfloat16)
        up = dot(x, w_up, ((1,), (0,))).astype(jnp.bfloat16)
        dhid = dot(dy, w_down, ((1,), (1,))).astype(jnp.bfloat16)
        halves.append((gate, up, dhid))
    grads = []
    for (lower, upper), parts in zip(spans, halves):
        gate, up, dhid = [summed(part, "wid") for part in parts]
        hidden, d_gate, d_up = swiglu_grads(gate, up, dhid)
        grads.append((hidden, d_gate, d_up))
        back = dot(d_gate, w_gate, ((1,), (1,))) + dot(d_up, w_up, ((1,), (1,)))
        rows = upper - lower
        n = lax.axis_size("tok")
        back = back.astype(jnp.bfloat16)
        total = back[:rows].astype(jnp.float32)
        for step in range(1, n):
            block = back[step * rows : (step + 1) * rows]
            total = total + shifted(block, "tok", n - step).astype(jnp.float32)
        backs.append(scatter_cols(total, "hid"))
    x_all = jnp.concatenate([x for x, _ in ins], axis=0)
    dy_all = jnp.concatenate([dy for _, dy in ins], axis=0)
    hidden, d_gate, d_up = [jnp.concatenate([g[i] for g in grads], axis=0) for i in range(3)]
    grad_gate = dot(x_all, d_gate, ((0,), (0,))).astype(jnp.bfloat16)
    grad_up = dot(x_all, d_up, ((0,), (0,))).astype(jnp.bfloat16)
    grad_down = dot(hidden, dy_all, ((0,), (0,))).astype(jnp.bfloat16)
    return jnp.concatenate(backs, axis=0), grad_gate, grad_up, grad_down


def solution(mesh):
    placed = (
        P(("groups", "tok"), ("wid", "hid")),
        P(("groups", "tok"), ("wid", "hid")),
        P("wid", ("hid", "tok")),
        P("wid", ("hid", "tok")),
        P(("hid", "tok"), "wid"),
    )
    return jax.shard_map(
        shards,
        mesh=mesh,
        in_specs=placed,
        out_specs=(
            P(("groups", "tok"), ("wid", "hid")),
            P(("groups", "wid"), ("hid", "tok")),
            P(("groups", "wid"), ("hid", "tok")),
            P(("groups", "hid", "tok"), "wid"),
        ),
        check_vma=False,
    )
```

```python
import functools

import jax
import jax.numpy as jnp
from jax import lax
from jax.experimental import pallas as pl
from jax.experimental.pallas import tpu as pltpu
from jax.sharding import PartitionSpec as P

SIXTEENTHS = (2, 3, 4, 3)
MIB = 1 << 20


def dot(left, right, dims):
    return lax.dot_general(left, right, (dims, ((), ())), preferred_element_type=jnp.float32)


def rows_by_cols(left, right):
    return dot(left, right, ((1,), (0,)))


def over_cols(left, right):
    return dot(left, right, ((1,), (1,)))


def over_rows(left, right):
    return dot(left, right, ((0,), (0,)))


def swiglu_grads(gate, up, dhid):
    sig = jax.nn.sigmoid(gate)
    hidden = (gate * sig * up).astype(jnp.bfloat16)
    d_gate = (dhid * up * sig * (1.0 + gate * (1.0 - sig))).astype(jnp.bfloat16)
    d_up = (dhid * gate * sig).astype(jnp.bfloat16)
    return hidden, d_gate, d_up


def shifted(value, axis, step):
    n = lax.axis_size(axis)
    return lax.ppermute(value, axis, [(i, (i + step) % n) for i in range(n)])


def swapped(value, axis, bit):
    n = lax.axis_size(axis)
    return lax.ppermute(value, axis, [(i, i ^ bit) for i in range(n)])


def summed(value, axis):
    total = value.astype(jnp.float32)
    for step in range(1, lax.axis_size(axis)):
        total = total + shifted(value, axis, step).astype(jnp.float32)
    return total


def own_first(value, axis):
    return jnp.concatenate([value] + [shifted(value, axis, step) for step in range(1, lax.axis_size(axis))], axis=0)


def home_rows(back, axis):
    n = lax.axis_size(axis)
    rows = back.shape[0] // n
    sent = back.astype(jnp.bfloat16)
    total = back[:rows]
    for step in range(1, n):
        block = sent[step * rows : (step + 1) * rows]
        total = total + shifted(block, axis, n - step).astype(jnp.float32)
    return total


def plain(acts, grad_out, w_gate, w_up, w_down):
    x = own_first(lax.all_gather(acts, "hid", axis=1, tiled=True), "tok")
    dy = own_first(lax.all_gather(grad_out, "hid", axis=1, tiled=True), "tok")
    gate = summed(rows_by_cols(x, w_gate).astype(jnp.bfloat16), "wid")
    up = summed(rows_by_cols(x, w_up).astype(jnp.bfloat16), "wid")
    dhid = summed(over_cols(dy, w_down).astype(jnp.bfloat16), "wid")
    hidden, d_gate, d_up = swiglu_grads(gate, up, dhid)
    back = home_rows(over_cols(d_gate, w_gate) + over_cols(d_up, w_up), "tok").astype(jnp.bfloat16)
    back = lax.psum_scatter(back, "hid", scatter_dimension=1, tiled=True)
    return (
        back,
        over_rows(x, d_gate).astype(jnp.bfloat16),
        over_rows(x, d_up).astype(jnp.bfloat16),
        over_rows(hidden, dy).astype(jnp.bfloat16),
    )


def nothing(*refs):
    pass


def ordered(value, *after):
    anywhere = pl.BlockSpec(memory_space=pl.ANY)
    return pl.pallas_call(
        nothing,
        out_shape=jax.ShapeDtypeStruct(value.shape, value.dtype),
        in_specs=[anywhere] * (1 + len(after)),
        out_specs=anywhere,
        input_output_aliases={0: 0},
    )(value, *after)


def arrange(value, far, near):
    me = lax.axis_index("hid")
    width = value.shape[1]
    own = (value, far)
    other = (near[:, :width], near[:, width:])
    odd, upper = lax.rem(me, 2) == 1, me >= 2
    blocks = []
    for pair in range(2):
        blocks.append(jnp.where(odd, other[pair], own[pair]))
        blocks.append(jnp.where(odd, own[pair], other[pair]))
    return jnp.concatenate([jnp.where(upper, blocks[i ^ 2], blocks[i]) for i in range(4)], axis=1)


def scatter_cols(value):
    me = lax.axis_index("hid")
    width = value.shape[1] // 4
    odd, upper = lax.rem(me, 2) == 1, me >= 2
    blocks = [value[:, i * width : (i + 1) * width] for i in range(4)]
    keep = [jnp.where(odd, blocks[2 * i + 1], blocks[2 * i]) for i in range(2)]
    give = [jnp.where(odd, blocks[2 * i], blocks[2 * i + 1]) for i in range(2)]
    near = swapped(jnp.concatenate(give, axis=1).astype(jnp.bfloat16), "hid", 1).astype(jnp.float32)
    sums = [keep[i] + near[:, i * width : (i + 1) * width] for i in range(2)]
    mine = jnp.where(upper, sums[1], sums[0])
    theirs = jnp.where(upper, sums[0], sums[1])
    return (mine + swapped(theirs.astype(jnp.bfloat16), "hid", 2).astype(jnp.float32)).astype(jnp.bfloat16)


def load_all(pairs, sem):
    copies = [pltpu.make_async_copy(source, target, sem.at[i]) for i, (source, target) in enumerate(pairs)]
    for copy in copies:
        copy.start()
    for copy in copies:
        copy.wait()


def columns_kernel(heights, starts, width, n_old, *refs):
    count = len(heights)
    x_refs, g_refs, u_refs = refs[:count], refs[count : 2 * count], refs[2 * count : 3 * count]
    gate_ref, up_ref, x_all, g_all, u_all, sem = refs[3 * count + n_old :]
    step = pl.program_id(0)

    @pl.when(step == 0)
    def _():
        pairs, top = [], 0
        for c, height in enumerate(heights):
            rows = pl.ds(top, height)
            pairs.append((x_refs[c], x_all.at[rows]))
            pairs.append((g_refs[c].at[:, pl.ds(starts[c], width)], g_all.at[rows]))
            pairs.append((u_refs[c].at[:, pl.ds(starts[c], width)], u_all.at[rows]))
            top += height
        load_all(pairs, sem)

    block = gate_ref.shape[0]
    x = x_all[:, pl.ds(pl.multiple_of(step * block, block), block)]
    gate_ref[...] = over_rows(x, g_all[...]).astype(gate_ref.dtype)
    up_ref[...] = over_rows(x, u_all[...]).astype(up_ref.dtype)


def column_grads(xs, gs, us, starts, part, parts, total, old):
    heights = [x.shape[0] for x in xs]
    tokens, features, width = sum(heights), xs[0].shape[1], total // parts
    block = 256
    anywhere = pl.BlockSpec(memory_space=pl.ANY)
    shape = jax.ShapeDtypeStruct((features, total), jnp.bfloat16)
    spec = pl.BlockSpec((block, width), lambda i: (i, part))
    first = 3 * len(xs)
    return pl.pallas_call(
        functools.partial(columns_kernel, heights, starts, width, len(old)),
        grid=(features // block,),
        out_shape=(shape, shape),
        in_specs=[anywhere] * (first + len(old)),
        out_specs=(spec, spec),
        scratch_shapes=[
            pltpu.VMEM((tokens, features), jnp.bfloat16),
            pltpu.VMEM((tokens, width), jnp.bfloat16),
            pltpu.VMEM((tokens, width), jnp.bfloat16),
            pltpu.SemaphoreType.DMA((first,)),
        ],
        input_output_aliases={first + i: i for i in range(len(old))},
        compiler_params=pltpu.CompilerParams(vmem_limit_bytes=20 * MIB),
        cost_estimate=pl.CostEstimate(
            flops=4 * tokens * features * width, bytes_accessed=4 * features * width, transcendentals=0
        ),
    )(*xs, *gs, *us, *old)


def rows_kernel(heights, starts, width, n_old, *refs):
    count = len(heights)
    h_refs, y_refs = refs[:count], refs[count : 2 * count]
    out_ref, h_all, y_all, sem = refs[2 * count + n_old :]
    step = pl.program_id(0)

    @pl.when(step == 0)
    def _():
        pairs, top = [], 0
        for c, height in enumerate(heights):
            rows = pl.ds(top, height)
            pairs.append((h_refs[c].at[:, pl.ds(starts[c], width)], h_all.at[rows]))
            pairs.append((y_refs[c], y_all.at[rows]))
            top += height
        load_all(pairs, sem)

    block = out_ref.shape[0]
    h = h_all[:, pl.ds(pl.multiple_of(step * block, block), block)]
    out_ref[...] = over_rows(h, y_all[...]).astype(out_ref.dtype)


def row_grads(hs, ys, starts, part, parts, total, old):
    heights = [y.shape[0] for y in ys]
    tokens, features, width = sum(heights), ys[0].shape[1], total // parts
    block = 128
    steps = width // block
    anywhere = pl.BlockSpec(memory_space=pl.ANY)
    first = 2 * len(ys)
    return pl.pallas_call(
        functools.partial(rows_kernel, heights, starts, width, len(old)),
        grid=(steps,),
        out_shape=jax.ShapeDtypeStruct((total, features), jnp.bfloat16),
        in_specs=[anywhere] * (first + len(old)),
        out_specs=pl.BlockSpec((block, features), lambda i: (part * steps + i, 0)),
        scratch_shapes=[
            pltpu.VMEM((tokens, width), jnp.bfloat16),
            pltpu.VMEM((tokens, features), jnp.bfloat16),
            pltpu.SemaphoreType.DMA((first,)),
        ],
        input_output_aliases={first + i: i for i in range(len(old))},
        compiler_params=pltpu.CompilerParams(vmem_limit_bytes=20 * MIB),
        cost_estimate=pl.CostEstimate(
            flops=2 * tokens * features * width, bytes_accessed=2 * features * width, transcendentals=0
        ),
    )(*hs, *ys, *old)


def forward(x, dy, w_gate, w_up, w_down, cuts):
    parts = []
    for lower, upper in cuts:
        gate = rows_by_cols(x, w_gate[:, lower:upper]).astype(jnp.bfloat16)
        up = rows_by_cols(x, w_up[:, lower:upper]).astype(jnp.bfloat16)
        dhid = over_cols(dy, w_down[lower:upper]).astype(jnp.bfloat16)
        parts.append((gate, up, dhid))
    return parts


def piped(acts, grad_out, w_gate, w_up, w_down):
    unit = acts.shape[0] // sum(SIXTEENTHS)
    bounds = [0]
    for size in SIXTEENTHS:
        bounds.append(bounds[-1] + size * unit)
    spans = list(zip(bounds[:-1], bounds[1:]))
    last = len(spans) - 1
    total = w_gate.shape[1]
    whole, halves = [(0, total)], [(0, total // 2), (total // 2, total)]

    lower, upper = spans[0]
    ready = []
    for value in (acts[lower:upper], grad_out[lower:upper]):
        far = swapped(value, "hid", 2)
        near = swapped(jnp.concatenate([value, far], axis=1), "hid", 1)
        ready.append(own_first(arrange(value, far, near), "tok"))
    inputs = [tuple(ready)]
    sums = [forward(*ready, w_gate, w_up, w_down, whole)]
    anchor = sums[0][0]

    grads, backs = [], []

    def backward(index):
        results, back = [], None
        for (lower, upper), partial in zip(halves if index == last else whole, sums[index]):
            others = [shifted(part, "wid", 1) for part in partial]
            if index < last:
                others[0] = ordered(others[0], sums[index + 1][-1][2])
            gate, up, dhid = [
                part.astype(jnp.float32) + other.astype(jnp.float32) for part, other in zip(partial, others)
            ]
            hidden, d_gate, d_up = swiglu_grads(gate, up, dhid)
            term = over_cols(d_gate, w_gate[:, lower:upper]) + over_cols(d_up, w_up[:, lower:upper])
            back = term if back is None else back + term
            results.append((hidden, d_gate, d_up))
        grads.append(results)
        backs.append(scatter_cols(home_rows(back, "tok")))

    for index in range(1, len(spans)):
        lower, upper = spans[index]
        rows = upper - lower
        both = jnp.concatenate([acts[lower:upper], grad_out[lower:upper]], axis=0)
        both = ordered(both, anchor[0] if index == 1 else near)
        far = swapped(both, "hid", 2)
        far = ordered(far, anchor[2])
        near = swapped(jnp.concatenate([both, far], axis=1), "hid", 1)
        mixed = arrange(both, far, near)
        theirs = shifted(mixed, "tok", 1)
        x = jnp.concatenate([mixed[:rows], theirs[:rows]], axis=0)
        dy = jnp.concatenate([mixed[rows:], theirs[rows:]], axis=0)
        inputs.append((x, dy))
        sums.append(forward(x, dy, w_gate, w_up, w_down, halves if index == last else whole))
        anchor = sums[index][0]
    for index in range(len(spans)):
        backward(index)

    xs, dys = [x for x, _ in inputs], [dy for _, dy in inputs]
    columns, rows = (), ()
    for part in range(2):
        starts = [part * (total // 2)] * last + [0]
        hs, gs, us = [[g[0][i] for g in grads[:last]] + [grads[last][part][i]] for i in range(3)]
        columns = column_grads(xs, gs, us, starts, part, 2, total, columns)
        rows = (row_grads(hs, dys, starts, part, 2, total, rows),)
    return jnp.concatenate(backs, axis=0), columns[0], columns[1], rows[0]


def shards(acts, grad_out, w_gate, w_up, w_down):
    sizes = tuple(lax.axis_size(axis) for axis in ("hid", "wid", "tok"))
    aligned = acts.shape[0] % (16 * sum(SIXTEENTHS)) == 0 and acts.shape[1] % 128 == 0 and w_gate.shape[1] % 256 == 0
    if sizes == (4, 2, 2) and aligned:
        return piped(acts, grad_out, w_gate, w_up, w_down)
    return plain(acts, grad_out, w_gate, w_up, w_down)


def solution(mesh):
    placed = (
        P(("groups", "tok"), ("wid", "hid")),
        P(("groups", "tok"), ("wid", "hid")),
        P("wid", ("hid", "tok")),
        P("wid", ("hid", "tok")),
        P(("hid", "tok"), "wid"),
    )
    return jax.shard_map(
        shards,
        mesh=mesh,
        in_specs=placed,
        out_specs=(
            P(("groups", "tok"), ("wid", "hid")),
            P(("groups", "wid"), ("hid", "tok")),
            P(("groups", "wid"), ("hid", "tok")),
            P(("groups", "hid", "tok"), "wid"),
        ),
        check_vma=False,
    )
```

```python
import functools

import jax
import jax.numpy as jnp
from jax import lax
from jax.experimental import pallas as pl
from jax.experimental.pallas import tpu as pltpu
from jax.sharding import PartitionSpec as P

SIXTEENTHS = (2, 3, 4, 3)
MIB = 1 << 20


def dot(left, right, dims):
    return lax.dot_general(left, right, (dims, ((), ())), preferred_element_type=jnp.float32)


def rows_by_cols(left, right):
    return dot(left, right, ((1,), (0,)))


def over_cols(left, right):
    return dot(left, right, ((1,), (1,)))


def over_rows(left, right):
    return dot(left, right, ((0,), (0,)))


def swiglu_grads(gate, up, dhid):
    sig = jax.nn.sigmoid(gate)
    hidden = (gate * sig * up).astype(jnp.bfloat16)
    d_gate = (dhid * up * sig * (1.0 + gate * (1.0 - sig))).astype(jnp.bfloat16)
    d_up = (dhid * gate * sig).astype(jnp.bfloat16)
    return hidden, d_gate, d_up


def shifted(value, axis, step):
    n = lax.axis_size(axis)
    return lax.ppermute(value, axis, [(i, (i + step) % n) for i in range(n)])


def swapped(value, axis, bit):
    n = lax.axis_size(axis)
    return lax.ppermute(value, axis, [(i, i ^ bit) for i in range(n)])


def summed(value, axis):
    total = value.astype(jnp.float32)
    for step in range(1, lax.axis_size(axis)):
        total = total + shifted(value, axis, step).astype(jnp.float32)
    return total


def own_first(value, axis):
    return jnp.concatenate([value] + [shifted(value, axis, step) for step in range(1, lax.axis_size(axis))], axis=0)


def home_rows(back, axis):
    n = lax.axis_size(axis)
    rows = back.shape[0] // n
    sent = back.astype(jnp.bfloat16)
    total = back[:rows]
    for step in range(1, n):
        block = sent[step * rows : (step + 1) * rows]
        total = total + shifted(block, axis, n - step).astype(jnp.float32)
    return total


def plain(acts, grad_out, w_gate, w_up, w_down):
    x = own_first(lax.all_gather(acts, "hid", axis=1, tiled=True), "tok")
    dy = own_first(lax.all_gather(grad_out, "hid", axis=1, tiled=True), "tok")
    gate = summed(rows_by_cols(x, w_gate).astype(jnp.bfloat16), "wid")
    up = summed(rows_by_cols(x, w_up).astype(jnp.bfloat16), "wid")
    dhid = summed(over_cols(dy, w_down).astype(jnp.bfloat16), "wid")
    hidden, d_gate, d_up = swiglu_grads(gate, up, dhid)
    back = home_rows(over_cols(d_gate, w_gate) + over_cols(d_up, w_up), "tok").astype(jnp.bfloat16)
    back = lax.psum_scatter(back, "hid", scatter_dimension=1, tiled=True)
    return (
        back,
        over_rows(x, d_gate).astype(jnp.bfloat16),
        over_rows(x, d_up).astype(jnp.bfloat16),
        over_rows(hidden, dy).astype(jnp.bfloat16),
    )


def nothing(*refs):
    pass


def ordered(value, *after):
    anywhere = pl.BlockSpec(memory_space=pl.ANY)
    return pl.pallas_call(
        nothing,
        out_shape=jax.ShapeDtypeStruct(value.shape, value.dtype),
        in_specs=[anywhere] * (1 + len(after)),
        out_specs=anywhere,
        input_output_aliases={0: 0},
        compiler_params=pltpu.CompilerParams(vmem_limit_bytes=MIB // 4),
    )(value, *after)


def arrange(value, far, near):
    me = lax.axis_index("hid")
    width = value.shape[1]
    own = (value, far)
    other = (near[:, :width], near[:, width:])
    odd, upper = lax.rem(me, 2) == 1, me >= 2
    blocks = []
    for pair in range(2):
        blocks.append(jnp.where(odd, other[pair], own[pair]))
        blocks.append(jnp.where(odd, own[pair], other[pair]))
    return jnp.concatenate([jnp.where(upper, blocks[i ^ 2], blocks[i]) for i in range(4)], axis=1)


def scatter_cols(value):
    me = lax.axis_index("hid")
    width = value.shape[1] // 4
    odd, upper = lax.rem(me, 2) == 1, me >= 2
    blocks = [value[:, i * width : (i + 1) * width] for i in range(4)]
    keep = [jnp.where(odd, blocks[2 * i + 1], blocks[2 * i]) for i in range(2)]
    give = [jnp.where(odd, blocks[2 * i], blocks[2 * i + 1]) for i in range(2)]
    near = swapped(jnp.concatenate(give, axis=1).astype(jnp.bfloat16), "hid", 1).astype(jnp.float32)
    sums = [keep[i] + near[:, i * width : (i + 1) * width] for i in range(2)]
    mine = jnp.where(upper, sums[1], sums[0])
    theirs = jnp.where(upper, sums[0], sums[1])
    return (mine + swapped(theirs.astype(jnp.bfloat16), "hid", 2).astype(jnp.float32)).astype(jnp.bfloat16)


def load_all(pairs, sem):
    copies = [pltpu.make_async_copy(source, target, sem.at[i]) for i, (source, target) in enumerate(pairs)]
    for copy in copies:
        copy.start()
    for copy in copies:
        copy.wait()


def columns_kernel(heights, starts, width, n_old, *refs):
    count = len(heights)
    x_refs, g_refs, u_refs = refs[:count], refs[count : 2 * count], refs[2 * count : 3 * count]
    gate_ref, up_ref, x_all, g_all, u_all, sem = refs[3 * count + n_old :]
    step = pl.program_id(0)

    @pl.when(step == 0)
    def _():
        pairs, top = [], 0
        for c, height in enumerate(heights):
            rows = pl.ds(top, height)
            pairs.append((x_refs[c], x_all.at[rows]))
            pairs.append((g_refs[c].at[:, pl.ds(starts[c], width)], g_all.at[rows]))
            pairs.append((u_refs[c].at[:, pl.ds(starts[c], width)], u_all.at[rows]))
            top += height
        load_all(pairs, sem)

    block = gate_ref.shape[0]
    x = x_all[:, pl.ds(pl.multiple_of(step * block, block), block)]
    gate_ref[...] = over_rows(x, g_all[...]).astype(gate_ref.dtype)
    up_ref[...] = over_rows(x, u_all[...]).astype(up_ref.dtype)


def column_grads(xs, gs, us, starts, part, parts, total, old):
    heights = [x.shape[0] for x in xs]
    tokens, features, width = sum(heights), xs[0].shape[1], total // parts
    block = 256
    anywhere = pl.BlockSpec(memory_space=pl.ANY)
    shape = jax.ShapeDtypeStruct((features, total), jnp.bfloat16)
    spec = pl.BlockSpec((block, width), lambda i: (i, part))
    first = 3 * len(xs)
    return pl.pallas_call(
        functools.partial(columns_kernel, heights, starts, width, len(old)),
        grid=(features // block,),
        out_shape=(shape, shape),
        in_specs=[anywhere] * (first + len(old)),
        out_specs=(spec, spec),
        scratch_shapes=[
            pltpu.VMEM((tokens, features), jnp.bfloat16),
            pltpu.VMEM((tokens, width), jnp.bfloat16),
            pltpu.VMEM((tokens, width), jnp.bfloat16),
            pltpu.SemaphoreType.DMA((first,)),
        ],
        input_output_aliases={first + i: i for i in range(len(old))},
        compiler_params=pltpu.CompilerParams(vmem_limit_bytes=12 * MIB),
        cost_estimate=pl.CostEstimate(
            flops=4 * tokens * features * width, bytes_accessed=4 * features * width, transcendentals=0
        ),
    )(*xs, *gs, *us, *old)


def rows_kernel(heights, starts, width, n_old, *refs):
    count = len(heights)
    h_refs, y_refs = refs[:count], refs[count : 2 * count]
    out_ref, h_all, y_all, sem = refs[2 * count + n_old :]
    step = pl.program_id(0)

    @pl.when(step == 0)
    def _():
        pairs, top = [], 0
        for c, height in enumerate(heights):
            rows = pl.ds(top, height)
            pairs.append((h_refs[c].at[:, pl.ds(starts[c], width)], h_all.at[rows]))
            pairs.append((y_refs[c], y_all.at[rows]))
            top += height
        load_all(pairs, sem)

    block = out_ref.shape[0]
    h = h_all[:, pl.ds(pl.multiple_of(step * block, block), block)]
    out_ref[...] = over_rows(h, y_all[...]).astype(out_ref.dtype)


def row_grads(hs, ys, starts, part, parts, total, old):
    heights = [y.shape[0] for y in ys]
    tokens, features, width = sum(heights), ys[0].shape[1], total // parts
    block = 128
    steps = width // block
    anywhere = pl.BlockSpec(memory_space=pl.ANY)
    first = 2 * len(ys)
    return pl.pallas_call(
        functools.partial(rows_kernel, heights, starts, width, len(old)),
        grid=(steps,),
        out_shape=jax.ShapeDtypeStruct((total, features), jnp.bfloat16),
        in_specs=[anywhere] * (first + len(old)),
        out_specs=pl.BlockSpec((block, features), lambda i: (part * steps + i, 0)),
        scratch_shapes=[
            pltpu.VMEM((tokens, width), jnp.bfloat16),
            pltpu.VMEM((tokens, features), jnp.bfloat16),
            pltpu.SemaphoreType.DMA((first,)),
        ],
        input_output_aliases={first + i: i for i in range(len(old))},
        compiler_params=pltpu.CompilerParams(vmem_limit_bytes=12 * MIB),
        cost_estimate=pl.CostEstimate(
            flops=2 * tokens * features * width, bytes_accessed=2 * features * width, transcendentals=0
        ),
    )(*hs, *ys, *old)


def forward(x, dy, w_gate, w_up, w_down, cuts):
    parts = []
    for lower, upper in cuts:
        gate = rows_by_cols(x, w_gate[:, lower:upper]).astype(jnp.bfloat16)
        up = rows_by_cols(x, w_up[:, lower:upper]).astype(jnp.bfloat16)
        dhid = over_cols(dy, w_down[lower:upper]).astype(jnp.bfloat16)
        parts.append((gate, up, dhid))
    return parts


def piped(acts, grad_out, w_gate, w_up, w_down):
    unit = acts.shape[0] // sum(SIXTEENTHS)
    bounds = [0]
    for size in SIXTEENTHS:
        bounds.append(bounds[-1] + size * unit)
    spans = list(zip(bounds[:-1], bounds[1:]))
    last = len(spans) - 1
    total = w_gate.shape[1]
    whole, halves = [(0, total)], [(0, total // 2), (total // 2, total)]

    lower, upper = spans[0]
    ready = []
    for value in (acts[lower:upper], grad_out[lower:upper]):
        far = swapped(value, "hid", 2)
        near = swapped(jnp.concatenate([value, far], axis=1), "hid", 1)
        ready.append(own_first(arrange(value, far, near), "tok"))
    inputs = [tuple(ready)]
    sums = [forward(*ready, w_gate, w_up, w_down, whole)]
    anchor = sums[0][0]

    grads, backs = [], []

    def backward(index):
        results, back = [], None
        for (lower, upper), partial in zip(halves if index == last else whole, sums[index]):
            others = [shifted(part, "wid", 1) for part in partial]
            if index < last:
                others[0] = ordered(others[0], sums[index + 1][-1][2])
            gate, up, dhid = [
                part.astype(jnp.float32) + other.astype(jnp.float32) for part, other in zip(partial, others)
            ]
            hidden, d_gate, d_up = swiglu_grads(gate, up, dhid)
            term = over_cols(d_gate, w_gate[:, lower:upper]) + over_cols(d_up, w_up[:, lower:upper])
            back = term if back is None else back + term
            results.append((hidden, d_gate, d_up))
        grads.append(results)
        backs.append(scatter_cols(home_rows(back, "tok")))

    for index in range(1, len(spans)):
        lower, upper = spans[index]
        rows = upper - lower
        both = jnp.concatenate([acts[lower:upper], grad_out[lower:upper]], axis=0)
        both = ordered(both, anchor[0] if index == 1 else near)
        far = swapped(both, "hid", 2)
        far = ordered(far, anchor[2])
        near = swapped(jnp.concatenate([both, far], axis=1), "hid", 1)
        mixed = arrange(both, far, near)
        theirs = shifted(mixed, "tok", 1)
        x = jnp.concatenate([mixed[:rows], theirs[:rows]], axis=0)
        dy = jnp.concatenate([mixed[rows:], theirs[rows:]], axis=0)
        inputs.append((x, dy))
        sums.append(forward(x, dy, w_gate, w_up, w_down, halves if index == last else whole))
        anchor = sums[index][0]
    for index in range(len(spans)):
        backward(index)

    xs, dys = [x for x, _ in inputs], [dy for _, dy in inputs]
    columns, rows = (), ()
    for part in range(2):
        starts = [part * (total // 2)] * last + [0]
        hs, gs, us = [[g[0][i] for g in grads[:last]] + [grads[last][part][i]] for i in range(3)]
        columns = column_grads(xs, gs, us, starts, part, 2, total, columns)
        rows = (row_grads(hs, dys, starts, part, 2, total, rows),)
    return jnp.concatenate(backs, axis=0), columns[0], columns[1], rows[0]


def shards(acts, grad_out, w_gate, w_up, w_down):
    sizes = tuple(lax.axis_size(axis) for axis in ("hid", "wid", "tok"))
    aligned = acts.shape[0] % (16 * sum(SIXTEENTHS)) == 0 and acts.shape[1] % 128 == 0 and w_gate.shape[1] % 256 == 0
    if sizes == (4, 2, 2) and aligned:
        return piped(acts, grad_out, w_gate, w_up, w_down)
    return plain(acts, grad_out, w_gate, w_up, w_down)


def solution(mesh):
    placed = (
        P(("groups", "tok"), ("wid", "hid")),
        P(("groups", "tok"), ("wid", "hid")),
        P("wid", ("hid", "tok")),
        P("wid", ("hid", "tok")),
        P(("hid", "tok"), "wid"),
    )
    return jax.shard_map(
        shards,
        mesh=mesh,
        in_specs=placed,
        out_specs=(
            P(("groups", "tok"), ("wid", "hid")),
            P(("groups", "wid"), ("hid", "tok")),
            P(("groups", "wid"), ("hid", "tok")),
            P(("groups", "hid", "tok"), "wid"),
        ),
        check_vma=False,
    )
```

```python
import functools

import jax
import jax.numpy as jnp
from jax import lax
from jax.experimental import pallas as pl
from jax.experimental.pallas import tpu as pltpu
from jax.sharding import PartitionSpec as P

PIECES = (1, 2, 1)
MIB = 1 << 20


def dot(left, right, dims):
    return lax.dot_general(left, right, (dims, ((), ())), preferred_element_type=jnp.float32)


def rows_by_cols(left, right):
    return dot(left, right, ((1,), (0,)))


def over_cols(left, right):
    return dot(left, right, ((1,), (1,)))


def over_rows(left, right):
    return dot(left, right, ((0,), (0,)))


def swiglu_grads(gate, up, dhid):
    sig = jax.nn.sigmoid(gate)
    hidden = (gate * sig * up).astype(jnp.bfloat16)
    d_gate = (dhid * up * sig * (1.0 + gate * (1.0 - sig))).astype(jnp.bfloat16)
    d_up = (dhid * gate * sig).astype(jnp.bfloat16)
    return hidden, d_gate, d_up


def shifted(value, axis, step):
    n = lax.axis_size(axis)
    return lax.ppermute(value, axis, [(i, (i + step) % n) for i in range(n)])


def swapped(value, axis, bit):
    n = lax.axis_size(axis)
    return lax.ppermute(value, axis, [(i, i ^ bit) for i in range(n)])


def summed(value, axis):
    total = value.astype(jnp.float32)
    for step in range(1, lax.axis_size(axis)):
        total = total + shifted(value, axis, step).astype(jnp.float32)
    return total


def own_first(value, axis):
    return jnp.concatenate([value] + [shifted(value, axis, step) for step in range(1, lax.axis_size(axis))], axis=0)


def home_rows(back, axis):
    n = lax.axis_size(axis)
    rows = back.shape[0] // n
    sent = back.astype(jnp.bfloat16)
    total = back[:rows]
    for step in range(1, n):
        block = sent[step * rows : (step + 1) * rows]
        total = total + shifted(block, axis, n - step).astype(jnp.float32)
    return total


def plain(acts, grad_out, w_gate, w_up, w_down):
    x = own_first(lax.all_gather(acts, "hid", axis=1, tiled=True), "tok")
    dy = own_first(lax.all_gather(grad_out, "hid", axis=1, tiled=True), "tok")
    gate = summed(rows_by_cols(x, w_gate).astype(jnp.bfloat16), "wid")
    up = summed(rows_by_cols(x, w_up).astype(jnp.bfloat16), "wid")
    dhid = summed(over_cols(dy, w_down).astype(jnp.bfloat16), "wid")
    hidden, d_gate, d_up = swiglu_grads(gate, up, dhid)
    back = home_rows(over_cols(d_gate, w_gate) + over_cols(d_up, w_up), "tok").astype(jnp.bfloat16)
    back = lax.psum_scatter(back, "hid", scatter_dimension=1, tiled=True)
    return (
        back,
        over_rows(x, d_gate).astype(jnp.bfloat16),
        over_rows(x, d_up).astype(jnp.bfloat16),
        over_rows(hidden, dy).astype(jnp.bfloat16),
    )


VMEM = pl.BlockSpec(memory_space=pltpu.VMEM)
ANYWHERE = pl.BlockSpec(memory_space=pl.ANY)


def local(kernel, outs, args, after=(), flops=0, moved=0, limit=8, scratch=(), out_specs=None):
    def body(*refs):
        kernel(refs[: len(args)], refs[len(args) + len(after) :])

    shapes = [jax.ShapeDtypeStruct(shape, dtype) for shape, dtype in outs]
    return pl.pallas_call(
        body,
        out_shape=shapes,
        in_specs=[VMEM] * len(args) + [ANYWHERE] * len(after),
        out_specs=out_specs if out_specs else [VMEM] * len(outs),
        scratch_shapes=list(scratch),
        compiler_params=pltpu.CompilerParams(vmem_limit_bytes=limit * MIB),
        cost_estimate=pl.CostEstimate(flops=flops, bytes_accessed=moved, transcendentals=0),
    )(*args, *after)


def lanes(index, width):
    return pl.ds(pl.multiple_of(index * width, width), width)


def cut_piece(acts, grad_out, lower, upper, after):
    rows, width = upper - lower, acts.shape[1]

    def kernel(ins, outs):
        outs[0][:rows] = ins[0][lower:upper]
        outs[0][rows:] = ins[1][lower:upper]

    return local(kernel, [((2 * rows, width), acts.dtype)], (acts, grad_out), after, limit=1)[0]


def pack(value, far, after=()):
    rows, width = value.shape

    def kernel(ins, outs):
        outs[0][:, :width] = ins[0][...]
        outs[0][:, width:] = ins[1][...]

    return local(kernel, [((rows, 2 * width), value.dtype)], (value, far), after, limit=1)[0]


def arrange(pair, near, after=()):
    rows, width = pair.shape[0], pair.shape[1] // 2

    def kernel(ins, outs):
        me = lax.axis_index("hid")
        for step, (source, at) in enumerate(((0, 0), (1, 0), (0, 1), (1, 1))):
            outs[0][:, lanes(me ^ step, width)] = ins[source][:, at * width : (at + 1) * width]

    return local(kernel, [((rows, 4 * width), pair.dtype)], (pair, near), after, limit=1)[0]


def blocks_of(width):
    full = width // 256
    return full, width - full * 256


def over_blocks(width, body):
    full, rest = blocks_of(width)

    @pl.loop(0, full)
    def _(j):
        body(lambda base: pl.ds(pl.multiple_of(base + j * 256, 128), 256))

    if rest:
        body(lambda base: pl.ds(base + full * 256, rest))


def forward(sources, weights, span, rows, after=()):
    lower, upper = span
    width, features, tokens = upper - lower, sources[0][0].shape[1], 2 * rows
    arrays = [array for own, theirs, _, _ in sources for array in (own, theirs)]

    def kernel(ins, refs):
        out, held = refs
        loaded = None
        for k, (_, _, first, down) in enumerate(sources):
            if loaded is None or arrays[2 * k] is not arrays[2 * loaded] or first != sources[loaded][2]:
                held[:rows] = ins[2 * k][first : first + rows]
                held[rows:] = ins[2 * k + 1][first : first + rows]
                loaded = k
            weight = ins[len(arrays) + k]
            top = k * tokens

            def product(at, weight=weight, top=top, down=down):
                if down:
                    value = over_cols(held[...], weight[at(lower), :])
                else:
                    value = rows_by_cols(held[...], weight[:, at(lower)])
                out[top : top + tokens, at(0)] = value.astype(out.dtype)

            over_blocks(width, product)

    return local(
        kernel,
        [((len(sources) * tokens, width), jnp.bfloat16)],
        (*arrays, *weights),
        after,
        flops=2 * len(sources) * tokens * features * width,
        scratch=[pltpu.VMEM((tokens, features), jnp.bfloat16)],
    )[0]


def backward(own, other, where, weights, span, rows, before, final, after=()):
    lower, upper = span
    width, features, tokens = upper - lower, weights[0].shape[0], 2 * rows
    count = len(own)
    ins_all = (*own, *other, *weights, *(() if before is None else (before,)))
    outs_all = [((tokens, width), jnp.bfloat16)] * 3
    outs_all += [((rows, features), jnp.float32), ((rows, features), jnp.bfloat16)] if final else [((tokens, features), jnp.float32)]

    def kernel(ins, outs):
        step = width // 7

        @pl.loop(0, 7)
        def _(j):
            at = lanes(j, step)

            def total(k):
                array, top = where[k]
                mine = ins[array][top : top + tokens, at].astype(jnp.float32)
                return mine + ins[count + array][top : top + tokens, at].astype(jnp.float32)

            for ref, value in zip(outs[:3], swiglu_grads(total(0), total(1), total(2))):
                ref[:, at] = value

        @pl.loop(0, features // 256)
        def _(j):
            at = lanes(j, 256)
            value = over_cols(outs[1][...], ins[2 * count][at, lower:upper])
            value = value + over_cols(outs[2][...], ins[2 * count + 1][at, lower:upper])
            if before is not None:
                value = value + ins[2 * count + 2][:, at]
            if final:
                outs[3][:, at] = value[:rows]
                outs[4][:, at] = value[rows:].astype(jnp.bfloat16)
            else:
                outs[3][:, at] = value

    return local(kernel, outs_all, ins_all, after, flops=4 * tokens * features * width)


def fold_near(value, theirs):
    rows, width = value.shape[0], value.shape[1] // 4

    def kernel(ins, outs):
        odd = lax.rem(lax.axis_index("hid"), 2)
        for i in range(2):
            at = slice(i * width, (i + 1) * width)
            for block, out in ((2 * i + odd, outs[0]), (2 * i + 1 - odd, outs[1])):
                source = lanes(block, width)
                out[:, at] = (ins[0][:, source] + ins[1][:, source].astype(jnp.float32)).astype(out.dtype)

    outs = [((rows, 2 * width), jnp.float32), ((rows, 2 * width), jnp.bfloat16)]
    return local(kernel, outs, (value, theirs), limit=4)


def fold_far(value, theirs):
    rows, width = value.shape[0], value.shape[1] // 2

    def kernel(ins, outs):
        upper = lax.div(lax.axis_index("hid"), 2)
        for block, out in ((upper, outs[0]), (1 - upper, outs[1])):
            source = lanes(block, width)
            out[...] = (ins[0][:, source] + ins[1][:, source].astype(jnp.float32)).astype(out.dtype)

    outs = [((rows, width), jnp.float32), ((rows, width), jnp.bfloat16)]
    return local(kernel, outs, (value, theirs), limit=4)


def fold_last(pairs):
    heights = [mine.shape[0] for mine, _ in pairs]
    width = pairs[0][0].shape[1]

    def kernel(ins, outs):
        top = 0
        for c, height in enumerate(heights):
            value = ins[2 * c][...] + ins[2 * c + 1][...].astype(jnp.float32)
            outs[0][top : top + height] = value.astype(jnp.bfloat16)
            top += height

    return local(
        kernel,
        [((sum(heights), width), jnp.bfloat16)],
        [array for pair in pairs for array in pair],
        limit=4,
        out_specs=[pl.BlockSpec((sum(heights), width), lambda: (0, 0))],
    )[0]


def scatter(mine, sent):
    keep, give = fold_near(mine, shifted(sent, "tok", 1))
    mine, give_far = fold_far(keep, swapped(give, "hid", 1))
    return keep, (mine, swapped(give_far, "hid", 2))


def stack(target, pieces, refs, at=None):
    top = 0
    for index, first, rows, column in pieces:
        width = target.shape[1]
        target[top : top + rows] = refs[index][first : first + rows, column : column + width]
        top += rows


def gradients(kernel, outs, arrays, old, grid, specs, scratch, after, flops, moved):
    def body(*refs):
        kernel(refs[: len(arrays)], refs[len(arrays) + len(old) + len(after) :])

    return pl.pallas_call(
        body,
        grid=grid,
        out_shape=[jax.ShapeDtypeStruct(shape, jnp.bfloat16) for shape in outs],
        in_specs=[VMEM] * len(arrays) + [ANYWHERE] * (len(old) + len(after)),
        out_specs=specs,
        scratch_shapes=scratch,
        input_output_aliases={len(arrays) + i: i for i in range(len(old))},
        compiler_params=pltpu.CompilerParams(vmem_limit_bytes=14 * MIB),
        cost_estimate=pl.CostEstimate(flops=flops, bytes_accessed=moved, transcendentals=0),
    )(*arrays, *old, *after)


def column_grads(xs, gs, us, part, parts, total, old, after=()):
    arrays = [p[0] for p in (*xs, *gs, *us)]
    n_x, n_g = len(xs), len(gs)
    tokens, features, width = sum(p[2] for p in xs), xs[0][0].shape[1], total // parts
    block = 512

    def kernel(ins, refs):
        gate_out, up_out, g_all, u_all = refs
        step = pl.program_id(0)

        @pl.when(step == 0)
        def _():
            stack(g_all, [(n_x + i, *p[1:]) for i, p in enumerate(gs)], ins)
            stack(u_all, [(n_x + n_g + i, *p[1:]) for i, p in enumerate(us)], ins)

        at = lanes(step, block)
        x = jnp.concatenate([ins[i][p[1] : p[1] + p[2], at] for i, p in enumerate(xs)], axis=0).T
        gate_out[...] = rows_by_cols(x, g_all[...]).astype(gate_out.dtype)
        up_out[...] = rows_by_cols(x, u_all[...]).astype(up_out.dtype)

    spec = pl.BlockSpec((block, width), lambda i: (i, part))
    scratch = [pltpu.VMEM((tokens, width), jnp.bfloat16)] * 2
    return gradients(
        kernel, [(features, total)] * 2, arrays, old, (features // block,), [spec, spec], scratch, after,
        4 * tokens * features * width, 4 * features * width,
    )


def row_grads(hs, ys, part, parts, total, old, after=()):
    arrays = [p[0] for p in (*hs, *ys)]
    n_h = len(hs)
    tokens, features, width = sum(p[2] for p in ys), ys[0][0].shape[1], total // parts
    block = 256

    def kernel(ins, refs):
        out, h_all = refs
        step = pl.program_id(0)

        @pl.when(step == 0)
        def _():
            pieces = [ins[i][p[1] : p[1] + p[2], p[3] : p[3] + width] for i, p in enumerate(hs)]
            h_all[...] = jnp.concatenate(pieces, axis=0).T

        at = lanes(step, block)
        y = jnp.concatenate([ins[n_h + i][p[1] : p[1] + p[2], at] for i, p in enumerate(ys)], axis=0)
        out[...] = rows_by_cols(h_all[...], y).astype(out.dtype)

    spec = pl.BlockSpec((width, block), lambda i: (part, i))
    scratch = [pltpu.VMEM((width, tokens), jnp.bfloat16)]
    return gradients(
        kernel, [(total, features)], arrays, old, (features // block,), [spec], scratch, after,
        2 * tokens * features * width, 2 * features * width,
    )


def piped(acts, grad_out, w_gate, w_up, w_down):
    unit = acts.shape[0] // sum(PIECES)
    bounds = [0]
    for size in PIECES:
        bounds.append(bounds[-1] + size * unit)
    spans = list(zip(bounds[:-1], bounds[1:]))
    heights = [upper - lower for lower, upper in spans]
    last = len(spans) - 1
    total = w_gate.shape[1]
    whole, halves = (0, total), ((0, total // 2), (total // 2, total))
    back_weights = (w_gate, w_up)

    lower, upper = spans[0]
    rows = heights[0]
    mixed, theirs = [], []
    for value in (acts[lower:upper], grad_out[lower:upper]):
        pair = pack(value, swapped(value, "hid", 2))
        mixed.append(arrange(pair, swapped(pair, "hid", 1)))
        theirs.append(shifted(mixed[-1], "tok", 1))
    x, dy = [(mixed[i], theirs[i], 0) for i in range(2)]
    gate = forward([(*x, False)], (w_gate,), whole, rows)
    rest = forward([(*x, False), (*dy, True)], (w_up, w_down), whole, rows, (gate,))
    tokens = 2 * rows
    inputs = [(x, dy)]
    sums = [[((gate, rest), ((0, 0), (1, 0), (1, tokens)))]]
    anchor, cut_after = rest, mixed[1]

    grads, scattered = [None] * len(spans), [None] * len(spans)

    def backward_piece(index, after):
        (own, where), = sums[index]
        other = [shifted(part, "wid", 1) for part in own]
        hidden, d_gate, d_up, mine, sent = backward(
            own, other, where, back_weights, whole, heights[index], None, True, after
        )
        grads[index] = (hidden, d_gate, d_up)
        return scatter(mine, sent)[1]

    for index in range(1, len(spans)):
        rows = heights[index]
        tokens = 2 * rows
        both = cut_piece(acts, grad_out, *spans[index], (cut_after,))
        pair = pack(both, swapped(both, "hid", 2), (anchor,))
        cut_after = pair
        own = arrange(pair, swapped(pair, "hid", 1))
        other = shifted(own, "tok", 1)
        x, dy = (own, other, 0), (own, other, rows)
        inputs.append((x, dy))
        sources = [(*x, False), (*x, False), (*dy, True)]
        where = ((0, 0), (0, tokens), (0, 2 * tokens))
        done, after = [], ()
        for span in halves if index == last else (whole,):
            part = forward(sources, (w_gate, w_up, w_down), span, rows, after)
            done.append(((part,), where))
            after = (part,)
        sums.append(done)
        anchor = after[0]
        scattered[index - 1] = backward_piece(index - 1, (anchor,))

    rows = heights[last]
    xs, ys = [], []
    for index, (x, dy) in enumerate(inputs):
        for pieces, (own, other, first) in ((xs, x), (ys, dy)):
            pieces.append((own, first, heights[index], 0))
            pieces.append((other, first, heights[index], 0))
    before, after, columns, downs = None, (), (), ()
    for part, (own, where) in enumerate(sums[last]):
        other = [shifted(value, "wid", 1) for value in own]
        results = backward(own, other, where, back_weights, halves[part], rows, before, part == 1, after)
        before = results[3]
        hs, gs, us = [
            [(grads[c][k], 0, 2 * heights[c], halves[part][0]) for c in range(last)] + [(results[k], 0, 2 * rows, 0)]
            for k in range(3)
        ]
        downs = row_grads(hs, ys, part, 2, total, downs)
        if part == 1:
            keep, scattered[last] = scatter(*results[3:])
            after = (keep,)
        columns = column_grads(xs, gs, us, part, 2, total, columns, after if part == 1 else ())
        after = (downs[0], columns[0])
    return fold_last(scattered), columns[0], columns[1], downs[0]


def shards(acts, grad_out, w_gate, w_up, w_down):
    sizes = tuple(lax.axis_size(axis) for axis in ("hid", "wid", "tok"))
    aligned = acts.shape[0] % (16 * sum(PIECES)) == 0 and acts.shape[1] % 128 == 0 and w_gate.shape[0] % 512 == 0 and w_gate.shape[1] % 1792 == 0
    if sizes == (4, 2, 2) and aligned:
        return piped(acts, grad_out, w_gate, w_up, w_down)
    return plain(acts, grad_out, w_gate, w_up, w_down)


def solution(mesh):
    placed = (
        P(("groups", "tok"), ("wid", "hid")),
        P(("groups", "tok"), ("wid", "hid")),
        P("wid", ("hid", "tok")),
        P("wid", ("hid", "tok")),
        P(("hid", "tok"), "wid"),
    )
    return jax.shard_map(
        shards,
        mesh=mesh,
        in_specs=placed,
        out_specs=(
            P(("groups", "tok"), ("wid", "hid")),
            P(("groups", "wid"), ("hid", "tok")),
            P(("groups", "wid"), ("hid", "tok")),
            P(("groups", "hid", "tok"), "wid"),
        ),
        check_vma=False,
    )
```

```python
import functools

import jax
import jax.numpy as jnp
from jax import lax
from jax.experimental import pallas as pl
from jax.experimental.pallas import tpu as pltpu
from jax.sharding import PartitionSpec as P

PIECES = (1, 1, 1)
MIB = 1 << 20


def dot(left, right, dims):
    return lax.dot_general(left, right, (dims, ((), ())), preferred_element_type=jnp.float32)


def rows_by_cols(left, right):
    return dot(left, right, ((1,), (0,)))


def over_cols(left, right):
    return dot(left, right, ((1,), (1,)))


def over_rows(left, right):
    return dot(left, right, ((0,), (0,)))


def swiglu_grads(gate, up, dhid):
    sig = jax.nn.sigmoid(gate)
    hidden = (gate * sig * up).astype(jnp.bfloat16)
    d_gate = (dhid * up * sig * (1.0 + gate * (1.0 - sig))).astype(jnp.bfloat16)
    d_up = (dhid * gate * sig).astype(jnp.bfloat16)
    return hidden, d_gate, d_up


def shifted(value, axis, step):
    n = lax.axis_size(axis)
    return lax.ppermute(value, axis, [(i, (i + step) % n) for i in range(n)])


def swapped(value, axis, bit):
    n = lax.axis_size(axis)
    return lax.ppermute(value, axis, [(i, i ^ bit) for i in range(n)])


def summed(value, axis):
    total = value.astype(jnp.float32)
    for step in range(1, lax.axis_size(axis)):
        total = total + shifted(value, axis, step).astype(jnp.float32)
    return total


def own_first(value, axis):
    return jnp.concatenate([value] + [shifted(value, axis, step) for step in range(1, lax.axis_size(axis))], axis=0)


def home_rows(back, axis):
    n = lax.axis_size(axis)
    rows = back.shape[0] // n
    sent = back.astype(jnp.bfloat16)
    total = back[:rows]
    for step in range(1, n):
        block = sent[step * rows : (step + 1) * rows]
        total = total + shifted(block, axis, n - step).astype(jnp.float32)
    return total


def plain(acts, grad_out, w_gate, w_up, w_down):
    x = own_first(lax.all_gather(acts, "hid", axis=1, tiled=True), "tok")
    dy = own_first(lax.all_gather(grad_out, "hid", axis=1, tiled=True), "tok")
    gate = summed(rows_by_cols(x, w_gate).astype(jnp.bfloat16), "wid")
    up = summed(rows_by_cols(x, w_up).astype(jnp.bfloat16), "wid")
    dhid = summed(over_cols(dy, w_down).astype(jnp.bfloat16), "wid")
    hidden, d_gate, d_up = swiglu_grads(gate, up, dhid)
    back = home_rows(over_cols(d_gate, w_gate) + over_cols(d_up, w_up), "tok").astype(jnp.bfloat16)
    back = lax.psum_scatter(back, "hid", scatter_dimension=1, tiled=True)
    return (
        back,
        over_rows(x, d_gate).astype(jnp.bfloat16),
        over_rows(x, d_up).astype(jnp.bfloat16),
        over_rows(hidden, dy).astype(jnp.bfloat16),
    )


VMEM = pl.BlockSpec(memory_space=pltpu.VMEM)
ANYWHERE = pl.BlockSpec(memory_space=pl.ANY)


def declared(cost):
    return pl.CostEstimate(flops=int(cost * 1.15e9), bytes_accessed=0, transcendentals=0)


def local(kernel, outs, args, after=(), limit=12, scratch=(), out_specs=None, resident=(), cost=0.1):
    waits = len(resident) + len(after)

    def body(*refs):
        kernel(refs[: len(args)], refs[len(args) + waits :])

    shapes = [jax.ShapeDtypeStruct(shape, dtype) for shape, dtype in outs]
    return pl.pallas_call(
        body,
        out_shape=shapes,
        in_specs=[VMEM] * (len(args) + len(resident)) + [ANYWHERE] * len(after),
        out_specs=out_specs if out_specs else [VMEM] * len(outs),
        scratch_shapes=list(scratch),
        compiler_params=pltpu.CompilerParams(vmem_limit_bytes=limit * MIB),
        cost_estimate=declared(cost),
    )(*args, *resident, *after)


def lanes(index, width):
    return pl.ds(pl.multiple_of(index * width, width), width)


def cut_piece(acts, grad_out, lower, upper, after):
    rows, width = upper - lower, acts.shape[1]

    def kernel(ins, outs):
        outs[0][:rows] = ins[0][lower:upper]
        outs[0][rows:] = ins[1][lower:upper]

    return local(kernel, [((2 * rows, width), acts.dtype)], (acts, grad_out), after, limit=1)[0]


def pack(value, far, after=(), resident=(), cost=0.1):
    rows, width = value.shape

    def kernel(ins, outs):
        outs[0][:, :width] = ins[0][...]
        outs[0][:, width:] = ins[1][...]

    return local(kernel, [((rows, 2 * width), value.dtype)], (value, far), after, 1, resident=resident, cost=cost)[0]


def arrange(pair, near, resident=(), cost=0.1):
    rows, width = pair.shape[0], pair.shape[1] // 2

    def kernel(ins, outs):
        me = lax.axis_index("hid")
        for step, (source, at) in enumerate(((0, 0), (1, 0), (0, 1), (1, 1))):
            outs[0][:, lanes(me ^ step, width)] = ins[source][:, at * width : (at + 1) * width]

    return local(kernel, [((rows, 4 * width), pair.dtype)], (pair, near), (), 1, resident=resident, cost=cost)[0]


def over_blocks(width, step, body):
    for base in range(0, width, step):
        body(base, min(step, width - base))


def forward(sources, weights, span, rows, after=(), cost=0.3):
    lower, upper = span
    width, features, tokens = upper - lower, sources[0][0].shape[1], 2 * rows
    arrays = [array for own, theirs, _, _ in sources for array in (own, theirs)]

    def kernel(ins, refs):
        out, held = refs
        loaded = None
        for k, (_, _, first, down) in enumerate(sources):
            if loaded is None or arrays[2 * k] is not arrays[2 * loaded] or first != sources[loaded][2]:
                held[:rows] = ins[2 * k][first : first + rows]
                held[rows:] = ins[2 * k + 1][first : first + rows]
                loaded = k
            weight = ins[len(arrays) + k]
            top = k * tokens

            def product(base, size, weight=weight, top=top, down=down):
                at = slice(lower + base, lower + base + size)
                if down:
                    value = over_cols(held[...], weight[at, :])
                else:
                    value = rows_by_cols(held[...], weight[:, at])
                out[top : top + tokens, base : base + size] = value.astype(out.dtype)

            over_blocks(width, 896, product)

    return local(
        kernel,
        [((len(sources) * tokens, width), jnp.bfloat16)],
        (*arrays, *weights),
        after,
        scratch=[pltpu.VMEM((tokens, features), jnp.bfloat16)],
        cost=cost,
    )[0]


def backward(own, other, where, weights, span, rows, before, final, after=(), cost=1.0):
    lower, upper = span
    width, features, tokens = upper - lower, weights[0].shape[0], 2 * rows
    count = len(own)
    ins_all = (*own, *other, *weights, *(() if before is None else (before,)))
    outs_all = [((tokens, width), jnp.bfloat16)] * 3
    outs_all += [((rows, features), jnp.float32), ((rows, features), jnp.bfloat16)] if final else [((tokens, features), jnp.float32)]

    def kernel(ins, outs):
        step = width // 7

        @pl.loop(0, 7)
        def _(j):
            at = lanes(j, step)

            def total(k):
                array, top = where[k]
                mine = ins[array][top : top + tokens, at].astype(jnp.float32)
                return mine + ins[count + array][top : top + tokens, at].astype(jnp.float32)

            for ref, value in zip(outs[:3], swiglu_grads(total(0), total(1), total(2))):
                ref[:, at] = value

        def product(base, size):
            at = slice(base, base + size)
            value = over_cols(outs[1][...], ins[2 * count][at, lower:upper])
            value = value + over_cols(outs[2][...], ins[2 * count + 1][at, lower:upper])
            if before is not None:
                value = value + ins[2 * count + 2][:, at]
            if final:
                outs[3][:, at] = value[:rows]
                outs[4][:, at] = value[rows:].astype(jnp.bfloat16)
            else:
                outs[3][:, at] = value

        over_blocks(features, 1024, product)

    return local(kernel, outs_all, ins_all, after, cost=cost)


def fold_near(value, theirs):
    rows, width = value.shape[0], value.shape[1] // 4

    def kernel(ins, outs):
        odd = lax.rem(lax.axis_index("hid"), 2)
        for i in range(2):
            at = slice(i * width, (i + 1) * width)
            for block, out in ((2 * i + odd, outs[0]), (2 * i + 1 - odd, outs[1])):
                source = lanes(block, width)
                out[:, at] = (ins[0][:, source] + ins[1][:, source].astype(jnp.float32)).astype(out.dtype)

    outs = [((rows, 2 * width), jnp.float32), ((rows, 2 * width), jnp.bfloat16)]
    return local(kernel, outs, (value, theirs), limit=4)


def fold_far(value, theirs):
    rows, width = value.shape[0], value.shape[1] // 2

    def kernel(ins, outs):
        upper = lax.div(lax.axis_index("hid"), 2)
        for block, out in ((upper, outs[0]), (1 - upper, outs[1])):
            source = lanes(block, width)
            out[...] = (ins[0][:, source] + ins[1][:, source].astype(jnp.float32)).astype(out.dtype)

    outs = [((rows, width), jnp.float32), ((rows, width), jnp.bfloat16)]
    return local(kernel, outs, (value, theirs), limit=4)


def fold_last(mine, theirs, earlier=()):
    heights = [piece.shape[0] for piece in earlier]
    rows, width = mine.shape
    shape = (sum(heights) + rows, width)

    def kernel(ins, outs):
        top = 0
        for c, height in enumerate(heights):
            outs[0][top : top + height] = ins[2 + c][...]
            top += height
        outs[0][top:] = (ins[0][...] + ins[1][...].astype(jnp.float32)).astype(jnp.bfloat16)

    specs = [pl.BlockSpec(shape, lambda: (0, 0))] if earlier else None
    return local(kernel, [(shape, jnp.bfloat16)], (mine, theirs, *earlier), limit=4, out_specs=specs)[0]


def stack(target, pieces, refs, at=None):
    top = 0
    for index, first, rows, column in pieces:
        width = target.shape[1]
        target[top : top + rows] = refs[index][first : first + rows, column : column + width]
        top += rows


def gradients(kernel, outs, arrays, old, grid, specs, scratch, after, cost):
    def body(*refs):
        kernel(refs[: len(arrays)], refs[len(arrays) + len(old) + len(after) :])

    outs, specs = [*outs, (16, 128)], [*specs, VMEM]
    return pl.pallas_call(
        body,
        grid=grid,
        out_shape=[jax.ShapeDtypeStruct(shape, jnp.bfloat16) for shape in outs],
        in_specs=[VMEM] * len(arrays) + [ANYWHERE] * (len(old) + len(after)),
        out_specs=specs,
        scratch_shapes=scratch,
        input_output_aliases={len(arrays) + i: i for i in range(len(old))},
        compiler_params=pltpu.CompilerParams(vmem_limit_bytes=14 * MIB),
        cost_estimate=declared(cost),
    )(*arrays, *old, *after)


def column_grads(xs, gs, us, part, parts, total, old, after=()):
    arrays = [p[0] for p in (*xs, *gs, *us)]
    n_x, n_g = len(xs), len(gs)
    tokens, features, width = sum(p[2] for p in xs), xs[0][0].shape[1], total // parts
    block = 512

    def kernel(ins, refs):
        gate_out, up_out, token, g_all, u_all = refs
        step = pl.program_id(0)

        @pl.when(step == 0)
        def _():
            token[...] = jnp.zeros_like(token)
            stack(g_all, [(n_x + i, *p[1:]) for i, p in enumerate(gs)], ins)
            stack(u_all, [(n_x + n_g + i, *p[1:]) for i, p in enumerate(us)], ins)

        at = lanes(step, block)
        x = jnp.concatenate([ins[i][p[1] : p[1] + p[2], at] for i, p in enumerate(xs)], axis=0).T
        gate_out[...] = rows_by_cols(x, g_all[...]).astype(gate_out.dtype)
        up_out[...] = rows_by_cols(x, u_all[...]).astype(up_out.dtype)

    spec = pl.BlockSpec((block, width), lambda i: (i, part))
    scratch = [pltpu.VMEM((tokens, width), jnp.bfloat16)] * 2
    return gradients(
        kernel, [(features, total)] * 2, arrays, old, (features // block,), [spec, spec], scratch, after, 5.0
    )


def row_grads(hs, ys, part, parts, total, old, after=()):
    arrays = [p[0] for p in (*hs, *ys)]
    n_h = len(hs)
    tokens, features, width = sum(p[2] for p in ys), ys[0][0].shape[1], total // parts
    block = 256

    def kernel(ins, refs):
        out, token, h_all = refs
        step = pl.program_id(0)

        @pl.when(step == 0)
        def _():
            token[...] = jnp.zeros_like(token)
            pieces = [ins[i][p[1] : p[1] + p[2], p[3] : p[3] + width] for i, p in enumerate(hs)]
            h_all[...] = jnp.concatenate(pieces, axis=0).T

        at = lanes(step, block)
        y = jnp.concatenate([ins[n_h + i][p[1] : p[1] + p[2], at] for i, p in enumerate(ys)], axis=0)
        out[...] = rows_by_cols(h_all[...], y).astype(out.dtype)

    spec = pl.BlockSpec((width, block), lambda i: (part, i))
    scratch = [pltpu.VMEM((width, tokens), jnp.bfloat16)]
    return gradients(
        kernel, [(total, features)], arrays, old, (features // block,), [spec], scratch, after, 3.0
    )


def piped(acts, grad_out, w_gate, w_up, w_down):
    unit = acts.shape[0] // sum(PIECES)
    bounds = [0]
    for size in PIECES:
        bounds.append(bounds[-1] + size * unit)
    spans = list(zip(bounds[:-1], bounds[1:]))
    heights = [upper - lower for lower, upper in spans]
    last = len(spans) - 1
    total = w_gate.shape[1]
    whole, halves = (0, total), ((0, total // 2), (total // 2, total))
    back_weights = (w_gate, w_up)

    lower, upper = spans[0]
    rows = heights[0]
    mixed, theirs = [], []
    for value in (acts, grad_out):
        value = value[lower:upper]
        pair = pack(value, swapped(value, "hid", 2), cost=3.0)
        mixed.append(arrange(pair, swapped(pair, "hid", 1), cost=3.0))
        theirs.append(shifted(mixed[-1], "tok", 1))
    x, dy = [(mixed[i], theirs[i], 0) for i in range(2)]
    gate_up = forward([(*x, False), (*x, False)], (w_gate, w_up), whole, rows)
    dhid = forward([(*dy, True)], (w_down,), whole, rows, (gate_up,))
    inputs = [(x, dy)]
    sums = [[((gate_up, dhid), ((0, 0), (0, 2 * rows), (1, 0)))]]

    def gather_piece(index, cut_after, pack_after):
        rows = heights[index]
        both = cut_piece(acts, grad_out, *spans[index], cut_after)
        pair = pack(both, swapped(both, "hid", 2), pack_after)
        own = arrange(pair, swapped(pair, "hid", 1))
        other = shifted(own, "tok", 1)
        inputs.append(((own, other, 0), (own, other, rows)))
        return pair

    def forward_piece(index, after):
        x, dy = inputs[index]
        rows = heights[index]
        where = ((0, 0), (0, 2 * rows), (0, 4 * rows))
        done = []
        for span in halves if index == last else (whole,):
            part = forward([(*x, False), (*x, False), (*dy, True)], (w_gate, w_up, w_down), span, rows, after)
            done.append(((part,), where))
            after = (part,)
        sums.append(done)
        return after

    def backward_piece(index, part, before, final, after):
        own, where = sums[index][part]
        span = halves[part] if index == last else whole
        other = [shifted(value, "wid", 1) for value in own]
        cost = 1.0 if index == last else 60.0
        return backward(own, other, where, back_weights, span, heights[index], before, final, after, cost)

    def near_step(results):
        return fold_near(results[3], shifted(results[4], "tok", 1))

    def far_step(near):
        return fold_far(near[0], swapped(near[1], "hid", 1))

    def end_step(far, earlier=()):
        return fold_last(far[0], swapped(far[1], "hid", 2), earlier)

    pair = gather_piece(1, (mixed[1],), (dhid,))
    done = forward_piece(1, ())
    grads = [backward_piece(0, 0, None, True, done)]
    gather_piece(2, (pair,), (grads[0][0],))
    near = near_step(grads[0])
    done = forward_piece(2, (near[0],))
    far = far_step(near)
    grads.append(backward_piece(1, 0, None, True, (*done, far[0])))
    finished = [end_step(far)]

    xs, ys = [], []
    for index, (x, dy) in enumerate(inputs):
        for pieces, (own, other, first) in ((xs, x), (ys, dy)):
            pieces.append((own, first, heights[index], 0))
            pieces.append((other, first, heights[index], 0))

    def with_last(results, k, part):
        pieces = [(grads[c][k], 0, 2 * heights[c], halves[part][0]) for c in range(last)]
        return pieces + [(results[k], 0, 2 * heights[last], 0)]

    first = backward_piece(last, 0, None, False, (grads[1][0], finished[0]))
    near = near_step(grads[1])
    down, down_token = row_grads(with_last(first, 0, 0), ys, 0, 2, total, (), (near[0],))
    far = far_step(near)
    gate, up, token = column_grads(
        xs, with_last(first, 1, 0), with_last(first, 2, 0), 0, 2, total, (), (far[0], down_token)
    )
    finished.append(end_step(far))
    second = backward_piece(last, 1, first[3], True, (token, finished[1]))
    near = near_step(second)
    down, down_token = row_grads(with_last(second, 0, 1), ys, 1, 2, total, (down,), ())
    far = far_step(near)
    gate, up, _ = column_grads(
        xs, with_last(second, 1, 1), with_last(second, 2, 1), 1, 2, total, (gate, up), (near[0], down_token)
    )
    return end_step(far, finished), gate, up, down


def shards(acts, grad_out, w_gate, w_up, w_down):
    sizes = tuple(lax.axis_size(axis) for axis in ("hid", "wid", "tok"))
    aligned = acts.shape[0] % (16 * sum(PIECES)) == 0 and acts.shape[1] % 128 == 0 and w_gate.shape[0] % 512 == 0 and w_gate.shape[1] % 1792 == 0
    if sizes == (4, 2, 2) and aligned:
        return piped(acts, grad_out, w_gate, w_up, w_down)
    return plain(acts, grad_out, w_gate, w_up, w_down)


def solution(mesh):
    placed = (
        P(("groups", "tok"), ("wid", "hid")),
        P(("groups", "tok"), ("wid", "hid")),
        P("wid", ("hid", "tok")),
        P("wid", ("hid", "tok")),
        P(("hid", "tok"), "wid"),
    )
    return jax.shard_map(
        shards,
        mesh=mesh,
        in_specs=placed,
        out_specs=(
            P(("groups", "tok"), ("wid", "hid")),
            P(("groups", "wid"), ("hid", "tok")),
            P(("groups", "wid"), ("hid", "tok")),
            P(("groups", "hid", "tok"), "wid"),
        ),
        check_vma=False,
    )
```

```python
import functools

import jax
import jax.numpy as jnp
from jax import lax
from jax.experimental import pallas as pl
from jax.experimental.pallas import tpu as pltpu
from jax.sharding import PartitionSpec as P

PIECES = (1, 1, 1)
MIB = 1 << 20


def dot(left, right, dims):
    return lax.dot_general(left, right, (dims, ((), ())), preferred_element_type=jnp.float32)


def rows_by_cols(left, right):
    return dot(left, right, ((1,), (0,)))


def over_cols(left, right):
    return dot(left, right, ((1,), (1,)))


def over_rows(left, right):
    return dot(left, right, ((0,), (0,)))


def swiglu_grads(gate, up, dhid):
    sig = jax.nn.sigmoid(gate)
    hidden = (gate * sig * up).astype(jnp.bfloat16)
    d_gate = (dhid * up * sig * (1.0 + gate * (1.0 - sig))).astype(jnp.bfloat16)
    d_up = (dhid * gate * sig).astype(jnp.bfloat16)
    return hidden, d_gate, d_up


def shifted(value, axis, step):
    n = lax.axis_size(axis)
    return lax.ppermute(value, axis, [(i, (i + step) % n) for i in range(n)])


def swapped(value, axis, bit):
    n = lax.axis_size(axis)
    return lax.ppermute(value, axis, [(i, i ^ bit) for i in range(n)])


def summed(value, axis):
    total = value.astype(jnp.float32)
    for step in range(1, lax.axis_size(axis)):
        total = total + shifted(value, axis, step).astype(jnp.float32)
    return total


def own_first(value, axis):
    return jnp.concatenate([value] + [shifted(value, axis, step) for step in range(1, lax.axis_size(axis))], axis=0)


def home_rows(back, axis):
    n = lax.axis_size(axis)
    rows = back.shape[0] // n
    sent = back.astype(jnp.bfloat16)
    total = back[:rows]
    for step in range(1, n):
        block = sent[step * rows : (step + 1) * rows]
        total = total + shifted(block, axis, n - step).astype(jnp.float32)
    return total


def plain(acts, grad_out, w_gate, w_up, w_down):
    x = own_first(lax.all_gather(acts, "hid", axis=1, tiled=True), "tok")
    dy = own_first(lax.all_gather(grad_out, "hid", axis=1, tiled=True), "tok")
    gate = summed(rows_by_cols(x, w_gate).astype(jnp.bfloat16), "wid")
    up = summed(rows_by_cols(x, w_up).astype(jnp.bfloat16), "wid")
    dhid = summed(over_cols(dy, w_down).astype(jnp.bfloat16), "wid")
    hidden, d_gate, d_up = swiglu_grads(gate, up, dhid)
    back = home_rows(over_cols(d_gate, w_gate) + over_cols(d_up, w_up), "tok").astype(jnp.bfloat16)
    back = lax.psum_scatter(back, "hid", scatter_dimension=1, tiled=True)
    return (
        back,
        over_rows(x, d_gate).astype(jnp.bfloat16),
        over_rows(x, d_up).astype(jnp.bfloat16),
        over_rows(hidden, dy).astype(jnp.bfloat16),
    )


VMEM = pl.BlockSpec(memory_space=pltpu.VMEM)
ANYWHERE = pl.BlockSpec(memory_space=pl.ANY)


def declared(cost):
    return pl.CostEstimate(flops=int(cost * 1.15e9), bytes_accessed=0, transcendentals=0)


def local(kernel, outs, args, after=(), limit=12, scratch=(), out_specs=None, resident=(), cost=0.1):
    waits = len(resident) + len(after)

    def body(*refs):
        kernel(refs[: len(args)], refs[len(args) + waits :])

    shapes = [jax.ShapeDtypeStruct(shape, dtype) for shape, dtype in outs]
    return pl.pallas_call(
        body,
        out_shape=shapes,
        in_specs=[VMEM] * (len(args) + len(resident)) + [ANYWHERE] * len(after),
        out_specs=out_specs if out_specs else [VMEM] * len(outs),
        scratch_shapes=list(scratch),
        compiler_params=pltpu.CompilerParams(vmem_limit_bytes=limit * MIB),
        cost_estimate=declared(cost),
    )(*args, *resident, *after)


def lanes(index, width):
    return pl.ds(pl.multiple_of(index * width, width), width)


def cut_piece(acts, grad_out, lower, upper, after):
    rows, width = upper - lower, acts.shape[1]

    def kernel(ins, outs):
        outs[0][:rows] = ins[0][lower:upper]
        outs[0][rows:] = ins[1][lower:upper]

    return local(kernel, [((2 * rows, width), acts.dtype)], (acts, grad_out), after, limit=1)[0]


def pack(value, far, after=(), resident=(), cost=0.1):
    rows, width = value.shape

    def kernel(ins, outs):
        outs[0][:, :width] = ins[0][...]
        outs[0][:, width:] = ins[1][...]

    return local(kernel, [((rows, 2 * width), value.dtype)], (value, far), after, 1, resident=resident, cost=cost)[0]


def arrange(pair, near, resident=(), cost=0.1):
    rows, width = pair.shape[0], pair.shape[1] // 2

    def kernel(ins, outs):
        me = lax.axis_index("hid")
        for step, (source, at) in enumerate(((0, 0), (1, 0), (0, 1), (1, 1))):
            outs[0][:, lanes(me ^ step, width)] = ins[source][:, at * width : (at + 1) * width]

    return local(kernel, [((rows, 4 * width), pair.dtype)], (pair, near), (), 1, resident=resident, cost=cost)[0]


def over_blocks(width, step, body):
    for base in range(0, width, step):
        body(base, min(step, width - base))


def forward(sources, weights, span, rows, after=(), cost=0.3):
    lower, upper = span
    width, features, tokens = upper - lower, sources[0][0].shape[1], 2 * rows
    arrays = [array for own, theirs, _, _ in sources for array in (own, theirs)]

    def kernel(ins, refs):
        out, held = refs
        loaded = None
        for k, (_, _, first, down) in enumerate(sources):
            if loaded is None or arrays[2 * k] is not arrays[2 * loaded] or first != sources[loaded][2]:
                held[:rows] = ins[2 * k][first : first + rows]
                held[rows:] = ins[2 * k + 1][first : first + rows]
                loaded = k
            weight = ins[len(arrays) + k]
            top = k * tokens

            def product(base, size, weight=weight, top=top, down=down):
                at = slice(lower + base, lower + base + size)
                if down:
                    value = over_cols(held[...], weight[at, :])
                else:
                    value = rows_by_cols(held[...], weight[:, at])
                out[top : top + tokens, base : base + size] = value.astype(out.dtype)

            over_blocks(width, 1024, product)

    return local(
        kernel,
        [((len(sources) * tokens, width), jnp.bfloat16)],
        (*arrays, *weights),
        after,
        scratch=[pltpu.VMEM((tokens, features), jnp.bfloat16)],
        cost=cost,
    )[0]


def backward(own, other, where, weights, span, rows, before, final, after=(), cost=1.0):
    lower, upper = span
    width, features, tokens = upper - lower, weights[0].shape[0], 2 * rows
    count = len(own)
    ins_all = (*own, *other, *weights, *(() if before is None else (before,)))
    outs_all = [((width, tokens), jnp.bfloat16)] + [((tokens, width), jnp.bfloat16)] * 2
    outs_all += [((rows, features), jnp.float32), ((rows, features), jnp.bfloat16)] if final else [((tokens, features), jnp.float32)]

    def kernel(ins, outs):
        @pl.loop(0, width // 256)
        def _(j):
            at = lanes(j, 256)

            def total(k):
                array, top = where[k]
                mine = ins[array][top : top + tokens, at].astype(jnp.float32)
                return mine + ins[count + array][top : top + tokens, at].astype(jnp.float32)

            hidden, outs[1][:, at], outs[2][:, at] = swiglu_grads(total(0), total(1), total(2))
            outs[0][at, :] = hidden.T

        def product(base, size):
            at = slice(base, base + size)
            value = over_cols(outs[1][...], ins[2 * count][at, lower:upper])
            value = value + over_cols(outs[2][...], ins[2 * count + 1][at, lower:upper])
            if before is not None:
                value = value + ins[2 * count + 2][:, at]
            if final:
                outs[3][:, at] = value[:rows]
                outs[4][:, at] = value[rows:].astype(jnp.bfloat16)
            else:
                outs[3][:, at] = value

        over_blocks(features, 1024, product)

    return local(kernel, outs_all, ins_all, after, cost=cost)


def fold_near(value, theirs):
    rows, width = value.shape[0], value.shape[1] // 4

    def kernel(ins, outs):
        odd = lax.rem(lax.axis_index("hid"), 2)
        for i in range(2):
            at = slice(i * width, (i + 1) * width)
            for block, out in ((2 * i + odd, outs[0]), (2 * i + 1 - odd, outs[1])):
                source = lanes(block, width)
                out[:, at] = (ins[0][:, source] + ins[1][:, source].astype(jnp.float32)).astype(out.dtype)

    outs = [((rows, 2 * width), jnp.float32), ((rows, 2 * width), jnp.bfloat16)]
    return local(kernel, outs, (value, theirs), limit=4)


def fold_far(value, theirs):
    rows, width = value.shape[0], value.shape[1] // 2

    def kernel(ins, outs):
        upper = lax.div(lax.axis_index("hid"), 2)
        for block, out in ((upper, outs[0]), (1 - upper, outs[1])):
            source = lanes(block, width)
            out[...] = (ins[0][:, source] + ins[1][:, source].astype(jnp.float32)).astype(out.dtype)

    outs = [((rows, width), jnp.float32), ((rows, width), jnp.bfloat16)]
    return local(kernel, outs, (value, theirs), limit=4)


def fold_last(mine, theirs, earlier=()):
    heights = [piece.shape[0] for piece in earlier]
    rows, width = mine.shape
    shape = (sum(heights) + rows, width)

    def kernel(ins, outs):
        top = 0
        for c, height in enumerate(heights):
            outs[0][top : top + height] = ins[2 + c][...]
            top += height
        outs[0][top:] = (ins[0][...] + ins[1][...].astype(jnp.float32)).astype(jnp.bfloat16)

    specs = [pl.BlockSpec(shape, lambda: (0, 0))] if earlier else None
    return local(kernel, [(shape, jnp.bfloat16)], (mine, theirs, *earlier), limit=4, out_specs=specs)[0]


def turned(own, theirs, first, rows, after=()):
    features = own.shape[1]

    def kernel(ins, outs):
        @pl.loop(0, features // 512)
        def _(j):
            at = lanes(j, 512)
            both = jnp.concatenate([ref[first : first + rows, at] for ref in ins], axis=0)
            outs[0][at, :] = both.T

    return local(kernel, [((features, 2 * rows), own.dtype)], (own, theirs), after, limit=4)[0]


def gradients(kernel, outs, arrays, old, grid, specs, scratch, after, cost):
    def body(*refs):
        kernel(refs[: len(arrays)], refs[len(arrays) + len(old) + len(after) :])

    outs, specs = [*outs, (16, 128)], [*specs, VMEM]
    return pl.pallas_call(
        body,
        grid=grid,
        out_shape=[jax.ShapeDtypeStruct(shape, jnp.bfloat16) for shape in outs],
        in_specs=[VMEM] * len(arrays) + [ANYWHERE] * (len(old) + len(after)),
        out_specs=specs,
        scratch_shapes=scratch,
        input_output_aliases={len(arrays) + i: i for i in range(len(old))},
        compiler_params=pltpu.CompilerParams(vmem_limit_bytes=14 * MIB),
        cost_estimate=declared(cost),
    )(*arrays, *old, *after)


def placed(rows, columns, where):
    return pl.BlockSpec((pl.Element(rows), pl.Element(columns)), where)


def column_grads(xs, gs, us, span, total, old, after=()):
    arrays = [*xs, *(p[0] for p in (*gs, *us))]
    count, lower, width = len(xs), span[0], span[1] - span[0]
    tokens, features = sum(x.shape[1] for x in xs), xs[0].shape[0]
    block = 512

    def kernel(ins, refs):
        gate_out, up_out, token, g_all, u_all = refs
        step = pl.program_id(0)

        @pl.when(step == 0)
        def _():
            token[...] = jnp.zeros_like(token)
            for first, pieces, target in ((count, gs, g_all), (2 * count, us, u_all)):
                top = 0
                for i, (piece, column) in enumerate(pieces):
                    rows = piece.shape[0]
                    target[top : top + rows] = ins[first + i][:, column : column + width]
                    top += rows

        at = lanes(step, block)
        x = jnp.concatenate([ins[i][at, :] for i in range(count)], axis=1)
        gate_out[...] = rows_by_cols(x, g_all[...]).astype(gate_out.dtype)
        up_out[...] = rows_by_cols(x, u_all[...]).astype(up_out.dtype)

    spec = placed(block, width, lambda i: (i * block, lower))
    scratch = [pltpu.VMEM((tokens, width), jnp.bfloat16)] * 2
    return gradients(kernel, [(features, total)] * 2, arrays, old, (features // block,), [spec, spec], scratch, after, 5.0)


def row_grads(hs, ys, span, total, old, after=()):
    arrays = [p[0] for p in (*hs, *ys)]
    count, lower, width = len(hs), span[0], span[1] - span[0]
    tokens, features = sum(p[0].shape[1] for p in hs), ys[0][0].shape[1]
    block = 512

    def kernel(ins, refs):
        out, token, h_all = refs
        step = pl.program_id(0)

        @pl.when(step == 0)
        def _():
            token[...] = jnp.zeros_like(token)
            left = 0
            for i, (piece, row) in enumerate(hs):
                h_all[:, left : left + piece.shape[1]] = ins[i][row : row + width]
                left += piece.shape[1]

        at = lanes(step, block)
        y = jnp.concatenate([ins[count + i][top : top + rows, at] for i, (_, top, rows) in enumerate(ys)], axis=0)
        out[...] = rows_by_cols(h_all[...], y).astype(out.dtype)

    spec = placed(width, block, lambda i: (lower, i * block))
    scratch = [pltpu.VMEM((width, tokens), jnp.bfloat16)]
    return gradients(kernel, [(total, features)], arrays, old, (features // block,), [spec], scratch, after, 3.0)


def piped(acts, grad_out, w_gate, w_up, w_down):
    unit = acts.shape[0] // sum(PIECES)
    bounds = [0]
    for size in PIECES:
        bounds.append(bounds[-1] + size * unit)
    spans = list(zip(bounds[:-1], bounds[1:]))
    heights = [upper - lower for lower, upper in spans]
    last = len(spans) - 1
    total = w_gate.shape[1]
    cut = total // 7 * 4
    whole, halves = (0, total), ((0, cut), (cut, total))
    back_weights = (w_gate, w_up)

    lower, upper = spans[0]
    rows = heights[0]
    mixed, theirs = [], []
    for value in (acts, grad_out):
        value = value[lower:upper]
        pair = pack(value, swapped(value, "hid", 2), cost=3.0)
        mixed.append(arrange(pair, swapped(pair, "hid", 1), cost=3.0))
        theirs.append(shifted(mixed[-1], "tok", 1))
    x, dy = [(mixed[i], theirs[i], 0) for i in range(2)]
    gate_up = forward([(*x, False), (*x, False)], (w_gate, w_up), whole, rows)
    dhid = forward([(*dy, True)], (w_down,), whole, rows, (gate_up,))
    inputs = [(x, dy)]
    sums = [[((gate_up, dhid), ((0, 0), (0, 2 * rows), (1, 0)))]]

    def gather_piece(index, cut_after, pack_after):
        rows = heights[index]
        both = cut_piece(acts, grad_out, *spans[index], cut_after)
        pair = pack(both, swapped(both, "hid", 2), pack_after)
        own = arrange(pair, swapped(pair, "hid", 1))
        other = shifted(own, "tok", 1)
        inputs.append(((own, other, 0), (own, other, rows)))
        return pair

    def forward_piece(index, after):
        x, dy = inputs[index]
        rows = heights[index]
        where = ((0, 0), (0, 2 * rows), (0, 4 * rows))
        done = []
        for span in halves if index == last else (whole,):
            part = forward([(*x, False), (*x, False), (*dy, True)], (w_gate, w_up, w_down), span, rows, after)
            done.append(((part,), where))
            after = (part,)
        sums.append(done)
        return after

    def backward_piece(index, part, before, final, after):
        own, where = sums[index][part]
        span = halves[part] if index == last else whole
        other = [shifted(value, "wid", 1) for value in own]
        cost = 1.0 if index == last else 60.0
        return backward(own, other, where, back_weights, span, heights[index], before, final, after, cost)

    def near_step(results):
        return fold_near(results[3], shifted(results[4], "tok", 1))

    def far_step(near):
        return fold_far(near[0], swapped(near[1], "hid", 1))

    def end_step(far, earlier=()):
        return fold_last(far[0], swapped(far[1], "hid", 2), earlier)

    pair = gather_piece(1, (dhid,), ())
    done = forward_piece(1, ())
    xs = [turned(*x, rows, done) for (x, _), rows in zip(inputs, heights)]
    grads = [backward_piece(0, 0, None, True, (*done, *xs))]
    gather_piece(2, (pair,), (grads[0][1],))
    near = near_step(grads[0])
    done = forward_piece(2, (near[0],))
    xs.append(turned(*inputs[last][0], heights[last], done))
    far = far_step(near)
    grads.append(backward_piece(1, 0, None, True, (*done, xs[last], far[0])))
    finished = [end_step(far)]

    ys = [(array, y[2], rows) for (_, y), rows in zip(inputs, heights) for array in y[:2]]

    def with_last(results, k, part):
        return [(grads[c][k], halves[part][0]) for c in range(last)] + [(results[k], 0)]

    first = backward_piece(last, 0, None, False, (grads[1][1], finished[0]))
    near = near_step(grads[1])
    down, down_token = row_grads(with_last(first, 0, 0), ys, halves[0], total, (), (near[0],))
    far = far_step(near)
    gate, up, token = column_grads(
        xs, with_last(first, 1, 0), with_last(first, 2, 0), halves[0], total, (), (far[0], down_token)
    )
    finished.append(end_step(far))
    second = backward_piece(last, 1, first[3], True, (token, finished[1]))
    near = near_step(second)
    down, down_token = row_grads(with_last(second, 0, 1), ys, halves[1], total, (down,), ())
    far = far_step(near)
    gate, up, _ = column_grads(
        xs, with_last(second, 1, 1), with_last(second, 2, 1), halves[1], total, (gate, up), (near[0], down_token)
    )
    return end_step(far, finished), gate, up, down


def shards(acts, grad_out, w_gate, w_up, w_down):
    sizes = tuple(lax.axis_size(axis) for axis in ("hid", "wid", "tok"))
    aligned = acts.shape[0] % (64 * sum(PIECES)) == 0 and acts.shape[1] % 128 == 0 and w_gate.shape[0] % 512 == 0 and w_gate.shape[1] % 1792 == 0
    if sizes == (4, 2, 2) and aligned:
        return piped(acts, grad_out, w_gate, w_up, w_down)
    return plain(acts, grad_out, w_gate, w_up, w_down)


def solution(mesh):
    placed = (
        P(("groups", "tok"), ("wid", "hid")),
        P(("groups", "tok"), ("wid", "hid")),
        P("wid", ("hid", "tok")),
        P("wid", ("hid", "tok")),
        P(("hid", "tok"), "wid"),
    )
    return jax.shard_map(
        shards,
        mesh=mesh,
        in_specs=placed,
        out_specs=(
            P(("groups", "tok"), ("wid", "hid")),
            P(("groups", "wid"), ("hid", "tok")),
            P(("groups", "wid"), ("hid", "tok")),
            P(("groups", "hid", "tok"), "wid"),
        ),
        check_vma=False,
    )
```

```python
import functools

import jax
import jax.numpy as jnp
from jax import lax
from jax.experimental import pallas as pl
from jax.experimental.pallas import tpu as pltpu
from jax.sharding import PartitionSpec as P

PIECES = (1, 1, 1)
MIB = 1 << 20


def dot(left, right, dims):
    return lax.dot_general(left, right, (dims, ((), ())), preferred_element_type=jnp.float32)


def rows_by_cols(left, right):
    return dot(left, right, ((1,), (0,)))


def over_cols(left, right):
    return dot(left, right, ((1,), (1,)))


def over_rows(left, right):
    return dot(left, right, ((0,), (0,)))


def swiglu_grads(gate, up, dhid):
    sig = jax.nn.sigmoid(gate)
    hidden = (gate * sig * up).astype(jnp.bfloat16)
    d_gate = (dhid * up * sig * (1.0 + gate * (1.0 - sig))).astype(jnp.bfloat16)
    d_up = (dhid * gate * sig).astype(jnp.bfloat16)
    return hidden, d_gate, d_up


def shifted(value, axis, step):
    n = lax.axis_size(axis)
    return lax.ppermute(value, axis, [(i, (i + step) % n) for i in range(n)])


def swapped(value, axis, bit):
    n = lax.axis_size(axis)
    return lax.ppermute(value, axis, [(i, i ^ bit) for i in range(n)])


def summed(value, axis):
    total = value.astype(jnp.float32)
    for step in range(1, lax.axis_size(axis)):
        total = total + shifted(value, axis, step).astype(jnp.float32)
    return total


def own_first(value, axis):
    return jnp.concatenate([value] + [shifted(value, axis, step) for step in range(1, lax.axis_size(axis))], axis=0)


def home_rows(back, axis):
    n = lax.axis_size(axis)
    rows = back.shape[0] // n
    sent = back.astype(jnp.bfloat16)
    total = back[:rows]
    for step in range(1, n):
        block = sent[step * rows : (step + 1) * rows]
        total = total + shifted(block, axis, n - step).astype(jnp.float32)
    return total


def plain(acts, grad_out, w_gate, w_up, w_down):
    x = own_first(lax.all_gather(acts, "hid", axis=1, tiled=True), "tok")
    dy = own_first(lax.all_gather(grad_out, "hid", axis=1, tiled=True), "tok")
    gate = summed(rows_by_cols(x, w_gate).astype(jnp.bfloat16), "wid")
    up = summed(rows_by_cols(x, w_up).astype(jnp.bfloat16), "wid")
    dhid = summed(over_cols(dy, w_down).astype(jnp.bfloat16), "wid")
    hidden, d_gate, d_up = swiglu_grads(gate, up, dhid)
    back = home_rows(over_cols(d_gate, w_gate) + over_cols(d_up, w_up), "tok").astype(jnp.bfloat16)
    back = lax.psum_scatter(back, "hid", scatter_dimension=1, tiled=True)
    return (
        back,
        over_rows(x, d_gate).astype(jnp.bfloat16),
        over_rows(x, d_up).astype(jnp.bfloat16),
        over_rows(hidden, dy).astype(jnp.bfloat16),
    )


VMEM = pl.BlockSpec(memory_space=pltpu.VMEM)
ANYWHERE = pl.BlockSpec(memory_space=pl.ANY)


def declared(cost):
    return pl.CostEstimate(flops=int(cost * 1.15e9), bytes_accessed=0, transcendentals=0)


def local(kernel, outs, args, after=(), limit=12, scratch=(), out_specs=None, cost=0.1):
    def body(*refs):
        kernel(refs[: len(args)], refs[len(args) + len(after) :])

    shapes = [jax.ShapeDtypeStruct(shape, dtype) for shape, dtype in outs]
    return pl.pallas_call(
        body,
        out_shape=shapes,
        in_specs=[VMEM] * len(args) + [ANYWHERE] * len(after),
        out_specs=out_specs if out_specs else [VMEM] * len(outs),
        scratch_shapes=list(scratch),
        compiler_params=pltpu.CompilerParams(vmem_limit_bytes=limit * MIB),
        cost_estimate=declared(cost),
    )(*args, *after)


def lanes(index, width):
    return pl.ds(pl.multiple_of(index * width, width), width)


def cut_rows(acts, grad_out, wanted, after=(), cost=0.1):
    width = acts.shape[1]
    height = sum(rows for _, _, rows in wanted)

    def kernel(ins, outs):
        top = 0
        for array, first, rows in wanted:
            outs[0][top : top + rows] = ins[array][first : first + rows]
            top += rows

    return local(kernel, [((height, width), acts.dtype)], (acts, grad_out), after, 1, cost=cost)[0]


def first_rows(value, rows):
    shape = (rows, value.shape[1])

    def kernel(source, out):
        out[...] = source[...]

    return pl.pallas_call(
        kernel,
        grid=(1,),
        out_shape=jax.ShapeDtypeStruct(shape, value.dtype),
        in_specs=[pl.BlockSpec(shape, lambda i: (0, 0))],
        out_specs=VMEM,
        compiler_params=pltpu.CompilerParams(vmem_limit_bytes=MIB),
        cost_estimate=declared(20.0),
    )(value)


def pack(value, far, after=()):
    rows, width = value.shape

    def kernel(ins, outs):
        outs[0][:, :width] = ins[0][...]
        outs[0][:, width:] = ins[1][...]

    return local(kernel, [((rows, 2 * width), value.dtype)], (value, far), after, 1)[0]


def arrange(pair, near, heights):
    width = pair.shape[1] // 2

    def kernel(ins, outs):
        me = lax.axis_index("hid")
        top = 0
        for out, height in zip(outs, heights):
            for step, (source, at) in enumerate(((0, 0), (1, 0), (0, 1), (1, 1))):
                block = ins[source][top : top + height, at * width : (at + 1) * width]
                out[:, lanes(me ^ step, width)] = block
            top += height

    return local(kernel, [((height, 4 * width), pair.dtype) for height in heights], (pair, near), (), 1)


def over_blocks(width, step, body):
    for base in range(0, width, step):
        body(base, min(step, width - base))


def forward(sources, weights, span, rows, after=(), cost=0.3):
    lower, upper = span
    width, features, tokens = upper - lower, sources[0][0].shape[1], 2 * rows
    arrays = [array for own, theirs, _, _ in sources for array in (own, theirs)]

    def kernel(ins, refs):
        out, held = refs
        loaded = None
        for k, (_, _, first, down) in enumerate(sources):
            if loaded is None or arrays[2 * k] is not arrays[2 * loaded] or first != sources[loaded][2]:
                held[:rows] = ins[2 * k][first : first + rows]
                held[rows:] = ins[2 * k + 1][first : first + rows]
                loaded = k
            weight = ins[len(arrays) + k]
            top = k * tokens

            def product(base, size, weight=weight, top=top, down=down):
                at = slice(lower + base, lower + base + size)
                if down:
                    value = over_cols(held[...], weight[at, :])
                else:
                    value = rows_by_cols(held[...], weight[:, at])
                out[top : top + tokens, base : base + size] = value.astype(out.dtype)

            over_blocks(width, 1024, product)

    return local(
        kernel,
        [((len(sources) * tokens, width), jnp.bfloat16)],
        (*arrays, *weights),
        after,
        scratch=[pltpu.VMEM((tokens, features), jnp.bfloat16)],
        cost=cost,
    )[0]


def backward(own, other, where, weights, span, rows, before, final, after=(), cost=1.0):
    lower, upper = span
    width, features, tokens = upper - lower, weights[0].shape[0], 2 * rows
    count = len(own)
    ins_all = (*own, *other, *weights, *(() if before is None else (before,)))
    outs_all = [((width, tokens), jnp.bfloat16)] + [((tokens, width), jnp.bfloat16)] * 2
    outs_all += [((rows, features), jnp.float32), ((rows, features), jnp.bfloat16)] if final else [((tokens, features), jnp.float32)]

    def kernel(ins, outs):
        @pl.loop(0, width // 256)
        def _(j):
            at = lanes(j, 256)

            def total(k):
                array, top = where[k]
                mine = ins[array][top : top + tokens, at].astype(jnp.float32)
                return mine + ins[count + array][top : top + tokens, at].astype(jnp.float32)

            hidden, outs[1][:, at], outs[2][:, at] = swiglu_grads(total(0), total(1), total(2))
            outs[0][at, :] = hidden.T

        def product(base, size):
            at = slice(base, base + size)
            value = over_cols(outs[1][...], ins[2 * count][at, lower:upper])
            value = value + over_cols(outs[2][...], ins[2 * count + 1][at, lower:upper])
            if before is not None:
                value = value + ins[2 * count + 2][:, at]
            if final:
                outs[3][:, at] = value[:rows]
                outs[4][:, at] = value[rows:].astype(jnp.bfloat16)
            else:
                outs[3][:, at] = value

        over_blocks(features, 1024, product)

    return local(kernel, outs_all, ins_all, after, cost=cost)


def fold_near(value, theirs):
    rows, width = value.shape[0], value.shape[1] // 4

    def kernel(ins, outs):
        odd = lax.rem(lax.axis_index("hid"), 2)
        for i in range(2):
            at = slice(i * width, (i + 1) * width)
            for block, out in ((2 * i + odd, outs[0]), (2 * i + 1 - odd, outs[1])):
                source = lanes(block, width)
                out[:, at] = (ins[0][:, source] + ins[1][:, source].astype(jnp.float32)).astype(out.dtype)

    outs = [((rows, 2 * width), jnp.float32), ((rows, 2 * width), jnp.bfloat16)]
    return local(kernel, outs, (value, theirs), limit=4)


def fold_far(value, theirs):
    rows, width = value.shape[0], value.shape[1] // 2

    def kernel(ins, outs):
        upper = lax.div(lax.axis_index("hid"), 2)
        for block, out in ((upper, outs[0]), (1 - upper, outs[1])):
            source = lanes(block, width)
            out[...] = (ins[0][:, source] + ins[1][:, source].astype(jnp.float32)).astype(out.dtype)

    outs = [((rows, width), jnp.float32), ((rows, width), jnp.bfloat16)]
    return local(kernel, outs, (value, theirs), limit=4)


def fold_last(mine, theirs, earlier=()):
    heights = [piece.shape[0] for piece in earlier]
    rows, width = mine.shape
    shape = (sum(heights) + rows, width)

    def kernel(ins, outs):
        top = 0
        for c, height in enumerate(heights):
            outs[0][top : top + height] = ins[2 + c][...]
            top += height
        outs[0][top:] = (ins[0][...] + ins[1][...].astype(jnp.float32)).astype(jnp.bfloat16)

    specs = [pl.BlockSpec(shape, lambda: (0, 0))] if earlier else None
    return local(kernel, [(shape, jnp.bfloat16)], (mine, theirs, *earlier), limit=4, out_specs=specs)[0]


def joined(pieces, turn, after=()):
    tokens, features = sum(p[2] for p in pieces), pieces[0][0].shape[1]

    def kernel(ins, outs):
        @pl.loop(0, features // 512)
        def _(j):
            at = lanes(j, 512)
            rows = jnp.concatenate([ins[i][p[1] : p[1] + p[2], at] for i, p in enumerate(pieces)], axis=0)
            if turn:
                outs[0][at, :] = rows.T
            else:
                outs[0][:, at] = rows

    shape = (features, tokens) if turn else (tokens, features)
    return local(kernel, [(shape, jnp.bfloat16)], [p[0] for p in pieces], after, limit=4)[0]


def gradients(kernel, outs, arrays, old, grid, specs, scratch, after, cost):
    def body(*refs):
        kernel(refs[: len(arrays)], refs[len(arrays) + len(old) + len(after) :])

    outs, specs = [*outs, (16, 128)], [*specs, VMEM]
    return pl.pallas_call(
        body,
        grid=grid,
        out_shape=[jax.ShapeDtypeStruct(shape, jnp.bfloat16) for shape in outs],
        in_specs=[VMEM] * len(arrays) + [ANYWHERE] * (len(old) + len(after)),
        out_specs=specs,
        scratch_shapes=scratch,
        input_output_aliases={len(arrays) + i: i for i in range(len(old))},
        compiler_params=pltpu.CompilerParams(vmem_limit_bytes=14 * MIB),
        cost_estimate=declared(cost),
    )(*arrays, *old, *after)


def placed(rows, columns, where):
    return pl.BlockSpec((pl.Element(rows), pl.Element(columns)), where)


def column_grads(x, gs, us, span, total, old, after=()):
    arrays = [x, *(p[0] for p in (*gs, *us))]
    count, lower, width = len(gs), span[0], span[1] - span[0]
    features, tokens = x.shape
    block = 256

    def kernel(ins, refs):
        gate_out, up_out, token, g_all, u_all = refs
        step = pl.program_id(0)

        @pl.when(step == 0)
        def _():
            token[...] = jnp.zeros_like(token)
            for first, pieces, target in ((1, gs, g_all), (1 + count, us, u_all)):
                top = 0
                for i, (piece, column) in enumerate(pieces):
                    rows = piece.shape[0]
                    target[top : top + rows] = ins[first + i][:, column : column + width]
                    top += rows

        rows = ins[0][lanes(step, block), :]
        gate_out[...] = rows_by_cols(rows, g_all[...]).astype(gate_out.dtype)
        up_out[...] = rows_by_cols(rows, u_all[...]).astype(up_out.dtype)

    spec = placed(block, width, lambda i: (pl.multiple_of(i * block, block), lower))
    scratch = [pltpu.VMEM((tokens, width), jnp.bfloat16)] * 2
    return gradients(kernel, [(features, total)] * 2, arrays, old, (features // block,), [spec, spec], scratch, after, 5.0)


def row_grads(hs, y, span, total, old, after=()):
    arrays = [*(p[0] for p in hs), y]
    count, lower, width = len(hs), span[0], span[1] - span[0]
    features = y.shape[1]
    block = 256

    def kernel(ins, refs):
        out, token = refs
        step = pl.program_id(0)

        @pl.when(step == 0)
        def _():
            token[...] = jnp.zeros_like(token)

        rows = []
        for i, (_, row) in enumerate(hs):
            rows.append(ins[i][pl.ds(pl.multiple_of(row + step * block, block), block), :])
        out[...] = rows_by_cols(jnp.concatenate(rows, axis=1), ins[count][...]).astype(out.dtype)

    spec = placed(block, features, lambda i: (pl.multiple_of(lower + i * block, block), 0))
    return gradients(kernel, [(total, features)], arrays, old, (width // block,), [spec], [], after, 3.0)


def piped(acts, grad_out, w_gate, w_up, w_down):
    unit = acts.shape[0] // sum(PIECES)
    bounds = [0]
    for size in PIECES:
        bounds.append(bounds[-1] + size * unit)
    spans = list(zip(bounds[:-1], bounds[1:]))
    heights = [upper - lower for lower, upper in spans]
    last = len(spans) - 1
    total = w_gate.shape[1]
    cut = total // 7 * 4
    whole, halves = (0, total), ((0, cut), (cut, total))
    back_weights = (w_gate, w_up)

    def gather(value, parts, early=()):
        pair = pack(value, swapped(value, "hid", 2), early)
        own = arrange(pair, swapped(pair, "hid", 1), [value.shape[0] // parts] * parts)
        return [(array, shifted(array, "tok", 1), 0) for array in own]

    def gather_both(index, after, early=()):
        lower, upper = spans[index]
        mixed = cut_rows(acts, grad_out, [(0, lower, upper - lower), (1, lower, upper - lower)], after)
        return gather(mixed, 2, early)

    rows = heights[0]
    x, = gather(first_rows(acts, rows), 1)
    dy, = gather(cut_rows(acts, grad_out, [(1, 0, rows)]), 1)
    inputs = [(x, dy), gather_both(1, (dy[0],))]
    gate_up = forward([(*x, False), (*x, False)], (w_gate, w_up), whole, rows)
    dhid = forward([(*dy, True)], (w_down,), whole, rows, (gate_up,))
    sums = [[((gate_up, dhid), ((0, 0), (0, 2 * rows), (1, 0)))]]

    def forward_piece(index, after):
        x, dy = inputs[index]
        rows = heights[index]
        where = ((0, 0), (0, 2 * rows), (0, 4 * rows))
        done = []
        for span in halves if index == last else (whole,):
            part = forward([(*x, False), (*x, False), (*dy, True)], (w_gate, w_up, w_down), span, rows, after)
            done.append(((part,), where))
            after = (part,)
        sums.append(done)
        return after

    def backward_piece(index, part, before, final, after):
        own, where = sums[index][part]
        span = halves[part] if index == last else whole
        other = [shifted(value, "wid", 1) for value in own]
        cost = 1.0 if index == last else 60.0
        return backward(own, other, where, back_weights, span, heights[index], before, final, after, cost)

    def near_step(results):
        return fold_near(results[3], shifted(results[4], "tok", 1))

    def far_step(near):
        return fold_far(near[0], swapped(near[1], "hid", 1))

    def end_step(far, earlier=()):
        return fold_last(far[0], swapped(far[1], "hid", 2), earlier)

    done = forward_piece(1, (dhid,))
    grads = [backward_piece(0, 0, None, True, done)]
    inputs.append(gather_both(last, (inputs[1][0][0],), (grads[0][1],)))
    near = near_step(grads[0])
    done = forward_piece(last, (near[0],))
    all_x, all_y = [
        joined([(array, p[k][2], rows) for p, rows in zip(inputs, heights) for array in p[k][:2]], k == 0, done)
        for k in range(2)
    ]
    far = far_step(near)
    grads.append(backward_piece(1, 0, None, True, (all_x, all_y, far[0])))
    finished = [end_step(far)]

    def with_last(results, k, part):
        return [(grads[c][k], halves[part][0]) for c in range(last)] + [(results[k], 0)]

    first = backward_piece(last, 0, None, False, (grads[1][1], finished[0]))
    near = near_step(grads[1])
    down, down_token = row_grads(with_last(first, 0, 0), all_y, halves[0], total, (), (near[0],))
    far = far_step(near)
    gate, up, token = column_grads(
        all_x, with_last(first, 1, 0), with_last(first, 2, 0), halves[0], total, (), (far[0], down_token)
    )
    finished.append(end_step(far))
    second = backward_piece(last, 1, first[3], True, (token, finished[1]))
    near = near_step(second)
    down, down_token = row_grads(with_last(second, 0, 1), all_y, halves[1], total, (down,), ())
    far = far_step(near)
    gate, up, _ = column_grads(
        all_x, with_last(second, 1, 1), with_last(second, 2, 1), halves[1], total, (gate, up), (near[0], down_token)
    )
    return end_step(far, finished), gate, up, down


def shards(acts, grad_out, w_gate, w_up, w_down):
    sizes = tuple(lax.axis_size(axis) for axis in ("hid", "wid", "tok"))
    aligned = acts.shape[0] % (64 * sum(PIECES)) == 0 and acts.shape[1] % 128 == 0 and w_gate.shape[0] % 512 == 0 and w_gate.shape[1] % 1792 == 0
    if sizes == (4, 2, 2) and aligned:
        return piped(acts, grad_out, w_gate, w_up, w_down)
    return plain(acts, grad_out, w_gate, w_up, w_down)


def solution(mesh):
    placed = (
        P(("groups", "tok"), ("wid", "hid")),
        P(("groups", "tok"), ("wid", "hid")),
        P("wid", ("hid", "tok")),
        P("wid", ("hid", "tok")),
        P(("hid", "tok"), "wid"),
    )
    return jax.shard_map(
        shards,
        mesh=mesh,
        in_specs=placed,
        out_specs=(
            P(("groups", "tok"), ("wid", "hid")),
            P(("groups", "wid"), ("hid", "tok")),
            P(("groups", "wid"), ("hid", "tok")),
            P(("groups", "hid", "tok"), "wid"),
        ),
        check_vma=False,
    )
```

```python
import functools

import jax
import jax.numpy as jnp
from jax import lax
from jax.experimental import pallas as pl
from jax.experimental.pallas import tpu as pltpu
from jax.sharding import PartitionSpec as P

PIECES = (1, 1, 1)
MIB = 1 << 20


def dot(left, right, dims):
    return lax.dot_general(left, right, (dims, ((), ())), preferred_element_type=jnp.float32)


def rows_by_cols(left, right):
    return dot(left, right, ((1,), (0,)))


def over_cols(left, right):
    return dot(left, right, ((1,), (1,)))


def over_rows(left, right):
    return dot(left, right, ((0,), (0,)))


def swiglu_grads(gate, up, dhid):
    sig = jax.nn.sigmoid(gate)
    hidden = (gate * sig * up).astype(jnp.bfloat16)
    d_gate = (dhid * up * sig * (1.0 + gate * (1.0 - sig))).astype(jnp.bfloat16)
    d_up = (dhid * gate * sig).astype(jnp.bfloat16)
    return hidden, d_gate, d_up


def shifted(value, axis, step):
    n = lax.axis_size(axis)
    return lax.ppermute(value, axis, [(i, (i + step) % n) for i in range(n)])


def swapped(value, axis, bit):
    n = lax.axis_size(axis)
    return lax.ppermute(value, axis, [(i, i ^ bit) for i in range(n)])


def summed(value, axis):
    total = value.astype(jnp.float32)
    for step in range(1, lax.axis_size(axis)):
        total = total + shifted(value, axis, step).astype(jnp.float32)
    return total


def own_first(value, axis):
    return jnp.concatenate([value] + [shifted(value, axis, step) for step in range(1, lax.axis_size(axis))], axis=0)


def home_rows(back, axis):
    n = lax.axis_size(axis)
    rows = back.shape[0] // n
    sent = back.astype(jnp.bfloat16)
    total = back[:rows]
    for step in range(1, n):
        block = sent[step * rows : (step + 1) * rows]
        total = total + shifted(block, axis, n - step).astype(jnp.float32)
    return total


def plain(acts, grad_out, w_gate, w_up, w_down):
    x = own_first(lax.all_gather(acts, "hid", axis=1, tiled=True), "tok")
    dy = own_first(lax.all_gather(grad_out, "hid", axis=1, tiled=True), "tok")
    gate = summed(rows_by_cols(x, w_gate).astype(jnp.bfloat16), "wid")
    up = summed(rows_by_cols(x, w_up).astype(jnp.bfloat16), "wid")
    dhid = summed(over_cols(dy, w_down).astype(jnp.bfloat16), "wid")
    hidden, d_gate, d_up = swiglu_grads(gate, up, dhid)
    back = home_rows(over_cols(d_gate, w_gate) + over_cols(d_up, w_up), "tok").astype(jnp.bfloat16)
    back = lax.psum_scatter(back, "hid", scatter_dimension=1, tiled=True)
    return (
        back,
        over_rows(x, d_gate).astype(jnp.bfloat16),
        over_rows(x, d_up).astype(jnp.bfloat16),
        over_rows(hidden, dy).astype(jnp.bfloat16),
    )


VMEM = pl.BlockSpec(memory_space=pltpu.VMEM)
ANYWHERE = pl.BlockSpec(memory_space=pl.ANY)


def declared(cost):
    return pl.CostEstimate(flops=int(cost * 1.15e9), bytes_accessed=0, transcendentals=0)


def local(kernel, outs, args, after=(), limit=12, scratch=(), out_specs=None, cost=0.1):
    def body(*refs):
        kernel(refs[: len(args)], refs[len(args) + len(after) :])

    shapes = [jax.ShapeDtypeStruct(shape, dtype) for shape, dtype in outs]
    return pl.pallas_call(
        body,
        out_shape=shapes,
        in_specs=[VMEM] * len(args) + [ANYWHERE] * len(after),
        out_specs=out_specs if out_specs else [VMEM] * len(outs),
        scratch_shapes=list(scratch),
        compiler_params=pltpu.CompilerParams(vmem_limit_bytes=limit * MIB),
        cost_estimate=declared(cost),
    )(*args, *after)


def lanes(index, width):
    return pl.ds(pl.multiple_of(index * width, width), width)


def cut_rows(acts, grad_out, wanted, after=(), cost=0.1):
    width = acts.shape[1]
    height = sum(rows for _, _, rows in wanted)

    def kernel(ins, outs):
        top = 0
        for array, first, rows in wanted:
            outs[0][top : top + rows] = ins[array][first : first + rows]
            top += rows

    return local(kernel, [((height, width), acts.dtype)], (acts, grad_out), after, 1, cost=cost)[0]


def first_rows(value, rows):
    shape = (rows, value.shape[1])

    def kernel(source, out):
        out[...] = source[...]

    return pl.pallas_call(
        kernel,
        grid=(1,),
        out_shape=jax.ShapeDtypeStruct(shape, value.dtype),
        in_specs=[pl.BlockSpec(shape, lambda i: (0, 0))],
        out_specs=VMEM,
        compiler_params=pltpu.CompilerParams(vmem_limit_bytes=MIB),
        cost_estimate=declared(20.0),
    )(value)


def pack(value, far, after=(), cost=0.1):
    rows, width = value.shape

    def kernel(ins, outs):
        outs[0][:, :width] = ins[0][...]
        outs[0][:, width:] = ins[1][...]

    return local(kernel, [((rows, 2 * width), value.dtype)], (value, far), after, 1, cost=cost)[0]


def arrange(pair, near, heights, cost=0.1):
    width = pair.shape[1] // 2

    def kernel(ins, outs):
        me = lax.axis_index("hid")
        top = 0
        for out, height in zip(outs, heights):
            for step, (source, at) in enumerate(((0, 0), (1, 0), (0, 1), (1, 1))):
                block = ins[source][top : top + height, at * width : (at + 1) * width]
                out[:, lanes(me ^ step, width)] = block
            top += height

    return local(kernel, [((height, 4 * width), pair.dtype) for height in heights], (pair, near), (), 1, cost=cost)


def over_blocks(width, step, body):
    for base in range(0, width, step):
        body(base, min(step, width - base))


def forward(sources, weights, span, rows, after=(), cost=0.3):
    lower, upper = span
    width, features, tokens = upper - lower, sources[0][0].shape[1], 2 * rows
    arrays = [array for own, theirs, _, _ in sources for array in (own, theirs)]

    def kernel(ins, refs):
        out, held = refs
        loaded = None
        for k, (_, _, first, down) in enumerate(sources):
            if loaded is None or arrays[2 * k] is not arrays[2 * loaded] or first != sources[loaded][2]:
                held[:rows] = ins[2 * k][first : first + rows]
                held[rows:] = ins[2 * k + 1][first : first + rows]
                loaded = k
            weight = ins[len(arrays) + k]
            top = k * tokens

            def product(base, size, weight=weight, top=top, down=down):
                at = slice(lower + base, lower + base + size)
                if down:
                    value = over_cols(held[...], weight[at, :])
                else:
                    value = rows_by_cols(held[...], weight[:, at])
                out[top : top + tokens, base : base + size] = value.astype(out.dtype)

            over_blocks(width, 1024, product)

    return local(
        kernel,
        [((len(sources) * tokens, width), jnp.bfloat16)],
        (*arrays, *weights),
        after,
        scratch=[pltpu.VMEM((tokens, features), jnp.bfloat16)],
        cost=cost,
    )[0]


def backward(own, other, where, weights, span, rows, before, final, after=(), cost=1.0):
    lower, upper = span
    width, features, tokens = upper - lower, weights[0].shape[0], 2 * rows
    count = len(own)
    ins_all = (*own, *other, *weights, *(() if before is None else (before,)))
    outs_all = [((width, tokens), jnp.bfloat16)] + [((tokens, width), jnp.bfloat16)] * 2
    outs_all += [((rows, features), jnp.float32), ((rows, features), jnp.bfloat16)] if final else [((tokens, features), jnp.float32)]

    def kernel(ins, outs):
        @pl.loop(0, width // 256)
        def _(j):
            at = lanes(j, 256)

            def total(k):
                array, top = where[k]
                mine = ins[array][top : top + tokens, at].astype(jnp.float32)
                return mine + ins[count + array][top : top + tokens, at].astype(jnp.float32)

            hidden, outs[1][:, at], outs[2][:, at] = swiglu_grads(total(0), total(1), total(2))
            outs[0][at, :] = hidden.T

        def product(base, size):
            at = slice(base, base + size)
            value = over_cols(outs[1][...], ins[2 * count][at, lower:upper])
            value = value + over_cols(outs[2][...], ins[2 * count + 1][at, lower:upper])
            if before is not None:
                value = value + ins[2 * count + 2][:, at]
            if final:
                outs[3][:, at] = value[:rows]
                outs[4][:, at] = value[rows:].astype(jnp.bfloat16)
            else:
                outs[3][:, at] = value

        over_blocks(features, 1024, product)

    return local(kernel, outs_all, ins_all, after, cost=cost)


def fold_near(value, theirs):
    rows, width = value.shape[0], value.shape[1] // 4

    def kernel(ins, outs):
        odd = lax.rem(lax.axis_index("hid"), 2)
        for i in range(2):
            at = slice(i * width, (i + 1) * width)
            for block, out in ((2 * i + odd, outs[0]), (2 * i + 1 - odd, outs[1])):
                source = lanes(block, width)
                out[:, at] = (ins[0][:, source] + ins[1][:, source].astype(jnp.float32)).astype(out.dtype)

    outs = [((rows, 2 * width), jnp.float32), ((rows, 2 * width), jnp.bfloat16)]
    return local(kernel, outs, (value, theirs), limit=4)


def fold_far(value, theirs):
    rows, width = value.shape[0], value.shape[1] // 2

    def kernel(ins, outs):
        upper = lax.div(lax.axis_index("hid"), 2)
        for block, out in ((upper, outs[0]), (1 - upper, outs[1])):
            source = lanes(block, width)
            out[...] = (ins[0][:, source] + ins[1][:, source].astype(jnp.float32)).astype(out.dtype)

    outs = [((rows, width), jnp.float32), ((rows, width), jnp.bfloat16)]
    return local(kernel, outs, (value, theirs), limit=4)


def fold_last(mine, theirs, earlier=()):
    heights = [piece.shape[0] for piece in earlier]
    rows, width = mine.shape
    shape = (sum(heights) + rows, width)

    def kernel(ins, outs):
        top = 0
        for c, height in enumerate(heights):
            outs[0][top : top + height] = ins[2 + c][...]
            top += height
        outs[0][top:] = (ins[0][...] + ins[1][...].astype(jnp.float32)).astype(jnp.bfloat16)

    specs = [pl.BlockSpec(shape, lambda: (0, 0))] if earlier else None
    return local(kernel, [(shape, jnp.bfloat16)], (mine, theirs, *earlier), limit=4, out_specs=specs)[0]


def joined(pieces, turn, after=()):
    tokens, features = sum(p[2] for p in pieces), pieces[0][0].shape[1]

    def kernel(ins, outs):
        @pl.loop(0, features // 512)
        def _(j):
            at = lanes(j, 512)
            rows = jnp.concatenate([ins[i][p[1] : p[1] + p[2], at] for i, p in enumerate(pieces)], axis=0)
            if turn:
                outs[0][at, :] = rows.T
            else:
                outs[0][:, at] = rows

    shape = (features, tokens) if turn else (tokens, features)
    return local(kernel, [(shape, jnp.bfloat16)], [p[0] for p in pieces], after, limit=4)[0]


def gradients(kernel, outs, arrays, old, grid, specs, scratch, after, cost):
    def body(*refs):
        kernel(refs[: len(arrays)], refs[len(arrays) + len(old) + len(after) :])

    outs, specs = [*outs, (16, 128)], [*specs, VMEM]
    return pl.pallas_call(
        body,
        grid=grid,
        out_shape=[jax.ShapeDtypeStruct(shape, jnp.bfloat16) for shape in outs],
        in_specs=[VMEM] * len(arrays) + [ANYWHERE] * (len(old) + len(after)),
        out_specs=specs,
        scratch_shapes=scratch,
        input_output_aliases={len(arrays) + i: i for i in range(len(old))},
        compiler_params=pltpu.CompilerParams(vmem_limit_bytes=14 * MIB),
        cost_estimate=declared(cost),
    )(*arrays, *old, *after)


def tiled(out, left, right):
    height, width = out.shape
    for top in range(0, height, 512):
        for start in range(0, width, 256):
            rows, columns = pl.ds(top, min(512, height - top)), pl.ds(start, min(256, width - start))
            out[rows, columns] = rows_by_cols(left[rows, :], right[:, columns]).astype(out.dtype)


def placed(rows, columns, where):
    return pl.BlockSpec((pl.Element(rows), pl.Element(columns)), where)


def column_grads(x, gs, us, span, total, old, after=()):
    arrays = [x, *(p[0] for p in (*gs, *us))]
    count, lower, width = len(gs), span[0], span[1] - span[0]
    features, tokens = x.shape
    block = 512

    def kernel(ins, refs):
        gate_out, up_out, token, g_all, u_all = refs
        step = pl.program_id(0)

        @pl.when(step == 0)
        def _():
            token[...] = jnp.zeros_like(token)
            for first, pieces, target in ((1, gs, g_all), (1 + count, us, u_all)):
                top = 0
                for i, (piece, column) in enumerate(pieces):
                    rows = piece.shape[0]
                    target[top : top + rows] = ins[first + i][:, column : column + width]
                    top += rows

        rows = ins[0].at[lanes(step, block), :]
        tiled(gate_out, rows, g_all)
        tiled(up_out, rows, u_all)

    spec = placed(block, width, lambda i: (pl.multiple_of(i * block, block), lower))
    scratch = [pltpu.VMEM((tokens, width), jnp.bfloat16)] * 2
    return gradients(kernel, [(features, total)] * 2, arrays, old, (features // block,), [spec, spec], scratch, after, 0.1)


def row_grads(hs, y, span, total, old, after=()):
    arrays = [*(p[0] for p in hs), y]
    count, lower, width = len(hs), span[0], span[1] - span[0]
    tokens, features = y.shape
    block = 512

    def kernel(ins, refs):
        out, token, h_all = refs
        step = pl.program_id(0)

        @pl.when(step == 0)
        def _():
            token[...] = jnp.zeros_like(token)
            left = 0
            for i, (piece, row) in enumerate(hs):
                h_all[:, left : left + piece.shape[1]] = ins[i][row : row + width]
                left += piece.shape[1]

        tiled(out, h_all, ins[count].at[:, lanes(step, block)])

    spec = placed(width, block, lambda i: (lower, pl.multiple_of(i * block, block)))
    scratch = [pltpu.VMEM((width, tokens), jnp.bfloat16)]
    return gradients(kernel, [(total, features)], arrays, old, (features // block,), [spec], scratch, after, 0.1)


def piped(acts, grad_out, w_gate, w_up, w_down):
    unit = acts.shape[0] // sum(PIECES)
    bounds = [0]
    for size in PIECES:
        bounds.append(bounds[-1] + size * unit)
    spans = list(zip(bounds[:-1], bounds[1:]))
    heights = [upper - lower for lower, upper in spans]
    last = len(spans) - 1
    total = w_gate.shape[1]
    cut = total // 7 * 4
    whole, halves = (0, total), ((0, cut), (cut, total))
    back_weights = (w_gate, w_up)

    def gather(value, parts, early=(), costs=(0.1, 0.1)):
        pair = pack(value, swapped(value, "hid", 2), early, costs[0])
        own = arrange(pair, swapped(pair, "hid", 1), [value.shape[0] // parts] * parts, costs[1])
        return [(array, shifted(array, "tok", 1), 0) for array in own]

    def gather_both(index, after, early=()):
        lower, upper = spans[index]
        mixed = cut_rows(acts, grad_out, [(0, lower, upper - lower), (1, lower, upper - lower)], after)
        return gather(mixed, 2, early)

    rows = heights[0]
    x, = gather(first_rows(acts, rows), 1)
    dy, = gather(cut_rows(acts, grad_out, [(1, 0, rows)]), 1, costs=(1.2, 5.0))
    inputs = [(x, dy), gather_both(1, (dy[0],))]
    gate_up = forward([(*x, False), (*x, False)], (w_gate, w_up), whole, rows)
    dhid = forward([(*dy, True)], (w_down,), whole, rows, (gate_up,))
    sums = [[((gate_up, dhid), ((0, 0), (0, 2 * rows), (1, 0)))]]

    def forward_piece(index, after):
        x, dy = inputs[index]
        rows = heights[index]
        where = ((0, 0), (0, 2 * rows), (0, 4 * rows))
        done = []
        for span in halves if index == last else (whole,):
            part = forward([(*x, False), (*x, False), (*dy, True)], (w_gate, w_up, w_down), span, rows, after)
            done.append(((part,), where))
            after = (part,)
        sums.append(done)
        return after

    def backward_piece(index, part, before, final, after):
        own, where = sums[index][part]
        span = halves[part] if index == last else whole
        other = [shifted(value, "wid", 1) for value in own]
        cost = 1.0 if index == last else 60.0
        return backward(own, other, where, back_weights, span, heights[index], before, final, after, cost)

    def near_step(results):
        return fold_near(results[3], shifted(results[4], "tok", 1))

    def far_step(near):
        return fold_far(near[0], swapped(near[1], "hid", 1))

    def end_step(far, earlier=()):
        return fold_last(far[0], swapped(far[1], "hid", 2), earlier)

    done = forward_piece(1, (dhid,))
    grads = [backward_piece(0, 0, None, True, done)]
    inputs.append(gather_both(last, (inputs[1][0][0],), (grads[0][1],)))
    near = near_step(grads[0])
    done = forward_piece(last, (near[0],))
    all_x, all_y = [
        joined([(array, p[k][2], rows) for p, rows in zip(inputs, heights) for array in p[k][:2]], k == 0, done)
        for k in range(2)
    ]
    far = far_step(near)
    grads.append(backward_piece(1, 0, None, True, (all_x, all_y, far[0])))
    finished = [end_step(far)]

    def with_last(results, k, part):
        return [(grads[c][k], halves[part][0]) for c in range(last)] + [(results[k], 0)]

    first = backward_piece(last, 0, None, False, (grads[1][1], finished[0]))
    near = near_step(grads[1])
    down, down_token = row_grads(with_last(first, 0, 0), all_y, halves[0], total, (), (near[0],))
    far = far_step(near)
    gate, up, token = column_grads(
        all_x, with_last(first, 1, 0), with_last(first, 2, 0), halves[0], total, (), (far[0], down_token)
    )
    finished.append(end_step(far))
    second = backward_piece(last, 1, first[3], True, (token, finished[1]))
    near = near_step(second)
    down, down_token = row_grads(with_last(second, 0, 1), all_y, halves[1], total, (down,), ())
    far = far_step(near)
    gate, up, _ = column_grads(
        all_x, with_last(second, 1, 1), with_last(second, 2, 1), halves[1], total, (gate, up), (near[0], down_token)
    )
    return end_step(far, finished), gate, up, down


def shards(acts, grad_out, w_gate, w_up, w_down):
    sizes = tuple(lax.axis_size(axis) for axis in ("hid", "wid", "tok"))
    aligned = acts.shape[0] % (64 * sum(PIECES)) == 0 and acts.shape[1] % 128 == 0 and w_gate.shape[0] % 512 == 0 and w_gate.shape[1] % 1792 == 0
    if sizes == (4, 2, 2) and aligned:
        return piped(acts, grad_out, w_gate, w_up, w_down)
    return plain(acts, grad_out, w_gate, w_up, w_down)


def solution(mesh):
    placed = (
        P(("groups", "tok"), ("wid", "hid")),
        P(("groups", "tok"), ("wid", "hid")),
        P("wid", ("hid", "tok")),
        P("wid", ("hid", "tok")),
        P(("hid", "tok"), "wid"),
    )
    return jax.shard_map(
        shards,
        mesh=mesh,
        in_specs=placed,
        out_specs=(
            P(("groups", "tok"), ("wid", "hid")),
            P(("groups", "wid"), ("hid", "tok")),
            P(("groups", "wid"), ("hid", "tok")),
            P(("groups", "hid", "tok"), "wid"),
        ),
        check_vma=False,
    )
```

```python
import functools

import jax
import jax.numpy as jnp
from jax import lax
from jax.experimental import pallas as pl
from jax.experimental.pallas import tpu as pltpu
from jax.sharding import PartitionSpec as P

PIECES = (1, 1, 1)
PARTS = (5, 5, 4)
MIB = 1 << 20


def dot(left, right, dims):
    return lax.dot_general(left, right, (dims, ((), ())), preferred_element_type=jnp.float32)


def rows_by_cols(left, right):
    return dot(left, right, ((1,), (0,)))


def over_cols(left, right):
    return dot(left, right, ((1,), (1,)))


def over_rows(left, right):
    return dot(left, right, ((0,), (0,)))


def swiglu_grads(gate, up, dhid):
    sig = jax.nn.sigmoid(gate)
    hidden = (gate * sig * up).astype(jnp.bfloat16)
    d_gate = (dhid * up * sig * (1.0 + gate * (1.0 - sig))).astype(jnp.bfloat16)
    d_up = (dhid * gate * sig).astype(jnp.bfloat16)
    return hidden, d_gate, d_up


def shifted(value, axis, step):
    n = lax.axis_size(axis)
    return lax.ppermute(value, axis, [(i, (i + step) % n) for i in range(n)])


def swapped(value, axis, bit):
    n = lax.axis_size(axis)
    return lax.ppermute(value, axis, [(i, i ^ bit) for i in range(n)])


def summed(value, axis):
    total = value.astype(jnp.float32)
    for step in range(1, lax.axis_size(axis)):
        total = total + shifted(value, axis, step).astype(jnp.float32)
    return total


def own_first(value, axis):
    return jnp.concatenate([value] + [shifted(value, axis, step) for step in range(1, lax.axis_size(axis))], axis=0)


def home_rows(back, axis):
    n = lax.axis_size(axis)
    rows = back.shape[0] // n
    sent = back.astype(jnp.bfloat16)
    total = back[:rows]
    for step in range(1, n):
        block = sent[step * rows : (step + 1) * rows]
        total = total + shifted(block, axis, n - step).astype(jnp.float32)
    return total


def plain(acts, grad_out, w_gate, w_up, w_down):
    x = own_first(lax.all_gather(acts, "hid", axis=1, tiled=True), "tok")
    dy = own_first(lax.all_gather(grad_out, "hid", axis=1, tiled=True), "tok")
    gate = summed(rows_by_cols(x, w_gate).astype(jnp.bfloat16), "wid")
    up = summed(rows_by_cols(x, w_up).astype(jnp.bfloat16), "wid")
    dhid = summed(over_cols(dy, w_down).astype(jnp.bfloat16), "wid")
    hidden, d_gate, d_up = swiglu_grads(gate, up, dhid)
    back = home_rows(over_cols(d_gate, w_gate) + over_cols(d_up, w_up), "tok").astype(jnp.bfloat16)
    back = lax.psum_scatter(back, "hid", scatter_dimension=1, tiled=True)
    return (
        back,
        over_rows(x, d_gate).astype(jnp.bfloat16),
        over_rows(x, d_up).astype(jnp.bfloat16),
        over_rows(hidden, dy).astype(jnp.bfloat16),
    )


VMEM = pl.BlockSpec(memory_space=pltpu.VMEM)
ANYWHERE = pl.BlockSpec(memory_space=pl.ANY)


def declared(cost):
    return pl.CostEstimate(flops=int(cost * 1.15e9), bytes_accessed=0, transcendentals=0)


def local(kernel, outs, args, after=(), limit=12, scratch=(), out_specs=None, cost=0.1):
    def body(*refs):
        kernel(refs[: len(args)], refs[len(args) + len(after) :])

    shapes = [jax.ShapeDtypeStruct(shape, dtype) for shape, dtype in outs]
    return pl.pallas_call(
        body,
        out_shape=shapes,
        in_specs=[VMEM] * len(args) + [ANYWHERE] * len(after),
        out_specs=out_specs if out_specs else [VMEM] * len(outs),
        scratch_shapes=list(scratch),
        compiler_params=pltpu.CompilerParams(vmem_limit_bytes=limit * MIB),
        cost_estimate=declared(cost),
    )(*args, *after)


def lanes(index, width):
    return pl.ds(pl.multiple_of(index * width, width), width)


def cut_rows(acts, grad_out, wanted, after=(), cost=0.1):
    width = acts.shape[1]
    height = sum(rows for _, _, rows in wanted)

    def kernel(ins, outs):
        top = 0
        for array, first, rows in wanted:
            outs[0][top : top + rows] = ins[array][first : first + rows]
            top += rows

    return local(kernel, [((height, width), acts.dtype)], (acts, grad_out), after, 1, cost=cost)[0]


def first_rows(value, rows):
    shape = (rows, value.shape[1])

    def kernel(source, out):
        out[...] = source[...]

    return pl.pallas_call(
        kernel,
        grid=(1,),
        out_shape=jax.ShapeDtypeStruct(shape, value.dtype),
        in_specs=[pl.BlockSpec(shape, lambda i: (0, 0))],
        out_specs=VMEM,
        compiler_params=pltpu.CompilerParams(vmem_limit_bytes=MIB),
        cost_estimate=declared(20.0),
    )(value)


def pack(value, far, after=(), cost=0.1):
    rows, width = value.shape

    def kernel(ins, outs):
        outs[0][:, :width] = ins[0][...]
        outs[0][:, width:] = ins[1][...]

    return local(kernel, [((rows, 2 * width), value.dtype)], (value, far), after, 1, cost=cost)[0]


def arrange(pair, near, heights, cost=0.1):
    width = pair.shape[1] // 2

    def kernel(ins, outs):
        me = lax.axis_index("hid")
        top = 0
        for out, height in zip(outs, heights):
            for step, (source, at) in enumerate(((0, 0), (1, 0), (0, 1), (1, 1))):
                block = ins[source][top : top + height, at * width : (at + 1) * width]
                out[:, lanes(me ^ step, width)] = block
            top += height

    return local(kernel, [((height, 4 * width), pair.dtype) for height in heights], (pair, near), (), 1, cost=cost)


def over_blocks(width, step, body):
    for base in range(0, width, step):
        body(base, min(step, width - base))


def forward(sources, weights, span, rows, after=(), cost=0.3):
    lower, upper = span
    width, features, tokens = upper - lower, sources[0][0].shape[1], 2 * rows
    arrays = [array for own, theirs, _, _ in sources for array in (own, theirs)]

    def kernel(ins, refs):
        out, held = refs
        loaded = None
        for k, (_, _, first, down) in enumerate(sources):
            if loaded is None or arrays[2 * k] is not arrays[2 * loaded] or first != sources[loaded][2]:
                held[:rows] = ins[2 * k][first : first + rows]
                held[rows:] = ins[2 * k + 1][first : first + rows]
                loaded = k
            weight = ins[len(arrays) + k]
            top = k * tokens

            def product(base, size, weight=weight, top=top, down=down):
                at = slice(lower + base, lower + base + size)
                if down:
                    value = over_cols(held[...], weight[at, :])
                else:
                    value = rows_by_cols(held[...], weight[:, at])
                out[top : top + tokens, base : base + size] = value.astype(out.dtype)

            over_blocks(width, 1024, product)

    return local(
        kernel,
        [((len(sources) * tokens, width), jnp.bfloat16)],
        (*arrays, *weights),
        after,
        scratch=[pltpu.VMEM((tokens, features), jnp.bfloat16)],
        cost=cost,
    )[0]


def backward(own, other, where, weights, span, rows, before, final, after=(), cost=1.0):
    lower, upper = span
    width, features, tokens = upper - lower, weights[0].shape[0], 2 * rows
    count = len(own)
    ins_all = (*own, *other, *weights, *(() if before is None else (before,)))
    outs_all = [((width, tokens), jnp.bfloat16)] + [((tokens, width), jnp.bfloat16)] * 2
    outs_all += [((rows, features), jnp.float32), ((rows, features), jnp.bfloat16)] if final else [((tokens, features), jnp.float32)]

    def kernel(ins, outs):
        @pl.loop(0, width // 128)
        def _(j):
            at = lanes(j, 128)

            def total(k):
                array, top = where[k]
                mine = ins[array][top : top + tokens, at].astype(jnp.float32)
                return mine + ins[count + array][top : top + tokens, at].astype(jnp.float32)

            hidden, outs[1][:, at], outs[2][:, at] = swiglu_grads(total(0), total(1), total(2))
            outs[0][at, :] = hidden.T

        def product(base, size):
            at = slice(base, base + size)
            value = over_cols(outs[1][...], ins[2 * count][at, lower:upper])
            value = value + over_cols(outs[2][...], ins[2 * count + 1][at, lower:upper])
            if before is not None:
                value = value + ins[2 * count + 2][:, at]
            if final:
                outs[3][:, at] = value[:rows]
                outs[4][:, at] = value[rows:].astype(jnp.bfloat16)
            else:
                outs[3][:, at] = value

        over_blocks(features, 1024, product)

    return local(kernel, outs_all, ins_all, after, cost=cost)


def fold_near(value, theirs):
    rows, width = value.shape[0], value.shape[1] // 4

    def kernel(ins, outs):
        odd = lax.rem(lax.axis_index("hid"), 2)
        for i in range(2):
            at = slice(i * width, (i + 1) * width)
            for block, out in ((2 * i + odd, outs[0]), (2 * i + 1 - odd, outs[1])):
                source = lanes(block, width)
                out[:, at] = (ins[0][:, source] + ins[1][:, source].astype(jnp.float32)).astype(out.dtype)

    outs = [((rows, 2 * width), jnp.float32), ((rows, 2 * width), jnp.bfloat16)]
    return local(kernel, outs, (value, theirs), limit=4)


def fold_far(value, theirs):
    rows, width = value.shape[0], value.shape[1] // 2

    def kernel(ins, outs):
        upper = lax.div(lax.axis_index("hid"), 2)
        for block, out in ((upper, outs[0]), (1 - upper, outs[1])):
            source = lanes(block, width)
            out[...] = (ins[0][:, source] + ins[1][:, source].astype(jnp.float32)).astype(out.dtype)

    outs = [((rows, width), jnp.float32), ((rows, width), jnp.bfloat16)]
    return local(kernel, outs, (value, theirs), limit=4)


def fold_last(mine, theirs, earlier=()):
    heights = [piece.shape[0] for piece in earlier]
    rows, width = mine.shape
    shape = (sum(heights) + rows, width)

    def kernel(ins, outs):
        top = 0
        for c, height in enumerate(heights):
            outs[0][top : top + height] = ins[2 + c][...]
            top += height
        outs[0][top:] = (ins[0][...] + ins[1][...].astype(jnp.float32)).astype(jnp.bfloat16)

    specs = [pl.BlockSpec(shape, lambda: (0, 0))] if earlier else None
    return local(kernel, [(shape, jnp.bfloat16)], (mine, theirs, *earlier), limit=4, out_specs=specs)[0]


def joined(pieces, turn, after=()):
    tokens, features = sum(p[2] for p in pieces), pieces[0][0].shape[1]

    def kernel(ins, outs):
        @pl.loop(0, features // 512)
        def _(j):
            at = lanes(j, 512)
            rows = jnp.concatenate([ins[i][p[1] : p[1] + p[2], at] for i, p in enumerate(pieces)], axis=0)
            if turn:
                outs[0][at, :] = rows.T
            else:
                outs[0][:, at] = rows

    shape = (features, tokens) if turn else (tokens, features)
    return local(kernel, [(shape, jnp.bfloat16)], [p[0] for p in pieces], after, limit=4)[0]


def gradients(kernel, outs, arrays, old, grid, specs, scratch, after, cost):
    def body(*refs):
        kernel(refs[: len(arrays)], refs[len(arrays) + len(old) + len(after) :])

    outs, specs = [*outs, (16, 128)], [*specs, VMEM]
    return pl.pallas_call(
        body,
        grid=grid,
        out_shape=[jax.ShapeDtypeStruct(shape, jnp.bfloat16) for shape in outs],
        in_specs=[VMEM] * len(arrays) + [ANYWHERE] * (len(old) + len(after)),
        out_specs=specs,
        scratch_shapes=scratch,
        input_output_aliases={len(arrays) + i: i for i in range(len(old))},
        compiler_params=pltpu.CompilerParams(vmem_limit_bytes=14 * MIB),
        cost_estimate=declared(cost),
    )(*arrays, *old, *after)


def tiled(out, left, right):
    height, width = out.shape
    for top in range(0, height, 512):
        for start in range(0, width, 256):
            rows, columns = pl.ds(top, min(512, height - top)), pl.ds(start, min(256, width - start))
            out[rows, columns] = rows_by_cols(left[rows, :], right[:, columns]).astype(out.dtype)


def placed(rows, columns, where):
    return pl.BlockSpec((pl.Element(rows), pl.Element(columns)), where)


def column_grads(x, gs, us, span, total, old, after=(), cost=0.1):
    arrays = [x, *(p[0] for p in (*gs, *us))]
    count, lower, width = len(gs), span[0], span[1] - span[0]
    features, tokens = x.shape
    block = 512

    def kernel(ins, refs):
        gate_out, up_out, token, g_all, u_all = refs
        step = pl.program_id(0)

        @pl.when(step == 0)
        def _():
            token[...] = jnp.zeros_like(token)
            for first, pieces, target in ((1, gs, g_all), (1 + count, us, u_all)):
                top = 0
                for i, (piece, column) in enumerate(pieces):
                    rows = piece.shape[0]
                    target[top : top + rows] = ins[first + i][:, column : column + width]
                    top += rows

        rows = ins[0].at[lanes(step, block), :]
        tiled(gate_out, rows, g_all)
        tiled(up_out, rows, u_all)

    spec = placed(block, width, lambda i: (pl.multiple_of(i * block, block), lower))
    scratch = [pltpu.VMEM((tokens, width), jnp.bfloat16)] * 2
    return gradients(kernel, [(features, total)] * 2, arrays, old, (features // block,), [spec, spec], scratch, after, cost)


def row_grads(hs, y, span, total, old, after=(), cost=0.1):
    arrays = [*(p[0] for p in hs), y]
    count, lower, width = len(hs), span[0], span[1] - span[0]
    tokens, features = y.shape
    block = 512

    def kernel(ins, refs):
        out, token, h_all = refs
        step = pl.program_id(0)

        @pl.when(step == 0)
        def _():
            token[...] = jnp.zeros_like(token)
            left = 0
            for i, (piece, row) in enumerate(hs):
                h_all[:, left : left + piece.shape[1]] = ins[i][row : row + width]
                left += piece.shape[1]

        tiled(out, h_all, ins[count].at[:, lanes(step, block)])

    spec = placed(width, block, lambda i: (lower, pl.multiple_of(i * block, block)))
    scratch = [pltpu.VMEM((width, tokens), jnp.bfloat16)]
    return gradients(kernel, [(total, features)], arrays, old, (features // block,), [spec], scratch, after, cost)


def piped(acts, grad_out, w_gate, w_up, w_down):
    unit = acts.shape[0] // sum(PIECES)
    bounds = [0]
    for size in PIECES:
        bounds.append(bounds[-1] + size * unit)
    spans = list(zip(bounds[:-1], bounds[1:]))
    heights = [upper - lower for lower, upper in spans]
    last = len(spans) - 1
    total = w_gate.shape[1]
    fraction = total // sum(PARTS)
    edges = [sum(PARTS[:i]) * fraction for i in range(len(PARTS) + 1)]
    whole, parts = (0, total), list(zip(edges[:-1], edges[1:]))
    back_weights = (w_gate, w_up)

    def gather(value, parts, early=(), costs=(0.1, 0.1)):
        pair = pack(value, swapped(value, "hid", 2), early, costs[0])
        own = arrange(pair, swapped(pair, "hid", 1), [value.shape[0] // parts] * parts, costs[1])
        return [(array, shifted(array, "tok", 1), 0) for array in own]

    def gather_both(index, after, early=()):
        lower, upper = spans[index]
        mixed = cut_rows(acts, grad_out, [(0, lower, upper - lower), (1, lower, upper - lower)], after)
        return gather(mixed, 2, early)

    rows = heights[0]
    x, = gather(first_rows(acts, rows), 1)
    dy, = gather(cut_rows(acts, grad_out, [(1, 0, rows)]), 1, costs=(1.2, 5.0))
    inputs = [(x, dy), gather_both(1, (dy[0],))]
    gate_up = forward([(*x, False), (*x, False)], (w_gate, w_up), whole, rows)
    dhid = forward([(*dy, True)], (w_down,), whole, rows, (gate_up,))
    sums = [[((gate_up, dhid), ((0, 0), (0, 2 * rows), (1, 0)))]]

    def forward_piece(index, after):
        x, dy = inputs[index]
        rows = heights[index]
        where = ((0, 0), (0, 2 * rows), (0, 4 * rows))
        done = []
        for span in parts if index == last else (whole,):
            part = forward([(*x, False), (*x, False), (*dy, True)], (w_gate, w_up, w_down), span, rows, after)
            done.append(((part,), where))
            after = (part,)
        sums.append(done)
        return after

    def backward_piece(index, part, before, final, after):
        own, where = sums[index][part]
        span = parts[part] if index == last else whole
        other = [shifted(value, "wid", 1) for value in own]
        cost = 1.0 if index == last else 60.0
        return backward(own, other, where, back_weights, span, heights[index], before, final, after, cost)

    def near_step(results):
        return fold_near(results[3], shifted(results[4], "tok", 1))

    def far_step(near):
        return fold_far(near[0], swapped(near[1], "hid", 1))

    def end_step(far, earlier=()):
        return fold_last(far[0], swapped(far[1], "hid", 2), earlier)

    done = forward_piece(1, (dhid,))
    grads = [backward_piece(0, 0, None, True, done)]
    inputs.append(gather_both(last, (inputs[1][0][0],), (grads[0][1],)))
    near = near_step(grads[0])
    done = forward_piece(last, (near[0],))
    all_x, all_y = [
        joined([(array, p[k][2], rows) for p, rows in zip(inputs, heights) for array in p[k][:2]], k == 0, done)
        for k in range(2)
    ]
    far = far_step(near)
    grads.append(backward_piece(1, 0, None, True, (all_x, all_y, far[0])))
    finished = [end_step(far)]

    def with_last(results, k, part):
        return [(grads[c][k], parts[part][0]) for c in range(last)] + [(results[k], 0)]

    down, columns, before, waits = (), (), None, (grads[1][1], finished[0])
    for part in range(len(parts)):
        final = part == len(parts) - 1
        results = backward_piece(last, part, before, final, waits)
        before = results[3]
        near = near_step(results if final else grads[1]) if final or part == 0 else None
        down, down_token = row_grads(
            with_last(results, 0, part), all_y, parts[part], total, down, () if final or near is None else (near[0],),
            3.0 if final else 0.1,
        )
        down = (down,)
        far = far_step(near) if near is not None else None
        ahead = () if near is None else (near[0],) if final else (far[0],)
        *columns, token = column_grads(
            all_x, with_last(results, 1, part), with_last(results, 2, part), parts[part], total, tuple(columns),
            (*ahead, down_token), 5.0 if final else 0.1,
        )
        if part == 0:
            finished.append(end_step(far))
        waits = (token, finished[-1])
    return end_step(far, finished), *columns, *down


def shards(acts, grad_out, w_gate, w_up, w_down):
    sizes = tuple(lax.axis_size(axis) for axis in ("hid", "wid", "tok"))
    aligned = acts.shape[0] % (64 * sum(PIECES)) == 0 and acts.shape[1] % 128 == 0 and w_gate.shape[0] % 512 == 0 and w_gate.shape[1] % 1792 == 0
    if sizes == (4, 2, 2) and aligned:
        return piped(acts, grad_out, w_gate, w_up, w_down)
    return plain(acts, grad_out, w_gate, w_up, w_down)


def solution(mesh):
    placed = (
        P(("groups", "tok"), ("wid", "hid")),
        P(("groups", "tok"), ("wid", "hid")),
        P("wid", ("hid", "tok")),
        P("wid", ("hid", "tok")),
        P(("hid", "tok"), "wid"),
    )
    return jax.shard_map(
        shards,
        mesh=mesh,
        in_specs=placed,
        out_specs=(
            P(("groups", "tok"), ("wid", "hid")),
            P(("groups", "wid"), ("hid", "tok")),
            P(("groups", "wid"), ("hid", "tok")),
            P(("groups", "hid", "tok"), "wid"),
        ),
        check_vma=False,
    )
```

```python
import functools

import jax
import jax.numpy as jnp
from jax import lax
from jax.experimental import pallas as pl
from jax.experimental.pallas import tpu as pltpu
from jax.sharding import PartitionSpec as P

PIECES = (1, 1, 1)
PARTS = (4, 3)
MIB = 1 << 20


def dot(left, right, dims):
    return lax.dot_general(left, right, (dims, ((), ())), preferred_element_type=jnp.float32)


def rows_by_cols(left, right):
    return dot(left, right, ((1,), (0,)))


def over_cols(left, right):
    return dot(left, right, ((1,), (1,)))


def over_rows(left, right):
    return dot(left, right, ((0,), (0,)))


def swiglu_grads(gate, up, dhid):
    sig = jax.nn.sigmoid(gate)
    hidden = (gate * sig * up).astype(jnp.bfloat16)
    d_gate = (dhid * up * sig * (1.0 + gate * (1.0 - sig))).astype(jnp.bfloat16)
    d_up = (dhid * gate * sig).astype(jnp.bfloat16)
    return hidden, d_gate, d_up


def shifted(value, axis, step):
    n = lax.axis_size(axis)
    return lax.ppermute(value, axis, [(i, (i + step) % n) for i in range(n)])


def swapped(value, axis, bit):
    n = lax.axis_size(axis)
    return lax.ppermute(value, axis, [(i, i ^ bit) for i in range(n)])


def summed(value, axis):
    total = value.astype(jnp.float32)
    for step in range(1, lax.axis_size(axis)):
        total = total + shifted(value, axis, step).astype(jnp.float32)
    return total


def own_first(value, axis):
    return jnp.concatenate([value] + [shifted(value, axis, step) for step in range(1, lax.axis_size(axis))], axis=0)


def home_rows(back, axis):
    n = lax.axis_size(axis)
    rows = back.shape[0] // n
    sent = back.astype(jnp.bfloat16)
    total = back[:rows]
    for step in range(1, n):
        block = sent[step * rows : (step + 1) * rows]
        total = total + shifted(block, axis, n - step).astype(jnp.float32)
    return total


def plain(acts, grad_out, w_gate, w_up, w_down):
    x = own_first(lax.all_gather(acts, "hid", axis=1, tiled=True), "tok")
    dy = own_first(lax.all_gather(grad_out, "hid", axis=1, tiled=True), "tok")
    gate = summed(rows_by_cols(x, w_gate).astype(jnp.bfloat16), "wid")
    up = summed(rows_by_cols(x, w_up).astype(jnp.bfloat16), "wid")
    dhid = summed(over_cols(dy, w_down).astype(jnp.bfloat16), "wid")
    hidden, d_gate, d_up = swiglu_grads(gate, up, dhid)
    back = home_rows(over_cols(d_gate, w_gate) + over_cols(d_up, w_up), "tok").astype(jnp.bfloat16)
    back = lax.psum_scatter(back, "hid", scatter_dimension=1, tiled=True)
    return (
        back,
        over_rows(x, d_gate).astype(jnp.bfloat16),
        over_rows(x, d_up).astype(jnp.bfloat16),
        over_rows(hidden, dy).astype(jnp.bfloat16),
    )


VMEM = pl.BlockSpec(memory_space=pltpu.VMEM)
ANYWHERE = pl.BlockSpec(memory_space=pl.ANY)


def declared(cost):
    return pl.CostEstimate(flops=int(cost * 1.15e9), bytes_accessed=0, transcendentals=0)


def local(kernel, outs, args, after=(), limit=12, scratch=(), out_specs=None, cost=0.1):
    def body(*refs):
        kernel(refs[: len(args)], refs[len(args) + len(after) :])

    shapes = [jax.ShapeDtypeStruct(shape, dtype) for shape, dtype in outs]
    return pl.pallas_call(
        body,
        out_shape=shapes,
        in_specs=[VMEM] * len(args) + [ANYWHERE] * len(after),
        out_specs=out_specs if out_specs else [VMEM] * len(outs),
        scratch_shapes=list(scratch),
        compiler_params=pltpu.CompilerParams(vmem_limit_bytes=limit * MIB),
        cost_estimate=declared(cost),
    )(*args, *after)


def lanes(index, width):
    return pl.ds(pl.multiple_of(index * width, width), width)


def cut_rows(acts, grad_out, wanted, after=(), cost=0.1):
    width = acts.shape[1]
    height = sum(rows for _, _, rows in wanted)

    def kernel(ins, outs):
        top = 0
        for array, first, rows in wanted:
            outs[0][top : top + rows] = ins[array][first : first + rows]
            top += rows

    return local(kernel, [((height, width), acts.dtype)], (acts, grad_out), after, 1, cost=cost)[0]


def first_rows(value, rows):
    shape = (rows, value.shape[1])

    def kernel(source, out):
        out[...] = source[...]

    return pl.pallas_call(
        kernel,
        grid=(1,),
        out_shape=jax.ShapeDtypeStruct(shape, value.dtype),
        in_specs=[pl.BlockSpec(shape, lambda i: (0, 0))],
        out_specs=VMEM,
        compiler_params=pltpu.CompilerParams(vmem_limit_bytes=MIB),
        cost_estimate=declared(20.0),
    )(value)


def pack(value, far, after=(), cost=0.1):
    rows, width = value.shape

    def kernel(ins, outs):
        outs[0][:, :width] = ins[0][...]
        outs[0][:, width:] = ins[1][...]

    return local(kernel, [((rows, 2 * width), value.dtype)], (value, far), after, 1, cost=cost)[0]


def arrange(pair, near, heights, cost=0.1):
    width = pair.shape[1] // 2

    def kernel(ins, outs):
        me = lax.axis_index("hid")
        top = 0
        for out, height in zip(outs, heights):
            for step, (source, at) in enumerate(((0, 0), (1, 0), (0, 1), (1, 1))):
                block = ins[source][top : top + height, at * width : (at + 1) * width]
                out[:, lanes(me ^ step, width)] = block
            top += height

    return local(kernel, [((height, 4 * width), pair.dtype) for height in heights], (pair, near), (), 1, cost=cost)


def over_blocks(width, step, body):
    for base in range(0, width, step):
        body(base, min(step, width - base))


def forward(sources, weights, span, rows, after=(), cost=0.3):
    lower, upper = span
    width, features, tokens = upper - lower, sources[0][0].shape[1], 2 * rows
    arrays = [array for own, theirs, _, _ in sources for array in (own, theirs)]

    def kernel(ins, refs):
        out, held = refs
        loaded = None
        for k, (_, _, first, down) in enumerate(sources):
            if loaded is None or arrays[2 * k] is not arrays[2 * loaded] or first != sources[loaded][2]:
                held[:rows] = ins[2 * k][first : first + rows]
                held[rows:] = ins[2 * k + 1][first : first + rows]
                loaded = k
            weight = ins[len(arrays) + k]
            top = k * tokens

            def product(base, size, weight=weight, top=top, down=down):
                at = slice(lower + base, lower + base + size)
                if down:
                    value = over_cols(held[...], weight[at, :])
                else:
                    value = rows_by_cols(held[...], weight[:, at])
                out[top : top + tokens, base : base + size] = value.astype(out.dtype)

            over_blocks(width, 1024, product)

    return local(
        kernel,
        [((len(sources) * tokens, width), jnp.bfloat16)],
        (*arrays, *weights),
        after,
        scratch=[pltpu.VMEM((tokens, features), jnp.bfloat16)],
        cost=cost,
    )[0]


def backward(own, other, where, weights, span, rows, before, final, after=(), cost=1.0, above=()):
    lower, upper = span
    width, features, tokens = upper - lower, weights[0].shape[0], 2 * rows
    count = len(own)
    ins_all = (*own, *other, *weights, *(() if before is None else (before,)), *above)
    upper_rows = above[0].shape[0] if above else 0
    outs_all = [((width, tokens), jnp.bfloat16)] + [((tokens, width), jnp.bfloat16)] * 2
    height = upper_rows + rows
    outs_all += [((height, features), jnp.float32), ((height, features), jnp.bfloat16)] if final else [((tokens, features), jnp.float32)]

    def kernel(ins, outs):
        for k in range(len(above)):
            outs[3 + k][:upper_rows] = ins[len(ins_all) - len(above) + k][...]

        @pl.loop(0, width // 128)
        def _(j):
            at = lanes(j, 128)

            def total(k):
                array, top = where[k]
                mine = ins[array][top : top + tokens, at].astype(jnp.float32)
                return mine + ins[count + array][top : top + tokens, at].astype(jnp.float32)

            hidden, outs[1][:, at], outs[2][:, at] = swiglu_grads(total(0), total(1), total(2))
            outs[0][at, :] = hidden.T

        def product(base, size):
            at = slice(base, base + size)
            value = over_cols(outs[1][...], ins[2 * count][at, lower:upper])
            value = value + over_cols(outs[2][...], ins[2 * count + 1][at, lower:upper])
            if before is not None:
                value = value + ins[2 * count + 2][:, at]
            if final:
                outs[3][upper_rows:, at] = value[:rows]
                outs[4][upper_rows:, at] = value[rows:].astype(jnp.bfloat16)
            else:
                outs[3][:, at] = value

        over_blocks(features, 1024, product)

    return local(kernel, outs_all, ins_all, after, cost=cost)


def fold_near(value, theirs):
    rows, width = value.shape[0], value.shape[1] // 4

    def kernel(ins, outs):
        odd = lax.rem(lax.axis_index("hid"), 2)
        for i in range(2):
            at = slice(i * width, (i + 1) * width)
            for block, out in ((2 * i + odd, outs[0]), (2 * i + 1 - odd, outs[1])):
                source = lanes(block, width)
                out[:, at] = (ins[0][:, source] + ins[1][:, source].astype(jnp.float32)).astype(out.dtype)

    outs = [((rows, 2 * width), jnp.float32), ((rows, 2 * width), jnp.bfloat16)]
    return local(kernel, outs, (value, theirs), limit=4)


def fold_far(value, theirs, after=()):
    rows, width = value.shape[0], value.shape[1] // 2

    def kernel(ins, outs):
        upper = lax.div(lax.axis_index("hid"), 2)
        for block, out in ((upper, outs[0]), (1 - upper, outs[1])):
            source = lanes(block, width)
            out[...] = (ins[0][:, source] + ins[1][:, source].astype(jnp.float32)).astype(out.dtype)

    outs = [((rows, width), jnp.float32), ((rows, width), jnp.bfloat16)]
    return local(kernel, outs, (value, theirs), after, limit=4)


def fold_last(mine, theirs, earlier=()):
    heights = [piece.shape[0] for piece in earlier]
    rows, width = mine.shape
    shape = (sum(heights) + rows, width)

    def kernel(ins, outs):
        top = 0
        for c, height in enumerate(heights):
            outs[0][top : top + height] = ins[2 + c][...]
            top += height
        outs[0][top:] = (ins[0][...] + ins[1][...].astype(jnp.float32)).astype(jnp.bfloat16)

    specs = [pl.BlockSpec(shape, lambda: (0, 0))] if earlier else None
    return local(kernel, [(shape, jnp.bfloat16)], (mine, theirs, *earlier), limit=4, out_specs=specs)[0]


def joined(pieces, turn, after=()):
    tokens, features = sum(p[2] for p in pieces), pieces[0][0].shape[1]

    def kernel(ins, outs):
        @pl.loop(0, features // 512)
        def _(j):
            at = lanes(j, 512)
            rows = jnp.concatenate([ins[i][p[1] : p[1] + p[2], at] for i, p in enumerate(pieces)], axis=0)
            if turn:
                outs[0][at, :] = rows.T
            else:
                outs[0][:, at] = rows

    shape = (features, tokens) if turn else (tokens, features)
    return local(kernel, [(shape, jnp.bfloat16)], [p[0] for p in pieces], after, limit=4)[0]


def gradients(kernel, outs, arrays, old, grid, specs, scratch, after, cost):
    def body(*refs):
        kernel(refs[: len(arrays)], refs[len(arrays) + len(old) + len(after) :])

    outs, specs = [*outs, (16, 128)], [*specs, VMEM]
    return pl.pallas_call(
        body,
        grid=grid,
        out_shape=[jax.ShapeDtypeStruct(shape, jnp.bfloat16) for shape in outs],
        in_specs=[VMEM] * len(arrays) + [ANYWHERE] * (len(old) + len(after)),
        out_specs=specs,
        scratch_shapes=scratch,
        input_output_aliases={len(arrays) + i: i for i in range(len(old))},
        compiler_params=pltpu.CompilerParams(vmem_limit_bytes=14 * MIB),
        cost_estimate=declared(cost),
    )(*arrays, *old, *after)


def tiled(out, left, right):
    height, width = out.shape
    for top in range(0, height, 512):
        for start in range(0, width, 256):
            rows, columns = pl.ds(top, min(512, height - top)), pl.ds(start, min(256, width - start))
            out[rows, columns] = rows_by_cols(left[rows, :], right[:, columns]).astype(out.dtype)


def placed(rows, columns, where):
    return pl.BlockSpec((pl.Element(rows), pl.Element(columns)), where)


def column_grads(x, gs, us, span, total, old, after=(), cost=0.1):
    arrays = [x, *(p[0] for p in (*gs, *us))]
    count, lower, width = len(gs), span[0], span[1] - span[0]
    features, tokens = x.shape
    block = 512

    def kernel(ins, refs):
        gate_out, up_out, token, g_all, u_all = refs
        step = pl.program_id(0)

        @pl.when(step == 0)
        def _():
            token[...] = jnp.zeros_like(token)
            for first, pieces, target in ((1, gs, g_all), (1 + count, us, u_all)):
                top = 0
                for i, (piece, column) in enumerate(pieces):
                    rows = piece.shape[0]
                    target[top : top + rows] = ins[first + i][:, column : column + width]
                    top += rows

        rows = ins[0].at[lanes(step, block), :]
        tiled(gate_out, rows, g_all)
        tiled(up_out, rows, u_all)

    spec = placed(block, width, lambda i: (pl.multiple_of(i * block, block), lower))
    scratch = [pltpu.VMEM((tokens, width), jnp.bfloat16)] * 2
    return gradients(kernel, [(features, total)] * 2, arrays, old, (features // block,), [spec, spec], scratch, after, cost)


def row_grads(hs, y, span, total, old, after=(), cost=0.1):
    arrays = [*(p[0] for p in hs), y]
    count, lower, width = len(hs), span[0], span[1] - span[0]
    tokens, features = y.shape
    block = 512

    def kernel(ins, refs):
        out, token, h_all = refs
        step = pl.program_id(0)

        @pl.when(step == 0)
        def _():
            token[...] = jnp.zeros_like(token)
            left = 0
            for i, (piece, row) in enumerate(hs):
                h_all[:, left : left + piece.shape[1]] = ins[i][row : row + width]
                left += piece.shape[1]

        tiled(out, h_all, ins[count].at[:, lanes(step, block)])

    spec = placed(width, block, lambda i: (lower, pl.multiple_of(i * block, block)))
    scratch = [pltpu.VMEM((width, tokens), jnp.bfloat16)]
    return gradients(kernel, [(total, features)], arrays, old, (features // block,), [spec], scratch, after, cost)


def piped(acts, grad_out, w_gate, w_up, w_down):
    unit = acts.shape[0] // sum(PIECES)
    bounds = [0]
    for size in PIECES:
        bounds.append(bounds[-1] + size * unit)
    spans = list(zip(bounds[:-1], bounds[1:]))
    heights = [upper - lower for lower, upper in spans]
    last = len(spans) - 1
    total = w_gate.shape[1]
    fraction = total // sum(PARTS)
    edges = [sum(PARTS[:i]) * fraction for i in range(len(PARTS) + 1)]
    whole, parts = (0, total), list(zip(edges[:-1], edges[1:]))
    back_weights = (w_gate, w_up)

    def gather(value, parts, early=(), costs=(0.1, 0.1)):
        pair = pack(value, swapped(value, "hid", 2), early, costs[0])
        own = arrange(pair, swapped(pair, "hid", 1), [value.shape[0] // parts] * parts, costs[1])
        return [(array, shifted(array, "tok", 1), 0) for array in own]

    def gather_both(index, after, early=()):
        lower, upper = spans[index]
        mixed = cut_rows(acts, grad_out, [(0, lower, upper - lower), (1, lower, upper - lower)], after)
        return gather(mixed, 2, early)

    rows = heights[0]
    x, = gather(first_rows(acts, rows), 1)
    dy, = gather(cut_rows(acts, grad_out, [(1, 0, rows)]), 1, costs=(1.2, 5.0))
    inputs = [(x, dy), gather_both(1, (dy[0],))]
    gate_up = forward([(*x, False), (*x, False)], (w_gate, w_up), whole, rows)
    dhid = forward([(*dy, True)], (w_down,), whole, rows, (gate_up,))
    sums = [[((gate_up, dhid), ((0, 0), (0, 2 * rows), (1, 0)))]]

    def forward_piece(index, after):
        x, dy = inputs[index]
        rows = heights[index]
        where = ((0, 0), (0, 2 * rows), (0, 4 * rows))
        done = []
        for span in parts if index == last else (whole,):
            part = forward([(*x, False), (*x, False), (*dy, True)], (w_gate, w_up, w_down), span, rows, after)
            done.append(((part,), where))
            after = (part,)
        sums.append(done)
        return after

    def backward_piece(index, part, before, final, after, above=()):
        own, where = sums[index][part]
        span = parts[part] if index == last else whole
        other = [shifted(value, "wid", 1) for value in own]
        cost = 0.1 if index == last else 60.0
        return backward(own, other, where, back_weights, span, heights[index], before, final, after, cost, above)

    def near_step(results):
        return fold_near(results[3], shifted(results[4], "tok", 1))

    def far_step(near, after=()):
        return fold_far(near[0], swapped(near[1], "hid", 1), after)

    def end_step(far, earlier=()):
        return fold_last(far[0], swapped(far[1], "hid", 2), earlier)

    done = forward_piece(1, (dhid,))
    grads = [backward_piece(0, 0, None, True, done)]
    inputs.append(gather_both(last, (inputs[1][0][0],), (grads[0][1],)))
    done = forward_piece(last, (grads[0][1],))
    all_x, all_y = [
        joined([(array, p[k][2], rows) for p, rows in zip(inputs, heights) for array in p[k][:2]], k == 0, done)
        for k in range(2)
    ]
    grads.append(backward_piece(1, 0, None, True, (all_x, all_y), grads[0][3:]))

    def with_last(results, k, part):
        return [(grads[c][k], parts[part][0]) for c in range(last)] + [(results[k], 0)]

    near = near_step(grads[1])
    first = backward_piece(last, 0, None, False, (near[0],))
    down, token = row_grads(with_last(first, 0, 0), all_y, parts[0], total, (), (), 2.0)
    far = far_step(near, (token,))
    gate, up, token = column_grads(
        all_x, with_last(first, 1, 0), with_last(first, 2, 0), parts[0], total, (), (far[0], token)
    )
    finished = end_step(far)
    second = backward_piece(last, 1, first[3], True, (token, finished))
    near = near_step(second)
    down, token = row_grads(with_last(second, 0, 1), all_y, parts[1], total, (down,), (), 3.0)
    far = far_step(near)
    gate, up, _ = column_grads(
        all_x, with_last(second, 1, 1), with_last(second, 2, 1), parts[1], total, (gate, up), (near[0], token), 5.0
    )
    return end_step(far, (finished,)), gate, up, down


def shards(acts, grad_out, w_gate, w_up, w_down):
    sizes = tuple(lax.axis_size(axis) for axis in ("hid", "wid", "tok"))
    aligned = acts.shape[0] % (64 * sum(PIECES)) == 0 and acts.shape[1] % 128 == 0 and w_gate.shape[0] % 512 == 0 and w_gate.shape[1] % 1792 == 0
    if sizes == (4, 2, 2) and aligned:
        return piped(acts, grad_out, w_gate, w_up, w_down)
    return plain(acts, grad_out, w_gate, w_up, w_down)


def solution(mesh):
    placed = (
        P(("groups", "tok"), ("wid", "hid")),
        P(("groups", "tok"), ("wid", "hid")),
        P("wid", ("hid", "tok")),
        P("wid", ("hid", "tok")),
        P(("hid", "tok"), "wid"),
    )
    return jax.shard_map(
        shards,
        mesh=mesh,
        in_specs=placed,
        out_specs=(
            P(("groups", "tok"), ("wid", "hid")),
            P(("groups", "wid"), ("hid", "tok")),
            P(("groups", "wid"), ("hid", "tok")),
            P(("groups", "hid", "tok"), "wid"),
        ),
        check_vma=False,
    )
```

```python
import functools

import jax
import jax.numpy as jnp
from jax import lax
from jax.experimental import pallas as pl
from jax.experimental.pallas import tpu as pltpu
from jax.sharding import PartitionSpec as P

PIECES = (1, 1, 1)
PARTS = (1, 1)
MIB = 1 << 20


def dot(left, right, dims):
    return lax.dot_general(left, right, (dims, ((), ())), preferred_element_type=jnp.float32)


def rows_by_cols(left, right):
    return dot(left, right, ((1,), (0,)))


def over_cols(left, right):
    return dot(left, right, ((1,), (1,)))


def over_rows(left, right):
    return dot(left, right, ((0,), (0,)))


def swiglu_grads(gate, up, dhid):
    sig = jax.nn.sigmoid(gate)
    hidden = (gate * sig * up).astype(jnp.bfloat16)
    d_gate = (dhid * up * sig * (1.0 + gate * (1.0 - sig))).astype(jnp.bfloat16)
    d_up = (dhid * gate * sig).astype(jnp.bfloat16)
    return hidden, d_gate, d_up


def shifted(value, axis, step):
    n = lax.axis_size(axis)
    return lax.ppermute(value, axis, [(i, (i + step) % n) for i in range(n)])


def swapped(value, axis, bit):
    n = lax.axis_size(axis)
    return lax.ppermute(value, axis, [(i, i ^ bit) for i in range(n)])


def summed(value, axis):
    total = value.astype(jnp.float32)
    for step in range(1, lax.axis_size(axis)):
        total = total + shifted(value, axis, step).astype(jnp.float32)
    return total


def own_first(value, axis):
    return jnp.concatenate([value] + [shifted(value, axis, step) for step in range(1, lax.axis_size(axis))], axis=0)


def home_rows(back, axis):
    n = lax.axis_size(axis)
    rows = back.shape[0] // n
    sent = back.astype(jnp.bfloat16)
    total = back[:rows]
    for step in range(1, n):
        block = sent[step * rows : (step + 1) * rows]
        total = total + shifted(block, axis, n - step).astype(jnp.float32)
    return total


def plain(acts, grad_out, w_gate, w_up, w_down):
    x = own_first(lax.all_gather(acts, "hid", axis=1, tiled=True), "tok")
    dy = own_first(lax.all_gather(grad_out, "hid", axis=1, tiled=True), "tok")
    gate = summed(rows_by_cols(x, w_gate).astype(jnp.bfloat16), "wid")
    up = summed(rows_by_cols(x, w_up).astype(jnp.bfloat16), "wid")
    dhid = summed(over_cols(dy, w_down).astype(jnp.bfloat16), "wid")
    hidden, d_gate, d_up = swiglu_grads(gate, up, dhid)
    back = home_rows(over_cols(d_gate, w_gate) + over_cols(d_up, w_up), "tok").astype(jnp.bfloat16)
    back = lax.psum_scatter(back, "hid", scatter_dimension=1, tiled=True)
    return (
        back,
        over_rows(x, d_gate).astype(jnp.bfloat16),
        over_rows(x, d_up).astype(jnp.bfloat16),
        over_rows(hidden, dy).astype(jnp.bfloat16),
    )


VMEM = pl.BlockSpec(memory_space=pltpu.VMEM)
ANYWHERE = pl.BlockSpec(memory_space=pl.ANY)


def declared(cost):
    return pl.CostEstimate(flops=int(cost * 1.15e9), bytes_accessed=0, transcendentals=0)


def local(kernel, outs, args, after=(), limit=12, scratch=(), out_specs=None, cost=0.1):
    def body(*refs):
        kernel(refs[: len(args)], refs[len(args) + len(after) :])

    shapes = [jax.ShapeDtypeStruct(shape, dtype) for shape, dtype in outs]
    return pl.pallas_call(
        body,
        out_shape=shapes,
        in_specs=[VMEM] * len(args) + [ANYWHERE] * len(after),
        out_specs=out_specs if out_specs else [VMEM] * len(outs),
        scratch_shapes=list(scratch),
        compiler_params=pltpu.CompilerParams(vmem_limit_bytes=limit * MIB),
        cost_estimate=declared(cost),
    )(*args, *after)


def lanes(index, width):
    return pl.ds(pl.multiple_of(index * width, width), width)


def cut_rows(acts, grad_out, wanted, after=(), cost=0.1):
    width = acts.shape[1]
    height = sum(rows for _, _, rows in wanted)

    def kernel(ins, outs):
        top = 0
        for array, first, rows in wanted:
            outs[0][top : top + rows] = ins[array][first : first + rows]
            top += rows

    return local(kernel, [((height, width), acts.dtype)], (acts, grad_out), after, 1, cost=cost)[0]


def first_rows(value, rows):
    shape = (rows, value.shape[1])

    def kernel(source, out):
        out[...] = source[...]

    return pl.pallas_call(
        kernel,
        grid=(1,),
        out_shape=jax.ShapeDtypeStruct(shape, value.dtype),
        in_specs=[pl.BlockSpec(shape, lambda i: (0, 0))],
        out_specs=VMEM,
        compiler_params=pltpu.CompilerParams(vmem_limit_bytes=MIB),
        cost_estimate=declared(20.0),
    )(value)


def pack(value, far, after=(), cost=0.1):
    rows, width = value.shape

    def kernel(ins, outs):
        outs[0][:, :width] = ins[0][...]
        outs[0][:, width:] = ins[1][...]

    return local(kernel, [((rows, 2 * width), value.dtype)], (value, far), after, 1, cost=cost)[0]


def arrange(pair, near, heights, cost=0.1):
    width = pair.shape[1] // 2

    def kernel(ins, outs):
        me = lax.axis_index("hid")
        top = 0
        for out, height in zip(outs, heights):
            for step, (source, at) in enumerate(((0, 0), (1, 0), (0, 1), (1, 1))):
                block = ins[source][top : top + height, at * width : (at + 1) * width]
                out[:, lanes(me ^ step, width)] = block
            top += height

    return local(kernel, [((height, 4 * width), pair.dtype) for height in heights], (pair, near), (), 1, cost=cost)


def over_blocks(width, step, body):
    for base in range(0, width, step):
        body(base, min(step, width - base))


def forward(sources, weights, span, rows, after=(), cost=0.3):
    lower, upper = span
    width, features, tokens = upper - lower, sources[0][0].shape[1], 2 * rows
    arrays = [array for own, theirs, _, _ in sources for array in (own, theirs)]

    def kernel(ins, refs):
        out, held = refs
        loaded = None
        for k, (_, _, first, down) in enumerate(sources):
            if loaded is None or arrays[2 * k] is not arrays[2 * loaded] or first != sources[loaded][2]:
                held[:rows] = ins[2 * k][first : first + rows]
                held[rows:] = ins[2 * k + 1][first : first + rows]
                loaded = k
            weight = ins[len(arrays) + k]
            top = k * tokens

            def product(base, size, weight=weight, top=top, down=down):
                at = slice(lower + base, lower + base + size)
                if down:
                    value = over_cols(held[...], weight[at, :])
                else:
                    value = rows_by_cols(held[...], weight[:, at])
                out[top : top + tokens, base : base + size] = value.astype(out.dtype)

            over_blocks(width, 1024, product)

    return local(
        kernel,
        [((len(sources) * tokens, width), jnp.bfloat16)],
        (*arrays, *weights),
        after,
        scratch=[pltpu.VMEM((tokens, features), jnp.bfloat16)],
        cost=cost,
    )[0]


def backward(own, other, where, weights, span, rows, before, final, after=(), cost=1.0, above=()):
    lower, upper = span
    width, features, tokens = upper - lower, weights[0].shape[0], 2 * rows
    count = len(own)
    ins_all = (*own, *other, *weights, *(() if before is None else (before,)), *above)
    upper_rows = above[0].shape[0] if above else 0
    outs_all = [((width, tokens), jnp.bfloat16)] + [((tokens, width), jnp.bfloat16)] * 2
    height = upper_rows + rows
    outs_all += [((height, features), jnp.float32), ((height, features), jnp.bfloat16)] if final else [((tokens, features), jnp.float32)]

    def kernel(ins, outs):
        for k in range(len(above)):
            outs[3 + k][:upper_rows] = ins[len(ins_all) - len(above) + k][...]

        step = 256 if width % 256 == 0 else 128

        @pl.loop(0, width // step)
        def _(j):
            at = lanes(j, step)

            def total(k):
                array, top = where[k]
                mine = ins[array][top : top + tokens, at].astype(jnp.float32)
                return mine + ins[count + array][top : top + tokens, at].astype(jnp.float32)

            hidden, outs[1][:, at], outs[2][:, at] = swiglu_grads(total(0), total(1), total(2))
            outs[0][at, :] = hidden.T

        def product(base, size):
            at = slice(base, base + size)
            value = over_cols(outs[1][...], ins[2 * count][at, lower:upper])
            value = value + over_cols(outs[2][...], ins[2 * count + 1][at, lower:upper])
            if before is not None:
                value = value + ins[2 * count + 2][:, at]
            if final:
                outs[3][upper_rows:, at] = value[:rows]
                outs[4][upper_rows:, at] = value[rows:].astype(jnp.bfloat16)
            else:
                outs[3][:, at] = value

        over_blocks(features, 1024, product)

    return local(kernel, outs_all, ins_all, after, cost=cost)


def fold_near(value, theirs):
    rows, width = value.shape[0], value.shape[1] // 4

    def kernel(ins, outs):
        odd = lax.rem(lax.axis_index("hid"), 2)
        for i in range(2):
            at = slice(i * width, (i + 1) * width)
            for block, out in ((2 * i + odd, outs[0]), (2 * i + 1 - odd, outs[1])):
                source = lanes(block, width)
                out[:, at] = (ins[0][:, source] + ins[1][:, source].astype(jnp.float32)).astype(out.dtype)

    outs = [((rows, 2 * width), jnp.float32), ((rows, 2 * width), jnp.bfloat16)]
    return local(kernel, outs, (value, theirs), limit=4)


def fold_far(value, theirs, after=()):
    rows, width = value.shape[0], value.shape[1] // 2

    def kernel(ins, outs):
        upper = lax.div(lax.axis_index("hid"), 2)
        for block, out in ((upper, outs[0]), (1 - upper, outs[1])):
            source = lanes(block, width)
            out[...] = (ins[0][:, source] + ins[1][:, source].astype(jnp.float32)).astype(out.dtype)

    outs = [((rows, width), jnp.float32), ((rows, width), jnp.bfloat16)]
    return local(kernel, outs, (value, theirs), after, limit=4)


def fold_last(mine, theirs, earlier=()):
    heights = [piece.shape[0] for piece in earlier]
    rows, width = mine.shape
    shape = (sum(heights) + rows, width)

    def kernel(ins, outs):
        top = 0
        for c, height in enumerate(heights):
            outs[0][top : top + height] = ins[2 + c][...]
            top += height
        outs[0][top:] = (ins[0][...] + ins[1][...].astype(jnp.float32)).astype(jnp.bfloat16)

    specs = [pl.BlockSpec(shape, lambda: (0, 0))] if earlier else None
    return local(kernel, [(shape, jnp.bfloat16)], (mine, theirs, *earlier), limit=4, out_specs=specs)[0]


def joined(pieces, turn, after=()):
    tokens, features = sum(p[2] for p in pieces), pieces[0][0].shape[1]

    def kernel(ins, outs):
        @pl.loop(0, features // 512)
        def _(j):
            at = lanes(j, 512)
            rows = jnp.concatenate([ins[i][p[1] : p[1] + p[2], at] for i, p in enumerate(pieces)], axis=0)
            if turn:
                outs[0][at, :] = rows.T
            else:
                outs[0][:, at] = rows

    shape = (features, tokens) if turn else (tokens, features)
    return local(kernel, [(shape, jnp.bfloat16)], [p[0] for p in pieces], after, limit=4)[0]


def gradients(kernel, outs, arrays, old, grid, specs, scratch, after, cost):
    def body(*refs):
        kernel(refs[: len(arrays)], refs[len(arrays) + len(old) + len(after) :])

    outs, specs = [*outs, (16, 128)], [*specs, VMEM]
    return pl.pallas_call(
        body,
        grid=grid,
        out_shape=[jax.ShapeDtypeStruct(shape, jnp.bfloat16) for shape in outs],
        in_specs=[VMEM] * len(arrays) + [ANYWHERE] * (len(old) + len(after)),
        out_specs=specs,
        scratch_shapes=scratch,
        input_output_aliases={len(arrays) + i: i for i in range(len(old))},
        compiler_params=pltpu.CompilerParams(vmem_limit_bytes=14 * MIB),
        cost_estimate=declared(cost),
    )(*arrays, *old, *after)


def tiled(out, left, right):
    height, width = out.shape
    for top in range(0, height, 512):
        for start in range(0, width, 256):
            rows, columns = pl.ds(top, min(512, height - top)), pl.ds(start, min(256, width - start))
            out[rows, columns] = rows_by_cols(left[rows, :], right[:, columns]).astype(out.dtype)


def placed(rows, columns, where):
    return pl.BlockSpec((pl.Element(rows), pl.Element(columns)), where)


def column_grads(x, gs, us, span, total, old, after=(), cost=0.1):
    arrays = [x, *(p[0] for p in (*gs, *us))]
    count, lower, width = len(gs), span[0], span[1] - span[0]
    features, tokens = x.shape
    block = 512

    def kernel(ins, refs):
        gate_out, up_out, token, g_all, u_all = refs
        step = pl.program_id(0)

        @pl.when(step == 0)
        def _():
            token[...] = jnp.zeros_like(token)
            for first, pieces, target in ((1, gs, g_all), (1 + count, us, u_all)):
                top = 0
                for i, (piece, column) in enumerate(pieces):
                    rows = piece.shape[0]
                    target[top : top + rows] = ins[first + i][:, column : column + width]
                    top += rows

        rows = ins[0].at[lanes(step, block), :]
        tiled(gate_out, rows, g_all)
        tiled(up_out, rows, u_all)

    spec = placed(block, width, lambda i: (pl.multiple_of(i * block, block), lower))
    scratch = [pltpu.VMEM((tokens, width), jnp.bfloat16)] * 2
    return gradients(kernel, [(features, total)] * 2, arrays, old, (features // block,), [spec, spec], scratch, after, cost)


def row_grads(hs, y, span, total, old, after=(), cost=0.1):
    arrays = [*(p[0] for p in hs), y]
    count, lower, width = len(hs), span[0], span[1] - span[0]
    tokens, features = y.shape
    block = 512

    def kernel(ins, refs):
        out, token, h_all = refs
        step = pl.program_id(0)

        @pl.when(step == 0)
        def _():
            token[...] = jnp.zeros_like(token)
            left = 0
            for i, (piece, row) in enumerate(hs):
                h_all[:, left : left + piece.shape[1]] = ins[i][row : row + width]
                left += piece.shape[1]

        tiled(out, h_all, ins[count].at[:, lanes(step, block)])

    spec = placed(width, block, lambda i: (lower, pl.multiple_of(i * block, block)))
    scratch = [pltpu.VMEM((width, tokens), jnp.bfloat16)]
    return gradients(kernel, [(total, features)], arrays, old, (features // block,), [spec], scratch, after, cost)


def piped(acts, grad_out, w_gate, w_up, w_down):
    unit = acts.shape[0] // sum(PIECES)
    bounds = [0]
    for size in PIECES:
        bounds.append(bounds[-1] + size * unit)
    spans = list(zip(bounds[:-1], bounds[1:]))
    heights = [upper - lower for lower, upper in spans]
    last = len(spans) - 1
    total = w_gate.shape[1]
    fraction = total // sum(PARTS)
    edges = [sum(PARTS[:i]) * fraction for i in range(len(PARTS) + 1)]
    whole, parts = (0, total), list(zip(edges[:-1], edges[1:]))
    back_weights = (w_gate, w_up)

    def gather(value, parts, early=(), costs=(0.1, 0.1)):
        pair = pack(value, swapped(value, "hid", 2), early, costs[0])
        own = arrange(pair, swapped(pair, "hid", 1), [value.shape[0] // parts] * parts, costs[1])
        return [(array, shifted(array, "tok", 1), 0) for array in own]

    def gather_both(index, after, early=()):
        lower, upper = spans[index]
        mixed = cut_rows(acts, grad_out, [(0, lower, upper - lower), (1, lower, upper - lower)], after)
        return gather(mixed, 2, early)

    rows = heights[0]
    x, = gather(first_rows(acts, rows), 1)
    dy, = gather(cut_rows(acts, grad_out, [(1, 0, rows)]), 1, costs=(1.2, 5.0))
    inputs = [(x, dy), gather_both(1, (dy[0],))]
    gate_up = forward([(*x, False), (*x, False)], (w_gate, w_up), whole, rows)
    dhid = forward([(*dy, True)], (w_down,), whole, rows, (gate_up,))
    sums = [[((gate_up, dhid), ((0, 0), (0, 2 * rows), (1, 0)))]]

    def forward_piece(index, after):
        x, dy = inputs[index]
        rows = heights[index]
        where = ((0, 0), (0, 2 * rows), (0, 4 * rows))
        done = []
        for span in parts if index == last else (whole,):
            part = forward([(*x, False), (*x, False), (*dy, True)], (w_gate, w_up, w_down), span, rows, after)
            done.append(((part,), where))
            after = (part,)
        sums.append(done)
        return after

    def backward_piece(index, part, before, final, after, above=()):
        own, where = sums[index][part]
        span = parts[part] if index == last else whole
        other = [shifted(value, "wid", 1) for value in own]
        cost = 0.1 if index == last else 60.0
        return backward(own, other, where, back_weights, span, heights[index], before, final, after, cost, above)

    def near_step(results):
        return fold_near(results[3], shifted(results[4], "tok", 1))

    def far_step(near, after=()):
        return fold_far(near[0], swapped(near[1], "hid", 1), after)

    def end_step(far, earlier=()):
        return fold_last(far[0], swapped(far[1], "hid", 2), earlier)

    done = forward_piece(1, (dhid,))
    grads = [backward_piece(0, 0, None, True, done)]
    inputs.append(gather_both(last, (inputs[1][0][0],), (grads[0][1],)))
    done = forward_piece(last, (grads[0][1],))
    all_x, all_y = [
        joined([(array, p[k][2], rows) for p, rows in zip(inputs, heights) for array in p[k][:2]], k == 0, done)
        for k in range(2)
    ]
    grads.append(backward_piece(1, 0, None, True, (all_x, all_y), grads[0][3:]))

    def with_last(results, k, part):
        return [(grads[c][k], parts[part][0]) for c in range(last)] + [(results[k], 0)]

    near = near_step(grads[1])
    first = backward_piece(last, 0, None, False, (near[0],))
    down, token = row_grads(with_last(first, 0, 0), all_y, parts[0], total, (), (), 2.0)
    far = far_step(near, (token,))
    gate, up, token = column_grads(
        all_x, with_last(first, 1, 0), with_last(first, 2, 0), parts[0], total, (), (far[0], token)
    )
    finished = end_step(far)
    second = backward_piece(last, 1, first[3], True, (token, finished))
    near = near_step(second)
    down, token = row_grads(with_last(second, 0, 1), all_y, parts[1], total, (down,), (), 3.0)
    far = far_step(near)
    gate, up, _ = column_grads(
        all_x, with_last(second, 1, 1), with_last(second, 2, 1), parts[1], total, (gate, up), (near[0], token), 5.0
    )
    return end_step(far, (finished,)), gate, up, down


def shards(acts, grad_out, w_gate, w_up, w_down):
    sizes = tuple(lax.axis_size(axis) for axis in ("hid", "wid", "tok"))
    aligned = acts.shape[0] % (64 * sum(PIECES)) == 0 and acts.shape[1] % 128 == 0 and w_gate.shape[0] % 512 == 0 and w_gate.shape[1] % 1792 == 0
    if sizes == (4, 2, 2) and aligned:
        return piped(acts, grad_out, w_gate, w_up, w_down)
    return plain(acts, grad_out, w_gate, w_up, w_down)


def solution(mesh):
    placed = (
        P(("groups", "tok"), ("wid", "hid")),
        P(("groups", "tok"), ("wid", "hid")),
        P("wid", ("hid", "tok")),
        P("wid", ("hid", "tok")),
        P(("hid", "tok"), "wid"),
    )
    return jax.shard_map(
        shards,
        mesh=mesh,
        in_specs=placed,
        out_specs=(
            P(("groups", "tok"), ("wid", "hid")),
            P(("groups", "wid"), ("hid", "tok")),
            P(("groups", "wid"), ("hid", "tok")),
            P(("groups", "hid", "tok"), "wid"),
        ),
        check_vma=False,
    )
```

```python
import functools

import jax
import jax.numpy as jnp
from jax import lax
from jax.experimental import pallas as pl
from jax.experimental.pallas import tpu as pltpu
from jax.sharding import PartitionSpec as P

PIECES = (1, 1, 1)
PARTS = (1, 1)
MIB = 1 << 20


def dot(left, right, dims):
    return lax.dot_general(left, right, (dims, ((), ())), preferred_element_type=jnp.float32)


def rows_by_cols(left, right):
    return dot(left, right, ((1,), (0,)))


def over_cols(left, right):
    return dot(left, right, ((1,), (1,)))


def over_rows(left, right):
    return dot(left, right, ((0,), (0,)))


def swiglu_grads(gate, up, dhid):
    sig = jax.nn.sigmoid(gate)
    hidden = (gate * sig * up).astype(jnp.bfloat16)
    d_gate = (dhid * up * sig * (1.0 + gate * (1.0 - sig))).astype(jnp.bfloat16)
    d_up = (dhid * gate * sig).astype(jnp.bfloat16)
    return hidden, d_gate, d_up


def shifted(value, axis, step):
    n = lax.axis_size(axis)
    return lax.ppermute(value, axis, [(i, (i + step) % n) for i in range(n)])


def swapped(value, axis, bit):
    n = lax.axis_size(axis)
    return lax.ppermute(value, axis, [(i, i ^ bit) for i in range(n)])


def summed(value, axis):
    total = value.astype(jnp.float32)
    for step in range(1, lax.axis_size(axis)):
        total = total + shifted(value, axis, step).astype(jnp.float32)
    return total


def own_first(value, axis):
    return jnp.concatenate([value] + [shifted(value, axis, step) for step in range(1, lax.axis_size(axis))], axis=0)


def home_rows(back, axis):
    n = lax.axis_size(axis)
    rows = back.shape[0] // n
    sent = back.astype(jnp.bfloat16)
    total = back[:rows]
    for step in range(1, n):
        block = sent[step * rows : (step + 1) * rows]
        total = total + shifted(block, axis, n - step).astype(jnp.float32)
    return total


def plain(acts, grad_out, w_gate, w_up, w_down):
    x = own_first(lax.all_gather(acts, "hid", axis=1, tiled=True), "tok")
    dy = own_first(lax.all_gather(grad_out, "hid", axis=1, tiled=True), "tok")
    gate = summed(rows_by_cols(x, w_gate).astype(jnp.bfloat16), "wid")
    up = summed(rows_by_cols(x, w_up).astype(jnp.bfloat16), "wid")
    dhid = summed(over_cols(dy, w_down).astype(jnp.bfloat16), "wid")
    hidden, d_gate, d_up = swiglu_grads(gate, up, dhid)
    back = home_rows(over_cols(d_gate, w_gate) + over_cols(d_up, w_up), "tok").astype(jnp.bfloat16)
    back = lax.psum_scatter(back, "hid", scatter_dimension=1, tiled=True)
    return (
        back,
        over_rows(x, d_gate).astype(jnp.bfloat16),
        over_rows(x, d_up).astype(jnp.bfloat16),
        over_rows(hidden, dy).astype(jnp.bfloat16),
    )


VMEM = pl.BlockSpec(memory_space=pltpu.VMEM)
ANYWHERE = pl.BlockSpec(memory_space=pl.ANY)


def declared(cost):
    return pl.CostEstimate(flops=int(cost * 1.15e9), bytes_accessed=0, transcendentals=0)


def local(kernel, outs, args, after=(), limit=12, scratch=(), out_specs=None, cost=0.1):
    def body(*refs):
        kernel(refs[: len(args)], refs[len(args) + len(after) :])

    shapes = [jax.ShapeDtypeStruct(shape, dtype) for shape, dtype in outs]
    return pl.pallas_call(
        body,
        out_shape=shapes,
        in_specs=[VMEM] * len(args) + [ANYWHERE] * len(after),
        out_specs=out_specs if out_specs else [VMEM] * len(outs),
        scratch_shapes=list(scratch),
        compiler_params=pltpu.CompilerParams(vmem_limit_bytes=limit * MIB),
        cost_estimate=declared(cost),
    )(*args, *after)


def lanes(index, width):
    return pl.ds(pl.multiple_of(index * width, width), width)


def cut_rows(acts, grad_out, wanted, after=(), cost=0.1):
    width = acts.shape[1]
    height = sum(rows for _, _, rows in wanted)

    def kernel(ins, outs):
        top = 0
        for array, first, rows in wanted:
            outs[0][top : top + rows] = ins[array][first : first + rows]
            top += rows

    return local(kernel, [((height, width), acts.dtype)], (acts, grad_out), after, 1, cost=cost)[0]


def first_rows(value, rows):
    shape = (rows, value.shape[1])

    def kernel(source, out):
        out[...] = source[...]

    return pl.pallas_call(
        kernel,
        grid=(1,),
        out_shape=jax.ShapeDtypeStruct(shape, value.dtype),
        in_specs=[pl.BlockSpec(shape, lambda i: (0, 0))],
        out_specs=VMEM,
        compiler_params=pltpu.CompilerParams(vmem_limit_bytes=MIB),
        cost_estimate=declared(20.0),
    )(value)


def pack(value, far, after=(), cost=0.1):
    rows, width = value.shape

    def kernel(ins, outs):
        outs[0][:, :width] = ins[0][...]
        outs[0][:, width:] = ins[1][...]

    return local(kernel, [((rows, 2 * width), value.dtype)], (value, far), after, 1, cost=cost)[0]


def arrange(pair, near, heights, cost=0.1):
    width = pair.shape[1] // 2

    def kernel(ins, outs):
        me = lax.axis_index("hid")
        top = 0
        for out, height in zip(outs, heights):
            for step, (source, at) in enumerate(((0, 0), (1, 0), (0, 1), (1, 1))):
                block = ins[source][top : top + height, at * width : (at + 1) * width]
                out[:, lanes(me ^ step, width)] = block
            top += height

    return local(kernel, [((height, 4 * width), pair.dtype) for height in heights], (pair, near), (), 1, cost=cost)


def over_blocks(width, step, body):
    for base in range(0, width, step):
        body(base, min(step, width - base))


def forward(sources, weights, span, rows, after=(), cost=0.3):
    lower, upper = span
    width, features, tokens = upper - lower, sources[0][0].shape[1], 2 * rows
    arrays = [array for own, theirs, _, _ in sources for array in (own, theirs)]

    def kernel(ins, refs):
        out, held = refs
        loaded = None
        for k, (_, _, first, down) in enumerate(sources):
            if loaded is None or arrays[2 * k] is not arrays[2 * loaded] or first != sources[loaded][2]:
                held[:rows] = ins[2 * k][first : first + rows]
                held[rows:] = ins[2 * k + 1][first : first + rows]
                loaded = k
            weight = ins[len(arrays) + k]
            top = k * tokens

            def product(base, size, weight=weight, top=top, down=down):
                at = slice(lower + base, lower + base + size)
                if down:
                    value = over_cols(held[...], weight[at, :])
                else:
                    value = rows_by_cols(held[...], weight[:, at])
                out[top : top + tokens, base : base + size] = value.astype(out.dtype)

            over_blocks(width, 1024, product)

    return local(
        kernel,
        [((len(sources) * tokens, width), jnp.bfloat16)],
        (*arrays, *weights),
        after,
        scratch=[pltpu.VMEM((tokens, features), jnp.bfloat16)],
        cost=cost,
    )[0]


def backward(own, other, where, weights, span, rows, before, final, after=(), cost=1.0, above=()):
    lower, upper = span
    width, features, tokens = upper - lower, weights[0].shape[0], 2 * rows
    count = len(own)
    ins_all = (*own, *other, *weights, *(() if before is None else (before,)), *above)
    upper_rows = above[0].shape[0] if above else 0
    outs_all = [((width, tokens), jnp.bfloat16)] + [((tokens, width), jnp.bfloat16)] * 2
    height = upper_rows + rows
    outs_all += [((height, features), jnp.float32), ((height, features), jnp.bfloat16)] if final else [((tokens, features), jnp.float32)]

    def kernel(ins, outs):
        for k in range(len(above)):
            outs[3 + k][:upper_rows] = ins[len(ins_all) - len(above) + k][...]

        step = 256 if width % 256 == 0 else 128

        @pl.loop(0, width // step)
        def _(j):
            at = lanes(j, step)

            def total(k):
                array, top = where[k]
                mine = ins[array][top : top + tokens, at].astype(jnp.float32)
                return mine + ins[count + array][top : top + tokens, at].astype(jnp.float32)

            hidden, outs[1][:, at], outs[2][:, at] = swiglu_grads(total(0), total(1), total(2))
            outs[0][at, :] = hidden.T

        def product(base, size):
            at = slice(base, base + size)
            value = over_cols(outs[1][...], ins[2 * count][at, lower:upper])
            value = value + over_cols(outs[2][...], ins[2 * count + 1][at, lower:upper])
            if before is not None:
                value = value + ins[2 * count + 2][:, at]
            if final:
                outs[3][upper_rows:, at] = value[:rows]
                outs[4][upper_rows:, at] = value[rows:].astype(jnp.bfloat16)
            else:
                outs[3][:, at] = value

        over_blocks(features, 1024, product)

    return local(kernel, outs_all, ins_all, after, cost=cost)


def fold_near(value, theirs):
    rows, width = value.shape[0], value.shape[1] // 4

    def kernel(ins, outs):
        odd = lax.rem(lax.axis_index("hid"), 2)
        for i in range(2):
            at = slice(i * width, (i + 1) * width)
            for block, out in ((2 * i + odd, outs[0]), (2 * i + 1 - odd, outs[1])):
                source = lanes(block, width)
                out[:, at] = (ins[0][:, source] + ins[1][:, source].astype(jnp.float32)).astype(out.dtype)

    outs = [((rows, 2 * width), jnp.float32), ((rows, 2 * width), jnp.bfloat16)]
    return local(kernel, outs, (value, theirs), limit=4)


def fold_far(value, theirs, after=()):
    rows, width = value.shape[0], value.shape[1] // 2

    def kernel(ins, outs):
        upper = lax.div(lax.axis_index("hid"), 2)
        for block, out in ((upper, outs[0]), (1 - upper, outs[1])):
            source = lanes(block, width)
            out[...] = (ins[0][:, source] + ins[1][:, source].astype(jnp.float32)).astype(out.dtype)

    outs = [((rows, width), jnp.float32), ((rows, width), jnp.bfloat16)]
    return local(kernel, outs, (value, theirs), after, limit=4)


def fold_last(mine, theirs, earlier=()):
    heights = [piece.shape[0] for piece in earlier]
    rows, width = mine.shape
    shape = (sum(heights) + rows, width)

    def kernel(ins, outs):
        top = 0
        for c, height in enumerate(heights):
            outs[0][top : top + height] = ins[2 + c][...]
            top += height
        outs[0][top:] = (ins[0][...] + ins[1][...].astype(jnp.float32)).astype(jnp.bfloat16)

    specs = [pl.BlockSpec(shape, lambda: (0, 0))] if earlier else None
    return local(kernel, [(shape, jnp.bfloat16)], (mine, theirs, *earlier), limit=4, out_specs=specs)[0]


def joined(pieces, turn, after=()):
    tokens, features = sum(p[2] for p in pieces), pieces[0][0].shape[1]

    def kernel(ins, outs):
        @pl.loop(0, features // 512)
        def _(j):
            at = lanes(j, 512)
            rows = jnp.concatenate([ins[i][p[1] : p[1] + p[2], at] for i, p in enumerate(pieces)], axis=0)
            if turn:
                outs[0][at, :] = rows.T
            else:
                outs[0][:, at] = rows

    shape = (features, tokens) if turn else (tokens, features)
    return local(kernel, [(shape, jnp.bfloat16)], [p[0] for p in pieces], after, limit=4)[0]


def gradients(kernel, outs, arrays, old, grid, specs, scratch, after, cost):
    def body(*refs):
        kernel(refs[: len(arrays)], refs[len(arrays) + len(old) + len(after) :])

    outs, specs = [*outs, (16, 128)], [*specs, VMEM]
    return pl.pallas_call(
        body,
        grid=grid,
        out_shape=[jax.ShapeDtypeStruct(shape, jnp.bfloat16) for shape in outs],
        in_specs=[VMEM] * len(arrays) + [ANYWHERE] * (len(old) + len(after)),
        out_specs=specs,
        scratch_shapes=scratch,
        input_output_aliases={len(arrays) + i: i for i in range(len(old))},
        compiler_params=pltpu.CompilerParams(vmem_limit_bytes=14 * MIB),
        cost_estimate=declared(cost),
    )(*arrays, *old, *after)


def tiled(out, left, right, above=None):
    height, width = out.shape
    for top in range(0, height, 512):
        for start in range(0, width, 256):
            rows, columns = pl.ds(top, min(512, height - top)), pl.ds(start, min(256, width - start))
            value = rows_by_cols(left[rows, :], right[:, columns])
            if above is not None:
                value = value + above[rows, columns].astype(jnp.float32)
            out[rows, columns] = value.astype(out.dtype)


def placed(rows, columns, where):
    return pl.BlockSpec((pl.Element(rows), pl.Element(columns)), where)


def column_grads(x, gs, us, span, total, old, after=(), cost=0.1):
    arrays = [x, *(p[0] for p in (*gs, *us))]
    count, lower, width = len(gs), span[0], span[1] - span[0]
    features, tokens = x.shape
    block = 512

    def kernel(ins, refs):
        gate_out, up_out, token, g_all, u_all = refs
        step = pl.program_id(0)

        @pl.when(step == 0)
        def _():
            token[...] = jnp.zeros_like(token)
            for first, pieces, target in ((1, gs, g_all), (1 + count, us, u_all)):
                top = 0
                for i, (piece, column) in enumerate(pieces):
                    rows = piece.shape[0]
                    target[top : top + rows] = ins[first + i][:, column : column + width]
                    top += rows

        rows = ins[0].at[lanes(step, block), :]
        tiled(gate_out, rows, g_all)
        tiled(up_out, rows, u_all)

    spec = placed(block, width, lambda i: (pl.multiple_of(i * block, block), lower))
    scratch = [pltpu.VMEM((tokens, width), jnp.bfloat16)] * 2
    return gradients(kernel, [(features, total)] * 2, arrays, old, (features // block,), [spec, spec], scratch, after, cost)


def row_grads(hs, y, span, total, old, after=(), cost=0.1):
    arrays = [*(p[0] for p in hs), y]
    count, lower, width = len(hs), span[0], span[1] - span[0]
    tokens, features = y.shape
    block = 512

    def kernel(ins, refs):
        out, token, h_all = refs
        step = pl.program_id(0)

        @pl.when(step == 0)
        def _():
            token[...] = jnp.zeros_like(token)
            left = 0
            for i, (piece, row) in enumerate(hs):
                h_all[:, left : left + piece.shape[1]] = ins[i][row : row + width]
                left += piece.shape[1]

        tiled(out, h_all, ins[count].at[:, lanes(step, block)])

    spec = placed(width, block, lambda i: (lower, pl.multiple_of(i * block, block)))
    scratch = [pltpu.VMEM((width, tokens), jnp.bfloat16)]
    return gradients(kernel, [(total, features)], arrays, old, (features // block,), [spec], scratch, after, cost)


def early_terms(x, y, hs, gs, us, span, after=()):
    count, lower, width = len(gs), span[0], span[1] - span[0]
    tokens, features = sum(g.shape[0] for g in gs), x.shape[0]

    def kernel(ins, refs):
        gate, up, down, h_all, g_all, u_all = refs
        top = 0
        for i, piece in enumerate(gs):
            rows = slice(top, top + piece.shape[0])
            h_all[:, rows] = ins[2 + i][lower : lower + width]
            g_all[rows] = ins[2 + count + i][:, lower : lower + width]
            u_all[rows] = ins[2 + 2 * count + i][:, lower : lower + width]
            top += piece.shape[0]
        tiled(gate, ins[0].at[:, :tokens], g_all)
        tiled(up, ins[0].at[:, :tokens], u_all)
        tiled(down, h_all, ins[1].at[:tokens, :])

    outs = [((features, width), jnp.bfloat16)] * 2 + [((width, features), jnp.bfloat16)]
    scratch = [pltpu.VMEM((width, tokens), jnp.bfloat16)] + [pltpu.VMEM((tokens, width), jnp.bfloat16)] * 2
    return local(kernel, outs, (x, y, *hs, *gs, *us), after, limit=6, scratch=scratch)


def last_columns(x, first, g, u, terms, span, total, old, after, cost):
    lower, width = span[0], span[1] - span[0]
    features, block = x.shape[0], 512

    def kernel(ins, refs):
        gate_out, up_out, token = refs
        step = pl.program_id(0)

        @pl.when(step == 0)
        def _():
            token[...] = jnp.zeros_like(token)

        at = lanes(step, block)
        rows = ins[0].at[at, first:]
        tiled(gate_out, rows, ins[1], ins[3].at[at, :])
        tiled(up_out, rows, ins[2], ins[4].at[at, :])

    spec = placed(block, width, lambda i: (pl.multiple_of(i * block, block), lower))
    arrays = [x, g, u, *terms]
    return gradients(kernel, [(features, total)] * 2, arrays, old, (features // block,), [spec, spec], [], after, cost)


def last_rows(h, y, first, term, span, total, old, after, cost):
    lower, width = span[0], span[1] - span[0]
    features, block = y.shape[1], 512

    def kernel(ins, refs):
        out, token = refs
        step = pl.program_id(0)

        @pl.when(step == 0)
        def _():
            token[...] = jnp.zeros_like(token)

        at = lanes(step, block)
        tiled(out, ins[0], ins[1].at[first:, at], ins[2].at[:, at])

    spec = placed(width, block, lambda i: (lower, pl.multiple_of(i * block, block)))
    return gradients(kernel, [(total, features)], [h, y, term], old, (features // block,), [spec], [], after, cost)


def piped(acts, grad_out, w_gate, w_up, w_down):
    unit = acts.shape[0] // sum(PIECES)
    bounds = [0]
    for size in PIECES:
        bounds.append(bounds[-1] + size * unit)
    spans = list(zip(bounds[:-1], bounds[1:]))
    heights = [upper - lower for lower, upper in spans]
    last = len(spans) - 1
    total = w_gate.shape[1]
    fraction = total // sum(PARTS)
    edges = [sum(PARTS[:i]) * fraction for i in range(len(PARTS) + 1)]
    whole, parts = (0, total), list(zip(edges[:-1], edges[1:]))
    back_weights = (w_gate, w_up)

    def gather(value, parts, early=(), costs=(0.1, 0.1)):
        pair = pack(value, swapped(value, "hid", 2), early, costs[0])
        own = arrange(pair, swapped(pair, "hid", 1), [value.shape[0] // parts] * parts, costs[1])
        return [(array, shifted(array, "tok", 1), 0) for array in own]

    def gather_both(index, after, early=()):
        lower, upper = spans[index]
        mixed = cut_rows(acts, grad_out, [(0, lower, upper - lower), (1, lower, upper - lower)], after)
        return gather(mixed, 2, early)

    rows = heights[0]
    x, = gather(first_rows(acts, rows), 1)
    dy, = gather(cut_rows(acts, grad_out, [(1, 0, rows)]), 1, costs=(1.2, 5.0))
    inputs = [(x, dy), gather_both(1, (dy[0],))]
    gate_up = forward([(*x, False), (*x, False)], (w_gate, w_up), whole, rows)
    dhid = forward([(*dy, True)], (w_down,), whole, rows, (gate_up,))
    sums = [[((gate_up, dhid), ((0, 0), (0, 2 * rows), (1, 0)))]]

    def forward_piece(index, after):
        x, dy = inputs[index]
        rows = heights[index]
        where = ((0, 0), (0, 2 * rows), (0, 4 * rows))
        done = []
        for span in parts if index == last else (whole,):
            part = forward([(*x, False), (*x, False), (*dy, True)], (w_gate, w_up, w_down), span, rows, after)
            done.append(((part,), where))
            after = (part,)
        sums.append(done)
        return after

    def backward_piece(index, part, before, final, after, above=()):
        own, where = sums[index][part]
        span = parts[part] if index == last else whole
        other = [shifted(value, "wid", 1) for value in own]
        cost = 0.1 if index == last else 60.0
        return backward(own, other, where, back_weights, span, heights[index], before, final, after, cost, above)

    def near_step(results):
        return fold_near(results[3], shifted(results[4], "tok", 1))

    def far_step(near, after=()):
        return fold_far(near[0], swapped(near[1], "hid", 1), after)

    def end_step(far, earlier=()):
        return fold_last(far[0], swapped(far[1], "hid", 2), earlier)

    done = forward_piece(1, (dhid,))
    grads = [backward_piece(0, 0, None, True, done)]
    inputs.append(gather_both(last, (inputs[1][0][0],), (grads[0][1],)))
    done = forward_piece(last, (grads[0][1],))
    all_x, all_y = [
        joined([(array, p[k][2], rows) for p, rows in zip(inputs, heights) for array in p[k][:2]], k == 0, done)
        for k in range(2)
    ]
    grads.append(backward_piece(1, 0, None, True, (all_x, all_y), grads[0][3:]))

    def with_last(results, k, part):
        return [(grads[c][k], parts[part][0]) for c in range(last)] + [(results[k], 0)]

    near = near_step(grads[1])
    *terms, down_term = early_terms(all_x, all_y, *([g[k] for g in grads] for k in range(3)), parts[1], (near[0],))
    first = backward_piece(last, 0, None, False, (down_term,))
    down, token = row_grads(with_last(first, 0, 0), all_y, parts[0], total, (), (), 2.0)
    far = far_step(near, (token,))
    gate, up, token = column_grads(
        all_x, with_last(first, 1, 0), with_last(first, 2, 0), parts[0], total, (), (far[0], token)
    )
    finished = end_step(far)
    second = backward_piece(last, 1, first[3], True, (token, finished))
    near = near_step(second)
    held = 2 * (heights[0] + heights[1])
    gate, up, token = last_columns(
        all_x, held, second[1], second[2], terms, parts[1], total, (gate, up), (near[0],), 5.0
    )
    far = far_step(near, (token,))
    down, _ = last_rows(second[0], all_y, held, down_term, parts[1], total, (down,), (far[0],), 3.0)
    return end_step(far, (finished,)), gate, up, down


def shards(acts, grad_out, w_gate, w_up, w_down):
    sizes = tuple(lax.axis_size(axis) for axis in ("hid", "wid", "tok"))
    aligned = acts.shape[0] % (64 * sum(PIECES)) == 0 and acts.shape[1] % 128 == 0 and w_gate.shape[0] % 512 == 0 and w_gate.shape[1] % 1792 == 0
    if sizes == (4, 2, 2) and aligned:
        return piped(acts, grad_out, w_gate, w_up, w_down)
    return plain(acts, grad_out, w_gate, w_up, w_down)


def solution(mesh):
    placed = (
        P(("groups", "tok"), ("wid", "hid")),
        P(("groups", "tok"), ("wid", "hid")),
        P("wid", ("hid", "tok")),
        P("wid", ("hid", "tok")),
        P(("hid", "tok"), "wid"),
    )
    return jax.shard_map(
        shards,
        mesh=mesh,
        in_specs=placed,
        out_specs=(
            P(("groups", "tok"), ("wid", "hid")),
            P(("groups", "wid"), ("hid", "tok")),
            P(("groups", "wid"), ("hid", "tok")),
            P(("groups", "hid", "tok"), "wid"),
        ),
        check_vma=False,
    )
```

```python
import functools

import jax
import jax.numpy as jnp
from jax import lax
from jax.experimental import pallas as pl
from jax.experimental.pallas import tpu as pltpu
from jax.sharding import PartitionSpec as P

PIECES = (1, 1, 1)
PARTS = (1, 1)
MIB = 1 << 20


def dot(left, right, dims):
    return lax.dot_general(left, right, (dims, ((), ())), preferred_element_type=jnp.float32)


def rows_by_cols(left, right):
    return dot(left, right, ((1,), (0,)))


def over_cols(left, right):
    return dot(left, right, ((1,), (1,)))


def over_rows(left, right):
    return dot(left, right, ((0,), (0,)))


def swiglu_grads(gate, up, dhid):
    sig = jax.nn.sigmoid(gate)
    hidden = (gate * sig * up).astype(jnp.bfloat16)
    d_gate = (dhid * up * sig * (1.0 + gate * (1.0 - sig))).astype(jnp.bfloat16)
    d_up = (dhid * gate * sig).astype(jnp.bfloat16)
    return hidden, d_gate, d_up


def shifted(value, axis, step):
    n = lax.axis_size(axis)
    return lax.ppermute(value, axis, [(i, (i + step) % n) for i in range(n)])


def swapped(value, axis, bit):
    n = lax.axis_size(axis)
    return lax.ppermute(value, axis, [(i, i ^ bit) for i in range(n)])


def summed(value, axis):
    total = value.astype(jnp.float32)
    for step in range(1, lax.axis_size(axis)):
        total = total + shifted(value, axis, step).astype(jnp.float32)
    return total


def own_first(value, axis):
    return jnp.concatenate([value] + [shifted(value, axis, step) for step in range(1, lax.axis_size(axis))], axis=0)


def home_rows(back, axis):
    n = lax.axis_size(axis)
    rows = back.shape[0] // n
    sent = back.astype(jnp.bfloat16)
    total = back[:rows]
    for step in range(1, n):
        block = sent[step * rows : (step + 1) * rows]
        total = total + shifted(block, axis, n - step).astype(jnp.float32)
    return total


def plain(acts, grad_out, w_gate, w_up, w_down):
    x = own_first(lax.all_gather(acts, "hid", axis=1, tiled=True), "tok")
    dy = own_first(lax.all_gather(grad_out, "hid", axis=1, tiled=True), "tok")
    gate = summed(rows_by_cols(x, w_gate).astype(jnp.bfloat16), "wid")
    up = summed(rows_by_cols(x, w_up).astype(jnp.bfloat16), "wid")
    dhid = summed(over_cols(dy, w_down).astype(jnp.bfloat16), "wid")
    hidden, d_gate, d_up = swiglu_grads(gate, up, dhid)
    back = home_rows(over_cols(d_gate, w_gate) + over_cols(d_up, w_up), "tok").astype(jnp.bfloat16)
    back = lax.psum_scatter(back, "hid", scatter_dimension=1, tiled=True)
    return (
        back,
        over_rows(x, d_gate).astype(jnp.bfloat16),
        over_rows(x, d_up).astype(jnp.bfloat16),
        over_rows(hidden, dy).astype(jnp.bfloat16),
    )


VMEM = pl.BlockSpec(memory_space=pltpu.VMEM)
ANYWHERE = pl.BlockSpec(memory_space=pl.ANY)


def declared(cost):
    return pl.CostEstimate(flops=int(cost * 1.15e9), bytes_accessed=0, transcendentals=0)


def local(kernel, outs, args, after=(), limit=12, scratch=(), out_specs=None, cost=0.1):
    def body(*refs):
        kernel(refs[: len(args)], refs[len(args) + len(after) :])

    shapes = [jax.ShapeDtypeStruct(shape, dtype) for shape, dtype in outs]
    return pl.pallas_call(
        body,
        out_shape=shapes,
        in_specs=[VMEM] * len(args) + [ANYWHERE] * len(after),
        out_specs=out_specs if out_specs else [VMEM] * len(outs),
        scratch_shapes=list(scratch),
        compiler_params=pltpu.CompilerParams(vmem_limit_bytes=limit * MIB),
        cost_estimate=declared(cost),
    )(*args, *after)


def lanes(index, width):
    return pl.ds(pl.multiple_of(index * width, width), width)


def cut_rows(acts, grad_out, wanted, after=(), cost=0.1):
    width = acts.shape[1]
    height = sum(rows for _, _, rows in wanted)

    def kernel(ins, outs):
        top = 0
        for array, first, rows in wanted:
            outs[0][top : top + rows] = ins[array][first : first + rows]
            top += rows

    return local(kernel, [((height, width), acts.dtype)], (acts, grad_out), after, 1, cost=cost)[0]


def first_rows(value, rows):
    shape = (rows, value.shape[1])

    def kernel(source, out):
        out[...] = source[...]

    return pl.pallas_call(
        kernel,
        grid=(1,),
        out_shape=jax.ShapeDtypeStruct(shape, value.dtype),
        in_specs=[pl.BlockSpec(shape, lambda i: (0, 0))],
        out_specs=VMEM,
        compiler_params=pltpu.CompilerParams(vmem_limit_bytes=MIB),
        cost_estimate=declared(20.0),
    )(value)


def pack(value, far, after=(), cost=0.1):
    rows, width = value.shape

    def kernel(ins, outs):
        outs[0][:, :width] = ins[0][...]
        outs[0][:, width:] = ins[1][...]

    return local(kernel, [((rows, 2 * width), value.dtype)], (value, far), after, 1, cost=cost)[0]


def arrange(pair, near, heights, cost=0.1):
    width = pair.shape[1] // 2

    def kernel(ins, outs):
        me = lax.axis_index("hid")
        top = 0
        for out, height in zip(outs, heights):
            for step, (source, at) in enumerate(((0, 0), (1, 0), (0, 1), (1, 1))):
                block = ins[source][top : top + height, at * width : (at + 1) * width]
                out[:, lanes(me ^ step, width)] = block
            top += height

    return local(kernel, [((height, 4 * width), pair.dtype) for height in heights], (pair, near), (), 1, cost=cost)


def over_blocks(width, step, body):
    for base in range(0, width, step):
        body(base, min(step, width - base))


def forward(sources, weights, span, rows, after=(), cost=0.3):
    lower, upper = span
    width, features, tokens = upper - lower, sources[0][0].shape[1], 2 * rows
    arrays = [array for own, theirs, _, _ in sources for array in (own, theirs)]

    def kernel(ins, refs):
        out, held = refs
        loaded = None
        for k, (_, _, first, down) in enumerate(sources):
            if loaded is None or arrays[2 * k] is not arrays[2 * loaded] or first != sources[loaded][2]:
                held[:rows] = ins[2 * k][first : first + rows]
                held[rows:] = ins[2 * k + 1][first : first + rows]
                loaded = k
            weight = ins[len(arrays) + k]
            top = k * tokens

            def product(base, size, weight=weight, top=top, down=down):
                at = slice(lower + base, lower + base + size)
                if down:
                    value = over_cols(held[...], weight[at, :])
                else:
                    value = rows_by_cols(held[...], weight[:, at])
                out[top : top + tokens, base : base + size] = value.astype(out.dtype)

            over_blocks(width, 1024, product)

    return local(
        kernel,
        [((len(sources) * tokens, width), jnp.bfloat16)],
        (*arrays, *weights),
        after,
        scratch=[pltpu.VMEM((tokens, features), jnp.bfloat16)],
        cost=cost,
    )[0]


def backward(own, other, where, weights, span, rows, before, final, after=(), cost=1.0, above=()):
    lower, upper = span
    width, features, tokens = upper - lower, weights[0].shape[0], 2 * rows
    count = len(own)
    ins_all = (*own, *other, *weights, *(() if before is None else (before,)), *above)
    upper_rows = above[0].shape[0] if above else 0
    outs_all = [((width, tokens), jnp.bfloat16)] + [((tokens, width), jnp.bfloat16)] * 2
    height = upper_rows + rows
    outs_all += [((height, features), jnp.float32), ((height, features), jnp.bfloat16)] if final else [((tokens, features), jnp.float32)]

    def kernel(ins, outs):
        for k in range(len(above)):
            outs[3 + k][:upper_rows] = ins[len(ins_all) - len(above) + k][...]

        step = 256 if width % 256 == 0 else 128

        @pl.loop(0, width // step)
        def _(j):
            at = lanes(j, step)

            def total(k):
                array, top = where[k]
                mine = ins[array][top : top + tokens, at].astype(jnp.float32)
                return mine + ins[count + array][top : top + tokens, at].astype(jnp.float32)

            hidden, outs[1][:, at], outs[2][:, at] = swiglu_grads(total(0), total(1), total(2))
            outs[0][at, :] = hidden.T

        def product(base, size):
            at = slice(base, base + size)
            value = over_cols(outs[1][...], ins[2 * count][at, lower:upper])
            value = value + over_cols(outs[2][...], ins[2 * count + 1][at, lower:upper])
            if before is not None:
                value = value + ins[2 * count + 2][:, at]
            if final:
                outs[3][upper_rows:, at] = value[:rows]
                outs[4][upper_rows:, at] = value[rows:].astype(jnp.bfloat16)
            else:
                outs[3][:, at] = value

        over_blocks(features, 1024, product)

    return local(kernel, outs_all, ins_all, after, cost=cost)


def fold_near(value, theirs):
    rows, width = value.shape[0], value.shape[1] // 4

    def kernel(ins, outs):
        odd = lax.rem(lax.axis_index("hid"), 2)
        for i in range(2):
            at = slice(i * width, (i + 1) * width)
            for block, out in ((2 * i + odd, outs[0]), (2 * i + 1 - odd, outs[1])):
                source = lanes(block, width)
                out[:, at] = (ins[0][:, source] + ins[1][:, source].astype(jnp.float32)).astype(out.dtype)

    outs = [((rows, 2 * width), jnp.float32), ((rows, 2 * width), jnp.bfloat16)]
    return local(kernel, outs, (value, theirs), limit=4)


def fold_far(value, theirs, after=()):
    rows, width = value.shape[0], value.shape[1] // 2

    def kernel(ins, outs):
        upper = lax.div(lax.axis_index("hid"), 2)
        for block, out in ((upper, outs[0]), (1 - upper, outs[1])):
            source = lanes(block, width)
            out[...] = (ins[0][:, source] + ins[1][:, source].astype(jnp.float32)).astype(out.dtype)

    outs = [((rows, width), jnp.float32), ((rows, width), jnp.bfloat16)]
    return local(kernel, outs, (value, theirs), after, limit=4)


def fold_last(mine, theirs, earlier=()):
    heights = [piece.shape[0] for piece in earlier]
    rows, width = mine.shape
    shape = (sum(heights) + rows, width)

    def kernel(ins, outs):
        top = 0
        for c, height in enumerate(heights):
            outs[0][top : top + height] = ins[2 + c][...]
            top += height
        outs[0][top:] = (ins[0][...] + ins[1][...].astype(jnp.float32)).astype(jnp.bfloat16)

    specs = [pl.BlockSpec(shape, lambda: (0, 0))] if earlier else None
    return local(kernel, [(shape, jnp.bfloat16)], (mine, theirs, *earlier), limit=4, out_specs=specs)[0]


def joined(pieces, turn, after=()):
    tokens, features = sum(p[2] for p in pieces), pieces[0][0].shape[1]

    def kernel(ins, outs):
        @pl.loop(0, features // 512)
        def _(j):
            at = lanes(j, 512)
            rows = jnp.concatenate([ins[i][p[1] : p[1] + p[2], at] for i, p in enumerate(pieces)], axis=0)
            if turn:
                outs[0][at, :] = rows.T
            else:
                outs[0][:, at] = rows

    shape = (features, tokens) if turn else (tokens, features)
    return local(kernel, [(shape, jnp.bfloat16)], [p[0] for p in pieces], after, limit=4)[0]


def gradients(kernel, outs, arrays, old, grid, specs, scratch, after, cost):
    def body(*refs):
        kernel(refs[: len(arrays)], refs[len(arrays) + len(old) + len(after) :])

    outs, specs = [*outs, (16, 128)], [*specs, VMEM]
    return pl.pallas_call(
        body,
        grid=grid,
        out_shape=[jax.ShapeDtypeStruct(shape, jnp.bfloat16) for shape in outs],
        in_specs=[VMEM] * len(arrays) + [ANYWHERE] * (len(old) + len(after)),
        out_specs=specs,
        scratch_shapes=scratch,
        input_output_aliases={len(arrays) + i: i for i in range(len(old))},
        compiler_params=pltpu.CompilerParams(vmem_limit_bytes=8 * MIB),
        cost_estimate=declared(cost),
    )(*arrays, *old, *after)


def tiled(out, left, right, above=None):
    height, width = out.shape
    for top in range(0, height, 512):
        for start in range(0, width, 256):
            rows, columns = pl.ds(top, min(512, height - top)), pl.ds(start, min(256, width - start))
            value = rows_by_cols(left[rows, :], right[:, columns])
            if above is not None:
                value = value + above[rows, columns].astype(jnp.float32)
            out[rows, columns] = value.astype(out.dtype)


def placed(rows, columns, where):
    return pl.BlockSpec((pl.Element(rows), pl.Element(columns)), where)


def early_terms(x, y, hs, gs, us, span, after=()):
    count, lower, width = len(gs), span[0], span[1] - span[0]
    tokens, features = sum(g.shape[0] for g in gs), x.shape[0]

    def kernel(ins, refs):
        gate, up, down, h_all, g_all, u_all = refs
        top = 0
        for i, piece in enumerate(gs):
            rows = slice(top, top + piece.shape[0])
            h_all[:, rows] = ins[2 + i][lower : lower + width]
            g_all[rows] = ins[2 + count + i][:, lower : lower + width]
            u_all[rows] = ins[2 + 2 * count + i][:, lower : lower + width]
            top += piece.shape[0]
        tiled(gate, ins[0].at[:, :tokens], g_all)
        tiled(up, ins[0].at[:, :tokens], u_all)
        tiled(down, h_all, ins[1].at[:tokens, :])

    outs = [((features, width), jnp.bfloat16)] * 2 + [((width, features), jnp.bfloat16)]
    scratch = [pltpu.VMEM((width, tokens), jnp.bfloat16)] + [pltpu.VMEM((tokens, width), jnp.bfloat16)] * 2
    return local(kernel, outs, (x, y, *hs, *gs, *us), after, limit=6, scratch=scratch)


def last_columns(x, first, g, u, terms, span, total, old, after, cost):
    lower, width = span[0], span[1] - span[0]
    features, block = x.shape[0], 512

    def kernel(ins, refs):
        gate_out, up_out, token = refs
        step = pl.program_id(0)

        @pl.when(step == 0)
        def _():
            token[...] = jnp.zeros_like(token)

        at = lanes(step, block)
        rows = ins[0].at[at, first:]
        tiled(gate_out, rows, ins[1], ins[3].at[at, :])
        tiled(up_out, rows, ins[2], ins[4].at[at, :])

    spec = placed(block, width, lambda i: (pl.multiple_of(i * block, block), lower))
    arrays = [x, g, u, *terms]
    return gradients(kernel, [(features, total)] * 2, arrays, old, (features // block,), [spec, spec], [], after, cost)


def last_rows(h, y, first, term, span, total, old, after, cost):
    lower, width = span[0], span[1] - span[0]
    features, block = y.shape[1], 512

    def kernel(ins, refs):
        out, token = refs
        step = pl.program_id(0)

        @pl.when(step == 0)
        def _():
            token[...] = jnp.zeros_like(token)

        at = lanes(step, block)
        tiled(out, ins[0], ins[1].at[first:, at], ins[2].at[:, at])

    spec = placed(width, block, lambda i: (lower, pl.multiple_of(i * block, block)))
    return gradients(kernel, [(total, features)], [h, y, term], old, (features // block,), [spec], [], after, cost)


def piped(acts, grad_out, w_gate, w_up, w_down):
    unit = acts.shape[0] // sum(PIECES)
    bounds = [0]
    for size in PIECES:
        bounds.append(bounds[-1] + size * unit)
    spans = list(zip(bounds[:-1], bounds[1:]))
    heights = [upper - lower for lower, upper in spans]
    last = len(spans) - 1
    total = w_gate.shape[1]
    fraction = total // sum(PARTS)
    edges = [sum(PARTS[:i]) * fraction for i in range(len(PARTS) + 1)]
    whole, parts = (0, total), list(zip(edges[:-1], edges[1:]))
    back_weights = (w_gate, w_up)

    def gather(value, parts, early=(), costs=(0.1, 0.1)):
        pair = pack(value, swapped(value, "hid", 2), early, costs[0])
        own = arrange(pair, swapped(pair, "hid", 1), [value.shape[0] // parts] * parts, costs[1])
        return [(array, shifted(array, "tok", 1), 0) for array in own]

    def gather_both(index, after, early=()):
        lower, upper = spans[index]
        mixed = cut_rows(acts, grad_out, [(0, lower, upper - lower), (1, lower, upper - lower)], after)
        return gather(mixed, 2, early)

    rows = heights[0]
    x, = gather(first_rows(acts, rows), 1)
    dy, = gather(cut_rows(acts, grad_out, [(1, 0, rows)]), 1, costs=(1.2, 5.0))
    inputs = [(x, dy), gather_both(1, (dy[0],))]
    gate_up = forward([(*x, False), (*x, False)], (w_gate, w_up), whole, rows)
    dhid = forward([(*dy, True)], (w_down,), whole, rows, (gate_up,))
    sums = [[((gate_up, dhid), ((0, 0), (0, 2 * rows), (1, 0)))]]

    def forward_piece(index, after):
        x, dy = inputs[index]
        rows = heights[index]
        where = ((0, 0), (0, 2 * rows), (0, 4 * rows))
        done = []
        for span in parts if index == last else (whole,):
            part = forward([(*x, False), (*x, False), (*dy, True)], (w_gate, w_up, w_down), span, rows, after)
            done.append(((part,), where))
            after = (part,)
        sums.append(done)
        return after

    def backward_piece(index, part, before, final, after, above=()):
        own, where = sums[index][part]
        span = parts[part] if index == last else whole
        other = [shifted(value, "wid", 1) for value in own]
        cost = 0.1 if index == last else 60.0
        return backward(own, other, where, back_weights, span, heights[index], before, final, after, cost, above)

    def near_step(results):
        return fold_near(results[3], shifted(results[4], "tok", 1))

    def far_step(near, after=()):
        return fold_far(near[0], swapped(near[1], "hid", 1), after)

    def end_step(far, earlier=()):
        return fold_last(far[0], swapped(far[1], "hid", 2), earlier)

    done = forward_piece(1, (dhid,))
    grads = [backward_piece(0, 0, None, True, done)]
    inputs.append(gather_both(last, (inputs[1][0][0],), (grads[0][1],)))
    done = forward_piece(last, (grads[0][1],))
    all_x, all_y = [
        joined([(array, p[k][2], rows) for p, rows in zip(inputs, heights) for array in p[k][:2]], k == 0, done)
        for k in range(2)
    ]
    grads.append(backward_piece(1, 0, None, True, (all_x, all_y), grads[0][3:]))

    near = near_step(grads[1])
    held = 2 * (heights[0] + heights[1])
    known = [[g[k] for g in grads] for k in range(3)]
    *terms, down_term = early_terms(all_x, all_y, *known, parts[1], (near[0],))
    *first_terms, first_down = early_terms(all_x, all_y, *known, parts[0], (down_term,))
    first = backward_piece(last, 0, None, False, (first_down,))
    down, token = last_rows(first[0], all_y, held, first_down, parts[0], total, (), (), 2.0)
    far = far_step(near, (token,))
    gate, up, token = last_columns(
        all_x, held, first[1], first[2], first_terms, parts[0], total, (), (far[0], token), 0.1
    )
    finished = end_step(far)
    second = backward_piece(last, 1, first[3], True, (token, finished))
    near = near_step(second)
    gate, up, token = last_columns(
        all_x, held, second[1], second[2], terms, parts[1], total, (gate, up), (near[0],), 5.0
    )
    far = far_step(near, (token,))
    down, _ = last_rows(second[0], all_y, held, down_term, parts[1], total, (down,), (far[0],), 3.0)
    return end_step(far, (finished,)), gate, up, down


def shards(acts, grad_out, w_gate, w_up, w_down):
    sizes = tuple(lax.axis_size(axis) for axis in ("hid", "wid", "tok"))
    aligned = acts.shape[0] % (64 * sum(PIECES)) == 0 and acts.shape[1] % 128 == 0 and w_gate.shape[0] % 512 == 0 and w_gate.shape[1] % 1792 == 0
    if sizes == (4, 2, 2) and aligned:
        return piped(acts, grad_out, w_gate, w_up, w_down)
    return plain(acts, grad_out, w_gate, w_up, w_down)


def solution(mesh):
    placed = (
        P(("groups", "tok"), ("wid", "hid")),
        P(("groups", "tok"), ("wid", "hid")),
        P("wid", ("hid", "tok")),
        P("wid", ("hid", "tok")),
        P(("hid", "tok"), "wid"),
    )
    return jax.shard_map(
        shards,
        mesh=mesh,
        in_specs=placed,
        out_specs=(
            P(("groups", "tok"), ("wid", "hid")),
            P(("groups", "wid"), ("hid", "tok")),
            P(("groups", "wid"), ("hid", "tok")),
            P(("groups", "hid", "tok"), "wid"),
        ),
        check_vma=False,
    )
```

```python
import functools

import jax
import jax.numpy as jnp
from jax import lax
from jax.experimental import pallas as pl
from jax.experimental.pallas import tpu as pltpu
from jax.sharding import PartitionSpec as P

PIECES = (1, 1, 1)
PARTS = (1, 1)
MIB = 1 << 20


def dot(left, right, dims):
    return lax.dot_general(left, right, (dims, ((), ())), preferred_element_type=jnp.float32)


def rows_by_cols(left, right):
    return dot(left, right, ((1,), (0,)))


def over_cols(left, right):
    return dot(left, right, ((1,), (1,)))


def over_rows(left, right):
    return dot(left, right, ((0,), (0,)))


def swiglu_grads(gate, up, dhid):
    sig = jax.nn.sigmoid(gate)
    hidden = (gate * sig * up).astype(jnp.bfloat16)
    d_gate = (dhid * up * sig * (1.0 + gate * (1.0 - sig))).astype(jnp.bfloat16)
    d_up = (dhid * gate * sig).astype(jnp.bfloat16)
    return hidden, d_gate, d_up


def shifted(value, axis, step):
    n = lax.axis_size(axis)
    return lax.ppermute(value, axis, [(i, (i + step) % n) for i in range(n)])


def swapped(value, axis, bit):
    n = lax.axis_size(axis)
    return lax.ppermute(value, axis, [(i, i ^ bit) for i in range(n)])


def summed(value, axis):
    total = value.astype(jnp.float32)
    for step in range(1, lax.axis_size(axis)):
        total = total + shifted(value, axis, step).astype(jnp.float32)
    return total


def own_first(value, axis):
    return jnp.concatenate([value] + [shifted(value, axis, step) for step in range(1, lax.axis_size(axis))], axis=0)


def home_rows(back, axis):
    n = lax.axis_size(axis)
    rows = back.shape[0] // n
    sent = back.astype(jnp.bfloat16)
    total = back[:rows]
    for step in range(1, n):
        block = sent[step * rows : (step + 1) * rows]
        total = total + shifted(block, axis, n - step).astype(jnp.float32)
    return total


def plain(acts, grad_out, w_gate, w_up, w_down):
    x = own_first(lax.all_gather(acts, "hid", axis=1, tiled=True), "tok")
    dy = own_first(lax.all_gather(grad_out, "hid", axis=1, tiled=True), "tok")
    gate = summed(rows_by_cols(x, w_gate).astype(jnp.bfloat16), "wid")
    up = summed(rows_by_cols(x, w_up).astype(jnp.bfloat16), "wid")
    dhid = summed(over_cols(dy, w_down).astype(jnp.bfloat16), "wid")
    hidden, d_gate, d_up = swiglu_grads(gate, up, dhid)
    back = home_rows(over_cols(d_gate, w_gate) + over_cols(d_up, w_up), "tok").astype(jnp.bfloat16)
    back = lax.psum_scatter(back, "hid", scatter_dimension=1, tiled=True)
    return (
        back,
        over_rows(x, d_gate).astype(jnp.bfloat16),
        over_rows(x, d_up).astype(jnp.bfloat16),
        over_rows(hidden, dy).astype(jnp.bfloat16),
    )


VMEM = pl.BlockSpec(memory_space=pltpu.VMEM)
ANYWHERE = pl.BlockSpec(memory_space=pl.ANY)


def declared(cost):
    return pl.CostEstimate(flops=int(cost * 1.15e9), bytes_accessed=0, transcendentals=0)


def local(kernel, outs, args, after=(), limit=12, scratch=(), out_specs=None, cost=0.1):
    def body(*refs):
        kernel(refs[: len(args)], refs[len(args) + len(after) :])

    shapes = [jax.ShapeDtypeStruct(shape, dtype) for shape, dtype in outs]
    return pl.pallas_call(
        body,
        out_shape=shapes,
        in_specs=[VMEM] * len(args) + [ANYWHERE] * len(after),
        out_specs=out_specs if out_specs else [VMEM] * len(outs),
        scratch_shapes=list(scratch),
        compiler_params=pltpu.CompilerParams(vmem_limit_bytes=limit * MIB),
        cost_estimate=declared(cost),
    )(*args, *after)


def lanes(index, width):
    return pl.ds(pl.multiple_of(index * width, width), width)


def cut_rows(acts, grad_out, wanted, after=(), cost=0.1):
    width = acts.shape[1]
    height = sum(rows for _, _, rows in wanted)

    def kernel(ins, outs):
        top = 0
        for array, first, rows in wanted:
            outs[0][top : top + rows] = ins[array][first : first + rows]
            top += rows

    return local(kernel, [((height, width), acts.dtype)], (acts, grad_out), after, 1, cost=cost)[0]


def first_rows(value, rows):
    shape = (rows, value.shape[1])

    def kernel(source, out):
        out[...] = source[...]

    return pl.pallas_call(
        kernel,
        grid=(1,),
        out_shape=jax.ShapeDtypeStruct(shape, value.dtype),
        in_specs=[pl.BlockSpec(shape, lambda i: (0, 0))],
        out_specs=VMEM,
        compiler_params=pltpu.CompilerParams(vmem_limit_bytes=MIB),
        cost_estimate=declared(20.0),
    )(value)


def pack(value, far, after=(), cost=0.1):
    rows, width = value.shape

    def kernel(ins, outs):
        outs[0][:, :width] = ins[0][...]
        outs[0][:, width:] = ins[1][...]

    return local(kernel, [((rows, 2 * width), value.dtype)], (value, far), after, 1, cost=cost)[0]


def arrange(pair, near, heights, cost=0.1):
    width = pair.shape[1] // 2

    def kernel(ins, outs):
        me = lax.axis_index("hid")
        top = 0
        for out, height in zip(outs, heights):
            for step, (source, at) in enumerate(((0, 0), (1, 0), (0, 1), (1, 1))):
                block = ins[source][top : top + height, at * width : (at + 1) * width]
                out[:, lanes(me ^ step, width)] = block
            top += height

    return local(kernel, [((height, 4 * width), pair.dtype) for height in heights], (pair, near), (), 1, cost=cost)


def over_blocks(width, step, body):
    for base in range(0, width, step):
        body(base, min(step, width - base))


def forward(sources, weights, span, rows, after=(), cost=0.3):
    lower, upper = span
    width, features, tokens = upper - lower, sources[0][0].shape[1], 2 * rows
    arrays = [array for own, theirs, _, _ in sources for array in (own, theirs)]

    def kernel(ins, refs):
        out, held = refs
        loaded = None
        for k, (_, _, first, down) in enumerate(sources):
            if loaded is None or arrays[2 * k] is not arrays[2 * loaded] or first != sources[loaded][2]:
                held[:rows] = ins[2 * k][first : first + rows]
                held[rows:] = ins[2 * k + 1][first : first + rows]
                loaded = k
            weight = ins[len(arrays) + k]
            top = k * tokens

            def product(base, size, weight=weight, top=top, down=down):
                at = slice(lower + base, lower + base + size)
                if down:
                    value = over_cols(held[...], weight[at, :])
                else:
                    value = rows_by_cols(held[...], weight[:, at])
                out[top : top + tokens, base : base + size] = value.astype(out.dtype)

            over_blocks(width, 1024, product)

    return local(
        kernel,
        [((len(sources) * tokens, width), jnp.bfloat16)],
        (*arrays, *weights),
        after,
        scratch=[pltpu.VMEM((tokens, features), jnp.bfloat16)],
        cost=cost,
    )[0]


def backward(own, other, where, weights, span, rows, before, final, after=(), cost=1.0, above=()):
    lower, upper = span
    width, features, tokens = upper - lower, weights[0].shape[0], 2 * rows
    count = len(own)
    ins_all = (*own, *other, *weights, *(() if before is None else (before,)), *above)
    upper_rows = above[0].shape[0] if above else 0
    outs_all = [((width, tokens), jnp.bfloat16)] + [((tokens, width), jnp.bfloat16)] * 2
    height = upper_rows + rows
    outs_all += [((height, features), jnp.float32), ((height, features), jnp.bfloat16)] if final else [((tokens, features), jnp.float32)]

    def kernel(ins, outs):
        for k in range(len(above)):
            outs[3 + k][:upper_rows] = ins[len(ins_all) - len(above) + k][...]

        step = 256 if width % 256 == 0 else 128

        @pl.loop(0, width // step)
        def _(j):
            at = lanes(j, step)

            def total(k):
                array, top = where[k]
                mine = ins[array][top : top + tokens, at].astype(jnp.float32)
                return mine + ins[count + array][top : top + tokens, at].astype(jnp.float32)

            hidden, outs[1][:, at], outs[2][:, at] = swiglu_grads(total(0), total(1), total(2))
            outs[0][at, :] = hidden.T

        def product(base, size):
            at = slice(base, base + size)
            value = over_cols(outs[1][...], ins[2 * count][at, lower:upper])
            value = value + over_cols(outs[2][...], ins[2 * count + 1][at, lower:upper])
            if before is not None:
                value = value + ins[2 * count + 2][:, at]
            if final:
                outs[3][upper_rows:, at] = value[:rows]
                outs[4][upper_rows:, at] = value[rows:].astype(jnp.bfloat16)
            else:
                outs[3][:, at] = value

        over_blocks(features, 1024, product)

    return local(kernel, outs_all, ins_all, after, cost=cost)


def fold_near(value, theirs):
    rows, width = value.shape[0], value.shape[1] // 4

    def kernel(ins, outs):
        odd = lax.rem(lax.axis_index("hid"), 2)
        for i in range(2):
            at = slice(i * width, (i + 1) * width)
            for block, out in ((2 * i + odd, outs[0]), (2 * i + 1 - odd, outs[1])):
                source = lanes(block, width)
                out[:, at] = (ins[0][:, source] + ins[1][:, source].astype(jnp.float32)).astype(out.dtype)

    outs = [((rows, 2 * width), jnp.float32), ((rows, 2 * width), jnp.bfloat16)]
    return local(kernel, outs, (value, theirs), limit=4)


def fold_far(value, theirs, after=()):
    rows, width = value.shape[0], value.shape[1] // 2

    def kernel(ins, outs):
        upper = lax.div(lax.axis_index("hid"), 2)
        for block, out in ((upper, outs[0]), (1 - upper, outs[1])):
            source = lanes(block, width)
            out[...] = (ins[0][:, source] + ins[1][:, source].astype(jnp.float32)).astype(out.dtype)

    outs = [((rows, width), jnp.float32), ((rows, width), jnp.bfloat16)]
    return local(kernel, outs, (value, theirs), after, limit=4)


def fold_last(mine, theirs, earlier=()):
    heights = [piece.shape[0] for piece in earlier]
    rows, width = mine.shape
    shape = (sum(heights) + rows, width)

    def kernel(ins, outs):
        top = 0
        for c, height in enumerate(heights):
            outs[0][top : top + height] = ins[2 + c][...]
            top += height
        outs[0][top:] = (ins[0][...] + ins[1][...].astype(jnp.float32)).astype(jnp.bfloat16)

    specs = [pl.BlockSpec(shape, lambda: (0, 0))] if earlier else None
    return local(kernel, [(shape, jnp.bfloat16)], (mine, theirs, *earlier), limit=4, out_specs=specs)[0]


def joined(pieces, turn, after=()):
    tokens, features = sum(p[2] for p in pieces), pieces[0][0].shape[1]

    def kernel(ins, outs):
        @pl.loop(0, features // 512)
        def _(j):
            at = lanes(j, 512)
            rows = jnp.concatenate([ins[i][p[1] : p[1] + p[2], at] for i, p in enumerate(pieces)], axis=0)
            if turn:
                outs[0][at, :] = rows.T
            else:
                outs[0][:, at] = rows

    shape = (features, tokens) if turn else (tokens, features)
    return local(kernel, [(shape, jnp.bfloat16)], [p[0] for p in pieces], after, limit=4)[0]


def gradients(kernel, outs, arrays, old, grid, specs, scratch, after, cost):
    def body(*refs):
        kernel(refs[: len(arrays)], refs[len(arrays) + len(old) + len(after) :])

    outs, specs = [*outs, (16, 128)], [*specs, VMEM]
    return pl.pallas_call(
        body,
        grid=grid,
        out_shape=[jax.ShapeDtypeStruct(shape, jnp.bfloat16) for shape in outs],
        in_specs=[VMEM] * len(arrays) + [ANYWHERE] * (len(old) + len(after)),
        out_specs=specs,
        scratch_shapes=scratch,
        input_output_aliases={len(arrays) + i: i for i in range(len(old))},
        compiler_params=pltpu.CompilerParams(vmem_limit_bytes=8 * MIB),
        cost_estimate=declared(cost),
    )(*arrays, *old, *after)


def tiled(out, left, right, above=None):
    height, width = out.shape
    for top in range(0, height, 512):
        for start in range(0, width, 256):
            rows, columns = pl.ds(top, min(512, height - top)), pl.ds(start, min(256, width - start))
            value = rows_by_cols(left[rows, :], right[:, columns])
            if above is not None:
                value = value + above[rows, columns].astype(jnp.float32)
            out[rows, columns] = value.astype(out.dtype)


def placed(rows, columns, where):
    return pl.BlockSpec((pl.Element(rows), pl.Element(columns)), where)


def early_terms(x, y, hs, gs, us, span, after=()):
    count, lower, width = len(gs), span[0], span[1] - span[0]
    tokens, features = sum(g.shape[0] for g in gs), x.shape[0]

    def kernel(ins, refs):
        gate, up, down, h_all, g_all, u_all = refs
        top = 0
        for i, piece in enumerate(gs):
            rows = slice(top, top + piece.shape[0])
            h_all[:, rows] = ins[2 + i][lower : lower + width]
            g_all[rows] = ins[2 + count + i][:, lower : lower + width]
            u_all[rows] = ins[2 + 2 * count + i][:, lower : lower + width]
            top += piece.shape[0]
        tiled(gate, ins[0].at[:, :tokens], g_all)
        tiled(up, ins[0].at[:, :tokens], u_all)
        tiled(down, h_all, ins[1].at[:tokens, :])

    outs = [((features, width), jnp.bfloat16)] * 2 + [((width, features), jnp.bfloat16)]
    scratch = [pltpu.VMEM((width, tokens), jnp.bfloat16)] + [pltpu.VMEM((tokens, width), jnp.bfloat16)] * 2
    return local(kernel, outs, (x, y, *hs, *gs, *us), after, limit=6, scratch=scratch)


def last_columns(x, first, g, u, terms, span, total, old, after, cost):
    lower, width = span[0], span[1] - span[0]
    features, block = x.shape[0], 512

    def kernel(ins, refs):
        gate_out, up_out, token = refs
        step = pl.program_id(0)

        @pl.when(step == 0)
        def _():
            token[...] = jnp.zeros_like(token)

        at = lanes(step, block)
        rows = ins[0].at[at, first:]
        tiled(gate_out, rows, ins[1], ins[3].at[at, :])
        tiled(up_out, rows, ins[2], ins[4].at[at, :])

    spec = placed(block, width, lambda i: (pl.multiple_of(i * block, block), lower))
    arrays = [x, g, u, *terms]
    return gradients(kernel, [(features, total)] * 2, arrays, old, (features // block,), [spec, spec], [], after, cost)


def last_rows(h, y, first, term, span, total, old, after, cost):
    lower, width = span[0], span[1] - span[0]
    features, block = y.shape[1], 512

    def kernel(ins, refs):
        out, token = refs
        step = pl.program_id(0)

        @pl.when(step == 0)
        def _():
            token[...] = jnp.zeros_like(token)

        at = lanes(step, block)
        tiled(out, ins[0], ins[1].at[first:, at], ins[2].at[:, at])

    spec = placed(width, block, lambda i: (lower, pl.multiple_of(i * block, block)))
    return gradients(kernel, [(total, features)], [h, y, term], old, (features // block,), [spec], [], after, cost)


def piped(acts, grad_out, w_gate, w_up, w_down):
    unit = acts.shape[0] // sum(PIECES)
    bounds = [0]
    for size in PIECES:
        bounds.append(bounds[-1] + size * unit)
    spans = list(zip(bounds[:-1], bounds[1:]))
    heights = [upper - lower for lower, upper in spans]
    last = len(spans) - 1
    total = w_gate.shape[1]
    fraction = total // sum(PARTS)
    edges = [sum(PARTS[:i]) * fraction for i in range(len(PARTS) + 1)]
    whole, parts = (0, total), list(zip(edges[:-1], edges[1:]))
    back_weights = (w_gate, w_up)

    def gather(value, parts, early=(), costs=(0.1, 0.1)):
        pair = pack(value, swapped(value, "hid", 2), early, costs[0])
        own = arrange(pair, swapped(pair, "hid", 1), [value.shape[0] // parts] * parts, costs[1])
        return [(array, shifted(array, "tok", 1), 0) for array in own]

    def gather_both(index, after, early=()):
        lower, upper = spans[index]
        mixed = cut_rows(acts, grad_out, [(0, lower, upper - lower), (1, lower, upper - lower)], after)
        return gather(mixed, 2, early)

    rows = heights[0]
    x, = gather(first_rows(acts, rows), 1)
    dy, = gather(cut_rows(acts, grad_out, [(1, 0, rows)]), 1, costs=(1.2, 5.0))
    inputs = [(x, dy), gather_both(1, (dy[0],))]
    gate_up = forward([(*x, False), (*x, False)], (w_gate, w_up), whole, rows)
    dhid = forward([(*dy, True)], (w_down,), whole, rows, (gate_up,))
    sums = [[((gate_up, dhid), ((0, 0), (0, 2 * rows), (1, 0)))]]

    def forward_piece(index, after):
        x, dy = inputs[index]
        rows = heights[index]
        where = ((0, 0), (0, 2 * rows), (0, 4 * rows))
        done = []
        for span in parts if index == last else (whole,):
            part = forward([(*x, False), (*x, False), (*dy, True)], (w_gate, w_up, w_down), span, rows, after)
            done.append(((part,), where))
            after = (part,)
        sums.append(done)
        return after

    def backward_piece(index, part, before, final, after, above=()):
        own, where = sums[index][part]
        span = parts[part] if index == last else whole
        other = [shifted(value, "wid", 1) for value in own]
        cost = 2.0 if index == last else 60.0
        return backward(own, other, where, back_weights, span, heights[index], before, final, after, cost, above)

    def near_step(results):
        return fold_near(results[3], shifted(results[4], "tok", 1))

    def far_step(near, after=()):
        return fold_far(near[0], swapped(near[1], "hid", 1), after)

    def end_step(far, earlier=()):
        return fold_last(far[0], swapped(far[1], "hid", 2), earlier)

    done = forward_piece(1, (dhid,))
    grads = [backward_piece(0, 0, None, True, done)]
    inputs.append(gather_both(last, (inputs[1][0][0],), (grads[0][1],)))
    done = forward_piece(last, (grads[0][1],))
    all_x, all_y = [
        joined([(array, p[k][2], rows) for p, rows in zip(inputs, heights) for array in p[k][:2]], k == 0, done)
        for k in range(2)
    ]
    grads.append(backward_piece(1, 0, None, True, (all_x, all_y), grads[0][3:]))

    near = near_step(grads[1])
    held = 2 * (heights[0] + heights[1])
    known = [[g[k] for g in grads] for k in range(3)]
    *terms, down_term = early_terms(all_x, all_y, *known, parts[1], (near[0],))
    *first_terms, first_down = early_terms(all_x, all_y, *known, parts[0], (down_term,))
    first = backward_piece(last, 0, None, False, (first_down,))
    far = far_step(near, (first[1],))
    down, token = last_rows(first[0], all_y, held, first_down, parts[0], total, (), (far[0],), 2.0)
    gate, up, token = last_columns(
        all_x, held, first[1], first[2], first_terms, parts[0], total, (), (token,), 0.1
    )
    finished = end_step(far)
    second = backward_piece(last, 1, first[3], True, (token, finished))
    near = near_step(second)
    gate, up, token = last_columns(
        all_x, held, second[1], second[2], terms, parts[1], total, (gate, up), (near[0],), 5.0
    )
    far = far_step(near, (token,))
    down, _ = last_rows(second[0], all_y, held, down_term, parts[1], total, (down,), (far[0],), 3.0)
    return end_step(far, (finished,)), gate, up, down


def shards(acts, grad_out, w_gate, w_up, w_down):
    sizes = tuple(lax.axis_size(axis) for axis in ("hid", "wid", "tok"))
    aligned = acts.shape[0] % (64 * sum(PIECES)) == 0 and acts.shape[1] % 128 == 0 and w_gate.shape[0] % 512 == 0 and w_gate.shape[1] % 1792 == 0
    if sizes == (4, 2, 2) and aligned:
        return piped(acts, grad_out, w_gate, w_up, w_down)
    return plain(acts, grad_out, w_gate, w_up, w_down)


def solution(mesh):
    placed = (
        P(("groups", "tok"), ("wid", "hid")),
        P(("groups", "tok"), ("wid", "hid")),
        P("wid", ("hid", "tok")),
        P("wid", ("hid", "tok")),
        P(("hid", "tok"), "wid"),
    )
    return jax.shard_map(
        shards,
        mesh=mesh,
        in_specs=placed,
        out_specs=(
            P(("groups", "tok"), ("wid", "hid")),
            P(("groups", "wid"), ("hid", "tok")),
            P(("groups", "wid"), ("hid", "tok")),
            P(("groups", "hid", "tok"), "wid"),
        ),
        check_vma=False,
    )
```
